32 devices in a mesh: groups: 2 (over x), dom: 8 (over z, y), rows: 2 (over core).
Axes of the slice: x: 2, y: 2, z: 4, core: 2. Of those that a mesh axis runs over, the one named last changes fastest.
Arguments:
- density: bfloat16 [4096, 2048], P(('groups', 'dom')), parts along dimension 0, may hold values from -0.25 to 0.25
- owner: int32 [32], P('groups'), parts along dimension 0, may hold values from 0 to 15, each once
- touched: int32 [16, 8], P(('groups', 'dom')), parts along dimension 0, may hold values from 0 to 15, as said below
- blocks: int32 [768, 4], P(('groups', 'dom', 'rows')), parts along dimension 0, may hold values from 0 to 7, as said below
- counts: int32 [768], P(('groups', 'dom', 'rows')), parts along dimension 0, may hold values from 2 to 4
- basis: bfloat16 [768, 512, 256], P(('groups', 'dom', 'rows')), parts along dimension 0, may hold values from -6 to 6
- points: float32 [768, 3, 256], P(('groups', 'dom', 'rows')), parts along dimension 0, may hold values from -3 to 3
- weights: float32 [768, 256], P(('groups', 'dom', 'rows')), parts along dimension 0, may hold values from 0.02 to 0.2
- centers: float32 [3, 4096], P(None, 'groups'), parts along dimension 1, may hold values from -3 to 3
- widths: float32 [4096], P('groups'), parts along dimension 0, may hold values from 0.5 to 2
Outputs:
- exchange: bfloat16 [4096, 2048], P(('groups', 'dom'), 'rows'), parts along dimension 0
The draws below stay inside these ranges and needn't reach their ends.
There are 2 independent parts, one for each index of `groups`. The reference program is written for one: setup_inputs(seed, part) draws one part's arguments, and reference() takes and returns one part's arrays. A program takes and returns all parts, laid end to end along the dimension named above; each array names one. Nothing has to cross between parts.
Inputs may be any that keep to these rules, and one draw needn't show every extreme that they name: `touched`: each row holds 8 different function blocks. `blocks`: each row names 4 different positions; the batches of one dom index are 48 consecutive rows, and every position is named by some batch of each dom index. `owner`: each block row has a stored position of its own.
All inputs are finite; a program needn't handle non-finite values.
Results may differ from the reference program's by a relative error of at most 0.0034.
Values may be sent and summed in bfloat16 or wider, within the bound.
No kernel may reach another device: no remote copies, remote signals or barrier semaphores. Data moves between devices by JAX's collectives and lax.ppermute only.
A program may use at most 128 MiB of HBM per device.

```python
import math
import jax
import jax.numpy as jnp
from jax import lax

FB = 128
TMAX = 4
PTS = 256
UMAX = 8
NBLK = 16
DOM_BATCH = 48
NFUNC = 2048
NBATCH = 384
N_DOM = 8


def draw_touched(key, part):
    key = jax.random.fold_in(key, 11)
    keys = jax.random.split(key, N_DOM)
    orders = jax.vmap(lambda k: jax.random.permutation(k, NBLK))(keys)
    return orders[:, :UMAX].astype(jnp.int32)


def draw_blocks(key, part):
    key = jax.random.fold_in(key, 23)
    keys = jax.random.split(key, NBATCH)
    orders = jax.vmap(lambda k: jax.random.permutation(k, UMAX))(keys)[:, :TMAX].astype(jnp.int32)
    within = jnp.arange(NBATCH, dtype=jnp.int32) % DOM_BATCH
    cover = (within[:, None] * TMAX + jnp.arange(TMAX, dtype=jnp.int32)[None, :]) % UMAX
    needed = (UMAX + TMAX - 1) // TMAX
    return jnp.where(within[:, None] < needed, cover, orders).astype(jnp.int32)


def place_ends(entries, rng, least, largest):
    longest = entries.shape.index(max(entries.shape))
    spots = []
    for shift in (0, 1):
        where = [jax.random.randint(jax.random.fold_in(rng, axis), (), 0, length) for axis, length in enumerate(entries.shape)]
        where[longest] = (where[longest] + shift) % entries.shape[longest]
        spots.append(tuple(where))
    return entries.at[spots[0]].set(least).at[spots[1]].set(largest)


def shard_levels(own_key, extent, cuts, low, top_value):
    gain = 1.0
    for dim, blocks in cuts:
        draws = jax.random.uniform(jax.random.fold_in(jax.random.fold_in(own_key, 6), dim), (blocks,), jnp.float32, low / len(cuts), top_value / len(cuts))
        gain = gain * jnp.repeat(jnp.exp(draws), extent[dim] // blocks).reshape((-1,) + (1,) * (len(extent) - 1 - dim))
    return gain


def bell_draw(stream_key, shape, deviation, reach, cuts=(), kind=jnp.bfloat16):
    gain = shard_levels(stream_key, shape, cuts, -0.22, 0.18) if cuts else 1.0
    drawn = jax.random.normal(stream_key, shape, jnp.float32) * deviation * gain
    return jnp.minimum(jnp.maximum(drawn, -reach), reach).astype(kind)


def setup_inputs(seed: int = 0, part: int = 0) -> dict:
    splits = jax.random.split(jax.random.key(seed), 11)
    part_splits = jax.random.split(jax.random.fold_in(splits[10], part), 11)
    return {
        "density": bell_draw(part_splits[0], (NFUNC, NFUNC), (TMAX * FB) ** -0.5, 0.25, ((0, 8),)),
        "owner": jax.random.permutation(part_splits[1], NBLK).astype(jnp.int32),
        "touched": draw_touched(jax.random.fold_in(jax.random.fold_in(splits[10], part), 71), part),
        "blocks": draw_blocks(jax.random.fold_in(jax.random.fold_in(splits[10], part), 71), part),
        "counts": place_ends(jax.random.randint(part_splits[4], (NBATCH,), 2, TMAX + 1), jax.random.fold_in(part_splits[4], 1), 2, TMAX).astype(jnp.int32),
        "basis": bell_draw(part_splits[5], (NBATCH, TMAX * FB, PTS), 1.0, 6.0, ((0, 16),)),
        "points": jnp.clip(jax.random.uniform(part_splits[6], (NBATCH, 3, PTS), jnp.float32, -3.0, 3.0) * shard_levels(part_splits[6], (NBATCH, 3, PTS), ((0, 16),), -0.4, 0.0), -3.0, 3.0),
        "weights": jnp.clip(jnp.exp(math.log(0.2) - 2.3025851 * jax.random.uniform(part_splits[7], (NBATCH, PTS), jnp.float32) ** shard_levels(part_splits[7], (NBATCH, PTS), ((0, 16),), -0.2, 0.2)), 0.02, 0.2),
        "centers": jnp.clip(jax.random.uniform(part_splits[8], (3, NFUNC), jnp.float32, -3.0, 3.0), -3.0, 3.0),
        "widths": jnp.clip(jnp.exp(jax.random.uniform(part_splits[9], (NFUNC,), jnp.float32, math.log(0.5), math.log(2.0))), 0.5, 2.0),
    }


def coulomb(centre_x, centre_y, centre_z, spread, point_x, point_y, point_z):
    dist = (centre_x - point_x) ** 2 + (centre_y - point_y) ** 2 + (centre_z - point_z) ** 2
    return 1.0 / jnp.sqrt(dist + spread * spread)

def reference(density, owner, touched, blocks, counts, basis, points, weights, centers, widths):
    width = TMAX * FB
    dense_four = density.reshape(NBLK, FB, NBLK, FB)
    centre_blocks = centers.reshape(3, NBLK, FB)
    spread_blocks = widths.reshape(NBLK, FB)
    slot_ids = jnp.arange(TMAX, dtype=jnp.int32)
    batch_dom = (jnp.arange(NBATCH, dtype=jnp.int32) // DOM_BATCH).astype(jnp.int32)
    global_ids = jnp.take_along_axis(touched[batch_dom], blocks, axis=1).astype(jnp.int32)

    def step(total, item):
        block_ids, count, values, coords, quad = item
        position = owner[block_ids].astype(jnp.int32)
        dloc = dense_four[position][:, :, block_ids, :].reshape(width, width)
        active = (slot_ids < count).astype(jnp.float32)
        rowmask = jnp.repeat(active, FB)[:, None]
        xmask = jnp.where(rowmask > 0, values, jnp.zeros_like(values))
        gval = jnp.dot(dloc, xmask, preferred_element_type=jnp.float32)
        centre = centre_blocks[:, block_ids, :].reshape(3, width)
        spread = spread_blocks[block_ids].reshape(width)
        vfac = coulomb(centre[0][:, None], centre[1][:, None], centre[2][:, None], spread[:, None], coords[0][None, :], coords[1][None, :], coords[2][None, :])
        fval = (gval * vfac * rowmask).astype(jnp.bfloat16)
        xweighted = (xmask.astype(jnp.float32) * quad[None, :]).astype(jnp.bfloat16)
        part = jnp.dot(fval, xweighted.T, preferred_element_type=jnp.float32)
        pieces = part.reshape(TMAX, FB, TMAX, FB).transpose(0, 2, 1, 3)
        total = total.at[position[:, None], :, block_ids[None, :], :].add(pieces)
        return (total, None)
    start = jnp.zeros((NBLK, FB, NBLK, FB), jnp.float32)
    total, _ = lax.scan(step, start, (global_ids, counts, basis, points, weights))
    return total.reshape(NFUNC, NFUNC).astype(jnp.bfloat16)
```

```python
import functools
import math

import jax
import jax.numpy as jnp
from jax import lax
from jax.experimental import pallas as pl
from jax.experimental.pallas import tpu as pltpu
from jax.sharding import PartitionSpec as P

FB = 128
TMAX = 4
UMAX = 8
MIB = 1024 * 1024


def coulomb(centre_x, centre_y, centre_z, spread, point_x, point_y, point_z):
    dist = (centre_x - point_x) ** 2 + (centre_y - point_y) ** 2 + (centre_z - point_z) ** 2
    return 1.0 / jnp.sqrt(dist + spread * spread)


def lookup_owner(owner, block_ids):
    match = block_ids[:, None] == jnp.arange(owner.shape[0], dtype=jnp.int32)[None, :]
    return jnp.sum(jnp.where(match, owner[None, :], 0), axis=1)


def answer_for(density, column_sets):
    rows_here = density.shape[0]
    sources, wanted = column_sets.shape
    blocked = density.reshape(rows_here, density.shape[1] // FB, FB)
    picked = jnp.take(blocked, column_sets.reshape(-1), axis=1)
    return picked.reshape(rows_here, sources, wanted * FB).transpose(1, 0, 2)


def spread_rows(terms, stored, block_count, sources):
    columns = terms.shape[1]
    expanded = jnp.zeros((block_count, FB, columns), jnp.float32)
    expanded = expanded.at[stored].set(terms.reshape(UMAX, FB, columns))
    return expanded.reshape(sources, block_count * FB // sources, columns)


def collect(returned, column_sets, block_count):
    sources, rows_here, columns = returned.shape
    wanted = column_sets.shape[1]
    pieces = returned.reshape(sources, rows_here, wanted, FB).transpose(1, 0, 2, 3)
    pieces = pieces.reshape(rows_here, sources * wanted, FB)
    total = jnp.zeros((rows_here, block_count, FB), jnp.float32)
    total = total.at[:, column_sets.reshape(-1)].add(pieces)
    return total.reshape(rows_here, block_count * FB)


def per_device_any(density, owner, touched, blocks, counts, basis, points, weights, centers, widths):
    rows_count = lax.axis_size("rows")
    rows_index = lax.axis_index("rows")
    batches = blocks.shape[0]
    block_count = owner.shape[0]
    width = TMAX * FB
    share = UMAX // rows_count
    own_set = touched[0]
    all_sets = lax.all_gather(touched, "dom", axis=0, tiled=True)
    sources = all_sets.shape[0]
    half_sets = lax.dynamic_slice_in_dim(all_sets, rows_index * share, share, 1)
    got = lax.all_to_all(
        answer_for(density, all_sets), "dom", split_axis=0, concat_axis=0, tiled=True
    )
    panel = got.reshape(block_count * FB, UMAX * FB)
    stored = lookup_owner(owner, own_set)
    tile = jnp.take(panel.reshape(block_count, FB, UMAX * FB), stored, axis=0).reshape(
        UMAX, FB, UMAX, FB
    )
    centre_blocks = centers.reshape(3, block_count, FB)
    spread_blocks = widths.reshape(block_count, FB)
    slot_ids = jnp.arange(TMAX, dtype=jnp.int32)
    group = math.gcd(batches, 8)
    turns = batches // group

    def work(total, item):
        slots, count, values, coords, quad = item
        gid = jnp.take(own_set, slots.reshape(-1), axis=0)
        active = (slot_ids[None, :] < count[:, None]).astype(jnp.float32)
        rowmask = jnp.repeat(active, FB, axis=1)[:, :, None]
        xmask = jnp.where(rowmask > 0, values, jnp.zeros_like(values))
        xweighted = (xmask.astype(jnp.float32) * quad[:, None, :]).astype(jnp.bfloat16)
        dloc = tile[slots[:, :, None], :, slots[:, None, :], :]
        dloc = dloc.transpose(0, 1, 3, 2, 4).reshape(group, width, width)
        centre = jnp.take(centre_blocks, gid, axis=1).reshape(3, group, width)
        spread = jnp.take(spread_blocks, gid, axis=0).reshape(group, width)
        vfac = coulomb(
            centre[0][:, :, None],
            centre[1][:, :, None],
            centre[2][:, :, None],
            spread[:, :, None],
            coords[:, 0][:, None, :],
            coords[:, 1][:, None, :],
            coords[:, 2][:, None, :],
        )
        gval = jnp.einsum("brc,bcg->brg", dloc, xmask, preferred_element_type=jnp.float32)
        fval = (gval * vfac * rowmask).astype(jnp.bfloat16)
        parts = jnp.einsum("brg,bcg->brc", fval, xweighted, preferred_element_type=jnp.float32)
        pieces = parts.reshape(group, TMAX, FB, TMAX, FB).transpose(0, 1, 3, 2, 4)
        total = total.at[slots[:, :, None], :, slots[:, None, :], :].add(pieces)
        return (total, None)

    items = (
        blocks.reshape(turns, group, TMAX),
        counts.reshape(turns, group),
        basis.reshape(turns, group, width, basis.shape[2]),
        points.reshape(turns, group, 3, points.shape[2]),
        weights.reshape(turns, group, weights.shape[1]),
    )
    start = jnp.zeros((UMAX, FB, UMAX, FB), jnp.float32)
    local_sum, _ = lax.scan(work, start, items)
    local_flat = local_sum.reshape(UMAX * FB, UMAX * FB)
    halved = lax.psum_scatter(local_flat, "rows", scatter_dimension=1, tiled=True)
    returned = lax.all_to_all(
        spread_rows(halved, stored, block_count, sources),
        "dom",
        split_axis=0,
        concat_axis=0,
        tiled=True,
    )
    gathered_terms = collect(returned, half_sets, block_count)
    summed = lax.psum_scatter(gathered_terms, "rows", scatter_dimension=1, tiled=True)
    return summed.astype(jnp.bfloat16)


def call(kernel, scalars, arrays, in_specs, out_shapes, out_specs, scratch, grid=(1,), cost=None, vmem=48):
    return pl.pallas_call(
        kernel,
        grid_spec=pltpu.PrefetchScalarGridSpec(
            num_scalar_prefetch=len(scalars),
            grid=grid,
            in_specs=in_specs,
            out_specs=out_specs,
            scratch_shapes=scratch,
        ),
        out_shape=out_shapes,
        cost_estimate=pl.CostEstimate(flops=cost[0], bytes_accessed=cost[1], transcendentals=0),
        compiler_params=pltpu.CompilerParams(vmem_limit_bytes=vmem * MIB),
    )(*scalars, *arrays)


def whole(shape):
    return pl.BlockSpec(shape, lambda *_: (0,) * len(shape))


def pick_kernel(sets, full, *outs):
    for k, out in enumerate(outs):
        for q in range(UMAX):
            block = sets[k * UMAX + q]
            out[:, :, q * FB : (q + 1) * FB] = full[:, :, pl.ds(pl.multiple_of(block * FB, FB), FB)]


def pick(sets, full, peers):
    nb, sub, cols = full.shape
    shape = (nb, sub, UMAX * FB)
    return call(
        pick_kernel,
        [sets],
        [full],
        [whole(full.shape)],
        [jax.ShapeDtypeStruct(shape, full.dtype)] * peers,
        [whole(shape)] * peers,
        [],
        cost=(0, 2 * nb * sub * (cols + peers * UMAX * FB)),
    )


def add_up(sets, terms, total):
    total[...] = jnp.zeros(total.shape, total.dtype)
    for k, term in enumerate(terms):
        for q in range(UMAX):
            cols = pl.ds(pl.multiple_of(sets[k * UMAX + q] * FB, FB), FB)
            total[:, :, cols] += term[:, :, q * FB : (q + 1) * FB].astype(jnp.float32)


def merge_kernel(peers, sets, *refs):
    terms, out, total = refs[:peers], refs[peers], refs[peers + 1]
    add_up(sets, terms, total)
    out[...] = total[...].astype(out.dtype)


def merge(sets, terms, cols):
    nb, sub, wide = terms[0].shape
    shape = (nb, sub, cols)
    return call(
        functools.partial(merge_kernel, len(terms)),
        [sets],
        terms,
        [whole(t.shape) for t in terms],
        jax.ShapeDtypeStruct(shape, jnp.bfloat16),
        whole(shape),
        [pltpu.VMEM(shape, jnp.float32)],
        cost=(0, 2 * nb * sub * (cols + 5 * wide)),
    )


def finish_kernel(peers, sets, core, *refs):
    terms, far = refs[:peers], refs[peers]
    keep, give, total = refs[peers + 1 :]
    add_up(sets, terms, total)
    half = keep.shape[2]
    for out, side in ((keep, core[0]), (give, 1 - core[0])):
        cols = pl.ds(pl.multiple_of(side * half, FB), half)
        out[...] = (total[:, :, cols] + far[:, :, cols].astype(jnp.float32)).astype(out.dtype)


def finish(sets, core, terms, far):
    nb, sub, wide = terms[0].shape
    cols = far.shape[2]
    shape = (nb, sub, cols // 2)
    return call(
        functools.partial(finish_kernel, len(terms)),
        [sets, core],
        [*terms, far],
        [whole(t.shape) for t in terms] + [whole(far.shape)],
        [jax.ShapeDtypeStruct(shape, jnp.bfloat16)] * 2,
        [whole(shape)] * 2,
        [pltpu.VMEM(far.shape, jnp.float32)],
        cost=(0, 2 * nb * sub * (2 * cols + 5 * wide)),
    )


def batch_kernel(steps, group, pieces, local, kbs, blocks, counts, *refs):
    xs, quads = refs[0:2], refs[2:4]
    centre = refs[4]
    parts = refs[5 : 5 + pieces]
    outs = refs[5 + pieces : 5 + 2 * pieces]
    dense, acc, sems = refs[5 + 2 * pieces :]
    nb, sub = parts[0].shape[:2]
    step = pl.program_id(0)
    batches = steps * group

    @pl.when(step == 0)
    def _():
        copies = [
            pltpu.make_async_copy(part, dense.at[pl.ds(nb * k, nb)], sems.at[k])
            for k, part in enumerate(parts)
        ]
        for copy in copies:
            copy.start()
        acc[...] = jnp.zeros(acc.shape, acc.dtype)
        for copy in copies:
            copy.wait()

    def one(side, g):
        b = side * batches + step * group + g
        count = counts[b]
        for live in range(2, TMAX + 1):

            @pl.when(count == live)
            def _():
                pos = [blocks[b * TMAX + s] for s in range(live)]
                row = [kbs[p] for p in pos]
                col = [pl.ds(pl.multiple_of(p * FB, FB), FB) for p in pos]
                x = xs[side][g, : live * FB, :]
                quad = quads[side]
                xw = (x.astype(jnp.float32) * quad[g, 3:4, :]).astype(jnp.bfloat16)
                d = jnp.concatenate(
                    [
                        jnp.concatenate([dense[row[s], :, col[t]] for t in range(live)], axis=1)
                        for s in range(live)
                    ],
                    axis=0,
                )
                gval = jnp.dot(d, x, preferred_element_type=jnp.float32)
                fval = []
                for s in range(live):
                    dist = None
                    for axis in range(3):
                        c = centre[axis, pos[s]]
                        c = jnp.concatenate([c] * (x.shape[1] // FB), axis=1)
                        diff = c - quad[g, axis : axis + 1, :]
                        dist = diff * diff if dist is None else dist + diff * diff
                    c = centre[3, pos[s]]
                    dist = dist + jnp.concatenate([c] * (x.shape[1] // FB), axis=1)
                    fval.append((gval[s * sub : (s + 1) * sub] * lax.rsqrt(dist)).astype(jnp.bfloat16))
                fval = jnp.concatenate(fval, axis=0)
                part = lax.dot_general(
                    fval, xw, (((1,), (1,)), ((), ())), preferred_element_type=jnp.float32
                )
                for s in range(live):
                    for t in range(live):
                        acc[row[s], :, col[t]] += part[s * sub : (s + 1) * sub, t * FB : (t + 1) * FB]

    for side in (0, 1):

        @pl.loop(0, group)
        def _(g):
            one(side, g)

    @pl.when(step == steps - 1)
    def _():
        for k, out in enumerate(outs):
            out[...] = acc[nb * k : nb * (k + 1)].astype(out.dtype)


def batch_sums(kbs, blocks, counts, xs, quads, centre, parts, local):
    batches, width, pts = xs[0].shape
    group = math.gcd(batches, 4)
    steps = batches // group
    nb, sub, wide = parts[0].shape
    pieces = len(parts)
    out_shapes = [
        jax.ShapeDtypeStruct(parts[0].shape, jnp.float32 if k in local else jnp.bfloat16)
        for k in range(pieces)
    ]
    flops = 2 * batches * 2 * 2 * width * (width // 2) * pts
    return call(
        functools.partial(batch_kernel, steps, group, pieces, local),
        [kbs, blocks, counts],
        [*xs, *quads, centre, *parts],
        [pl.BlockSpec((group, width, pts), lambda i, *_: (i, 0, 0))] * 2
        + [pl.BlockSpec((group, 4, pts), lambda i, *_: (i, 0, 0))] * 2
        + [whole(centre.shape)]
        + [pl.BlockSpec(memory_space=pl.ANY)] * pieces,
        out_shapes,
        [whole(parts[0].shape)] * pieces,
        [
            pltpu.VMEM((nb * pieces, sub, wide), jnp.bfloat16),
            pltpu.VMEM((nb * pieces, sub, wide), jnp.float32),
            pltpu.SemaphoreType.DMA((pieces,)),
        ],
        grid=(steps,),
        cost=(flops, 2 * batches * width * pts * 2),
    )


def per_device(density, owner, touched, blocks, counts, basis, points, weights, centers, widths):
    n = lax.axis_size("dom")
    cores = lax.axis_size("rows")
    i = lax.axis_index("dom")
    r = lax.axis_index("rows")
    nb = density.shape[0] // FB
    sub = FB // cores
    cols = density.shape[1]
    block_count = owner.shape[0]
    near = n // 2

    def swap(x, k):
        return lax.ppermute(x, "dom", [(a, a ^ k) for a in range(n)])

    def across(x):
        return lax.ppermute(x, "rows", [(a, cores - 1 - a) for a in range(cores)])

    own = lax.dynamic_index_in_dim(density.reshape(nb, cores, sub, cols), r, 1, keepdims=False)
    far = swap(own, near)
    near_sets = jnp.concatenate([touched] + [swap(touched, k) for k in range(1, near)], axis=0).reshape(-1)

    quads = jnp.concatenate([points, weights[:, None, :]], axis=1)
    tables = jnp.concatenate([blocks, counts[:, None]], axis=1)
    basis_b, quads_b, tables_b = across(basis), across(quads), across(tables)
    both = jnp.concatenate([tables, tables_b], axis=0)
    slots = both[:, :TMAX].reshape(-1)
    live = both[:, TMAX]

    own_set = touched[0]
    stored = lookup_owner(owner, own_set)
    kbs = jnp.bitwise_xor(stored // nb, i) * nb + stored % nb
    shaped = jnp.concatenate([centers, (widths * widths)[None]], axis=0).reshape(4, block_count, cores, sub)
    shaped = lax.dynamic_index_in_dim(shaped, r, 2, keepdims=False)
    centre = jnp.take(shaped, own_set, axis=1)
    centre = jnp.broadcast_to(centre[..., None], (4, UMAX, sub, FB))

    picked = pick(near_sets, own, near)
    parts = [picked[0]] + [swap(picked[k], k) for k in range(1, near)]
    picked = pick(near_sets, far, near)
    parts += [picked[0]] + [swap(picked[k], k) for k in range(1, near)]

    sums = batch_sums(kbs, slots, live, (basis, basis_b), (quads, quads_b), centre, parts, (0, near))
    terms = [sums[near]] + [swap(sums[near + k], k) for k in range(1, near)]
    far_sum = swap(merge(near_sets, terms, cols), near)
    terms = [sums[0]] + [swap(sums[k], k) for k in range(1, near)]
    keep, give = finish(near_sets, r.reshape(1), terms, far_sum)
    got = across(give)
    pair = jnp.where(r == 0, jnp.stack([keep, got], axis=1), jnp.stack([got, keep], axis=1))
    return pair.reshape(nb * FB, cols // cores)


def solution(mesh):
    in_specs = (
        P(("groups", "dom"), None),
        P("groups"),
        P(("groups", "dom"), None),
        P(("groups", "dom", "rows"), None),
        P(("groups", "dom", "rows")),
        P(("groups", "dom", "rows"), None, None),
        P(("groups", "dom", "rows"), None, None),
        P(("groups", "dom", "rows"), None),
        P(None, "groups"),
        P("groups"),
    )
    out_specs = P(("groups", "dom"), "rows")

    def run(*args):
        n, cores = mesh.shape["dom"], mesh.shape["rows"]
        rows_here = args[0].shape[0] // (mesh.shape["groups"] * n)
        split = rows_here % FB == 0 and cores == 2 and n >= 4 and n & (n - 1) == 0
        body = per_device if split else per_device_any
        return jax.shard_map(body, mesh=mesh, in_specs=in_specs, out_specs=out_specs, check_vma=False)(*args)

    return run
```

```python
import functools
import math

import jax
import jax.numpy as jnp
from jax import lax
from jax.experimental import pallas as pl
from jax.experimental.pallas import tpu as pltpu
from jax.sharding import PartitionSpec as P

FB = 128
TMAX = 4
UMAX = 8
MIB = 1024 * 1024


def coulomb(centre_x, centre_y, centre_z, spread, point_x, point_y, point_z):
    dist = (centre_x - point_x) ** 2 + (centre_y - point_y) ** 2 + (centre_z - point_z) ** 2
    return 1.0 / jnp.sqrt(dist + spread * spread)


def lookup_owner(owner, block_ids):
    match = block_ids[:, None] == jnp.arange(owner.shape[0], dtype=jnp.int32)[None, :]
    return jnp.sum(jnp.where(match, owner[None, :], 0), axis=1)


def answer_for(density, column_sets):
    rows_here = density.shape[0]
    sources, wanted = column_sets.shape
    blocked = density.reshape(rows_here, density.shape[1] // FB, FB)
    picked = jnp.take(blocked, column_sets.reshape(-1), axis=1)
    return picked.reshape(rows_here, sources, wanted * FB).transpose(1, 0, 2)


def spread_rows(terms, stored, block_count, sources):
    columns = terms.shape[1]
    expanded = jnp.zeros((block_count, FB, columns), jnp.float32)
    expanded = expanded.at[stored].set(terms.reshape(UMAX, FB, columns))
    return expanded.reshape(sources, block_count * FB // sources, columns)


def collect(returned, column_sets, block_count):
    sources, rows_here, columns = returned.shape
    wanted = column_sets.shape[1]
    pieces = returned.reshape(sources, rows_here, wanted, FB).transpose(1, 0, 2, 3)
    pieces = pieces.reshape(rows_here, sources * wanted, FB)
    total = jnp.zeros((rows_here, block_count, FB), jnp.float32)
    total = total.at[:, column_sets.reshape(-1)].add(pieces)
    return total.reshape(rows_here, block_count * FB)


def per_device_any(density, owner, touched, blocks, counts, basis, points, weights, centers, widths):
    rows_count = lax.axis_size("rows")
    rows_index = lax.axis_index("rows")
    batches = blocks.shape[0]
    block_count = owner.shape[0]
    width = TMAX * FB
    share = UMAX // rows_count
    own_set = touched[0]
    all_sets = lax.all_gather(touched, "dom", axis=0, tiled=True)
    sources = all_sets.shape[0]
    half_sets = lax.dynamic_slice_in_dim(all_sets, rows_index * share, share, 1)
    got = lax.all_to_all(
        answer_for(density, all_sets), "dom", split_axis=0, concat_axis=0, tiled=True
    )
    panel = got.reshape(block_count * FB, UMAX * FB)
    stored = lookup_owner(owner, own_set)
    tile = jnp.take(panel.reshape(block_count, FB, UMAX * FB), stored, axis=0).reshape(
        UMAX, FB, UMAX, FB
    )
    centre_blocks = centers.reshape(3, block_count, FB)
    spread_blocks = widths.reshape(block_count, FB)
    slot_ids = jnp.arange(TMAX, dtype=jnp.int32)
    group = math.gcd(batches, 8)
    turns = batches // group

    def work(total, item):
        slots, count, values, coords, quad = item
        gid = jnp.take(own_set, slots.reshape(-1), axis=0)
        active = (slot_ids[None, :] < count[:, None]).astype(jnp.float32)
        rowmask = jnp.repeat(active, FB, axis=1)[:, :, None]
        xmask = jnp.where(rowmask > 0, values, jnp.zeros_like(values))
        xweighted = (xmask.astype(jnp.float32) * quad[:, None, :]).astype(jnp.bfloat16)
        dloc = tile[slots[:, :, None], :, slots[:, None, :], :]
        dloc = dloc.transpose(0, 1, 3, 2, 4).reshape(group, width, width)
        centre = jnp.take(centre_blocks, gid, axis=1).reshape(3, group, width)
        spread = jnp.take(spread_blocks, gid, axis=0).reshape(group, width)
        vfac = coulomb(
            centre[0][:, :, None],
            centre[1][:, :, None],
            centre[2][:, :, None],
            spread[:, :, None],
            coords[:, 0][:, None, :],
            coords[:, 1][:, None, :],
            coords[:, 2][:, None, :],
        )
        gval = jnp.einsum("brc,bcg->brg", dloc, xmask, preferred_element_type=jnp.float32)
        fval = (gval * vfac * rowmask).astype(jnp.bfloat16)
        parts = jnp.einsum("brg,bcg->brc", fval, xweighted, preferred_element_type=jnp.float32)
        pieces = parts.reshape(group, TMAX, FB, TMAX, FB).transpose(0, 1, 3, 2, 4)
        total = total.at[slots[:, :, None], :, slots[:, None, :], :].add(pieces)
        return (total, None)

    items = (
        blocks.reshape(turns, group, TMAX),
        counts.reshape(turns, group),
        basis.reshape(turns, group, width, basis.shape[2]),
        points.reshape(turns, group, 3, points.shape[2]),
        weights.reshape(turns, group, weights.shape[1]),
    )
    start = jnp.zeros((UMAX, FB, UMAX, FB), jnp.float32)
    local_sum, _ = lax.scan(work, start, items)
    local_flat = local_sum.reshape(UMAX * FB, UMAX * FB)
    halved = lax.psum_scatter(local_flat, "rows", scatter_dimension=1, tiled=True)
    returned = lax.all_to_all(
        spread_rows(halved, stored, block_count, sources),
        "dom",
        split_axis=0,
        concat_axis=0,
        tiled=True,
    )
    gathered_terms = collect(returned, half_sets, block_count)
    summed = lax.psum_scatter(gathered_terms, "rows", scatter_dimension=1, tiled=True)
    return summed.astype(jnp.bfloat16)


def call(kernel, scalars, arrays, in_specs, out_shapes, out_specs, scratch, grid=(1,), cost=None, vmem=12):
    return pl.pallas_call(
        kernel,
        grid_spec=pltpu.PrefetchScalarGridSpec(
            num_scalar_prefetch=len(scalars),
            grid=grid,
            in_specs=in_specs,
            out_specs=out_specs,
            scratch_shapes=scratch,
        ),
        out_shape=out_shapes,
        cost_estimate=pl.CostEstimate(flops=cost[0], bytes_accessed=cost[1], transcendentals=0),
        compiler_params=pltpu.CompilerParams(vmem_limit_bytes=vmem * MIB),
    )(*scalars, *arrays)


def whole(shape):
    return pl.BlockSpec(shape, lambda *_: (0,) * len(shape))


def pick_kernel(sets, full, *outs):
    for k, out in enumerate(outs):
        for q in range(UMAX):
            block = sets[k * UMAX + q]
            out[:, :, q * FB : (q + 1) * FB] = full[:, :, pl.ds(pl.multiple_of(block * FB, FB), FB)]


def pick(sets, full, peers):
    nb, sub, cols = full.shape
    shape = (nb, sub, UMAX * FB)
    return call(
        pick_kernel,
        [sets],
        [full],
        [whole(full.shape)],
        [jax.ShapeDtypeStruct(shape, full.dtype)] * peers,
        [whole(shape)] * peers,
        [],
        cost=(0, 2 * nb * sub * (cols + peers * UMAX * FB)),
    )


def add_up(sets, terms, total):
    total[...] = jnp.zeros(total.shape, total.dtype)
    for k, term in enumerate(terms):
        for q in range(UMAX):
            cols = pl.ds(pl.multiple_of(sets[k * UMAX + q] * FB, FB), FB)
            total[:, :, cols] += term[:, :, q * FB : (q + 1) * FB].astype(jnp.float32)


def merge_kernel(peers, sets, *refs):
    terms, out, total = refs[:peers], refs[peers], refs[peers + 1]
    add_up(sets, terms, total)
    out[...] = total[...].astype(out.dtype)


def merge(sets, terms, cols):
    nb, sub, wide = terms[0].shape
    shape = (nb, sub, cols)
    return call(
        functools.partial(merge_kernel, len(terms)),
        [sets],
        terms,
        [whole(t.shape) for t in terms],
        jax.ShapeDtypeStruct(shape, jnp.bfloat16),
        whole(shape),
        [pltpu.VMEM(shape, jnp.float32)],
        cost=(0, 2 * nb * sub * (cols + 5 * wide)),
    )


def finish_kernel(peers, sets, core, *refs):
    terms, fars = refs[:peers], refs[peers:-3]
    keep, give, total = refs[-3:]
    add_up(sets, terms, total)
    half = keep.shape[2]
    for out, side in ((keep, core[0]), (give, 1 - core[0])):
        cols = pl.ds(pl.multiple_of(side * half, FB), half)
        for b, far in enumerate(fars):
            out[b] = (total[b, :, cols] + far[0, :, cols].astype(jnp.float32)).astype(out.dtype)


def finish(sets, core, terms, fars):
    nb, sub, wide = terms[0].shape
    cols = fars[0].shape[2]
    shape = (nb, sub, cols // 2)
    return call(
        functools.partial(finish_kernel, len(terms)),
        [sets, core],
        [*terms, *fars],
        [whole(t.shape) for t in (*terms, *fars)],
        [jax.ShapeDtypeStruct(shape, jnp.bfloat16)] * 2,
        [whole(shape)] * 2,
        [pltpu.VMEM((nb, sub, cols), jnp.float32)],
        cost=(0, 2 * nb * sub * (2 * cols + 5 * wide)),
    )


def batch_kernel(group, pieces, split, order, lives, rows, cols, poss, *refs):
    xs, quads, centre = refs[0:2], refs[2], refs[3]
    parts = refs[4 : 4 + pieces]
    outs = refs[4 + pieces : -5]
    dense, acc, xbuf, sems, xsems = refs[-5:]
    nb, sub, wide = parts[0].shape
    spare = nb * pieces
    batches, _, pts = xbuf.shape
    half = batches // 2

    def fetch(j, act):
        b = order[j]
        for side in (0, 1):

            @pl.when((b >= half) if side else (b < half))
            def _():
                act(pltpu.make_async_copy(xs[side].at[b - half * side], xbuf.at[j], xsems.at[j]))

    copies = [
        pltpu.make_async_copy(part, dense.at[pl.ds(nb * k, nb), :, pl.ds(0, wide)], sems.at[k])
        for k, part in enumerate(parts)
    ]
    for copy in copies:
        copy.start()

    @pl.loop(0, batches)
    def _(j):
        fetch(j, lambda copy: copy.start())

    acc[...] = jnp.zeros(acc.shape, acc.dtype)
    dense[:, :, wide:] = jnp.zeros((spare + 1, sub, FB), dense.dtype)
    dense[spare, :, :wide] = jnp.zeros((sub, wide), dense.dtype)
    for copy in copies:
        copy.wait()

    def lanes(col):
        return jnp.concatenate([col] * (pts // FB), axis=1)

    def one(j, live):
        b = order[j]
        row = [rows[b * TMAX + s] for s in range(live)]
        col = [pl.ds(pl.multiple_of(cols[b * TMAX + s] * FB, FB), FB) for s in range(live)]
        pos = [poss[b * TMAX + s] for s in range(live)]
        x = xbuf[j, : live * FB, :]
        quad = quads[b]
        d = jnp.concatenate(
            [
                jnp.concatenate([dense[row[s], :, col[t]] for t in range(live)], axis=1)
                for s in range(live)
            ],
            axis=0,
        )
        gval = jnp.dot(d, x, preferred_element_type=jnp.float32)
        fval = []
        for s in range(live):
            dist = None
            for axis in range(3):
                diff = lanes(centre[axis, pos[s]]) - quad[axis : axis + 1, :]
                dist = diff * diff if dist is None else dist + diff * diff
            dist = dist + lanes(centre[3, pos[s]])
            fval.append((gval[s * sub : (s + 1) * sub] * lax.rsqrt(dist)).astype(jnp.bfloat16))
        fval = jnp.concatenate(fval, axis=0)
        xw = (x.astype(jnp.float32) * quad[3:4, :]).astype(jnp.bfloat16)
        part = lax.dot_general(
            fval, xw, (((1,), (1,)), ((), ())), preferred_element_type=jnp.float32
        )
        return row, col, part

    @pl.loop(0, batches // group)
    def _(h):
        @pl.loop(0, group)
        def _(u):
            fetch(h * group + u, lambda copy: copy.wait())

        for live in range(2, TMAX + 1):

            @pl.when(lives[h] == live)
            def _():
                for row, col, part in [one(h * group + u, live) for u in range(group)]:
                    for s in range(live):
                        for t in range(live):
                            acc[row[s], :, col[t]] += part[s * sub : (s + 1) * sub, t * FB : (t + 1) * FB]

    for k, out in enumerate(outs):
        size = out.shape[0]
        out[...] = acc[size * k : size * (k + 1), :, :wide].astype(out.dtype)


def batch_sums(order, lives, rows, cols, poss, xs, quads, centre, parts, split):
    _, width, pts = xs[0].shape
    batches = order.shape[0]
    group = batches // lives.shape[0]
    nb, sub, wide = parts[0].shape
    pieces = len(parts)
    size = 1 if split else nb
    out_shapes = [
        jax.ShapeDtypeStruct((size, sub, wide), jnp.bfloat16 if k else jnp.float32)
        for k in range(pieces)
        for _ in range(nb // size)
    ]
    flops = 2 * batches * 2 * width * (width // 2) * pts
    return call(
        functools.partial(batch_kernel, group, pieces, split),
        [order, lives, rows, cols, poss],
        [*xs, quads, centre, *parts],
        [pl.BlockSpec(memory_space=pl.ANY)] * 2
        + [whole(quads.shape), whole(centre.shape)]
        + [pl.BlockSpec(memory_space=pl.ANY)] * pieces,
        out_shapes,
        [whole((size, sub, wide))] * len(out_shapes),
        [
            pltpu.VMEM((nb * pieces + 1, sub, wide + FB), jnp.bfloat16),
            pltpu.VMEM((nb * pieces + 1, sub, wide + FB), jnp.float32),
            pltpu.VMEM((batches, width, pts), jnp.bfloat16),
            pltpu.SemaphoreType.DMA((pieces,)),
            pltpu.SemaphoreType.DMA((batches,)),
        ],
        cost=(flops, 2 * batches * width * pts),
        vmem=32,
    )


def sort_by_count(counts, group):
    n = counts.shape[0]
    ids = jnp.arange(n, dtype=jnp.int32)
    ahead = (counts[None, :] > counts[:, None]) | (
        (counts[None, :] == counts[:, None]) & (ids[None, :] < ids[:, None])
    )
    rank = jnp.sum(ahead.astype(jnp.int32), axis=1)
    place = rank[None, :] == ids[:, None]
    order = jnp.sum(jnp.where(place, ids[None, :], 0), axis=1)
    lives = jnp.sum(jnp.where(place[::group], counts[None, :], 0), axis=1)
    return order, lives


def per_device(density, owner, touched, blocks, counts, basis, points, weights, centers, widths):
    n = lax.axis_size("dom")
    cores = lax.axis_size("rows")
    i = lax.axis_index("dom")
    r = lax.axis_index("rows")
    nb = density.shape[0] // FB
    sub = FB // cores
    cols = density.shape[1]
    block_count = owner.shape[0]
    near = n // 2

    def swap(x, k):
        return lax.ppermute(x, "dom", [(a, a ^ k) for a in range(n)])

    def across(x):
        return lax.ppermute(x, "rows", [(a, cores - 1 - a) for a in range(cores)])

    own = lax.dynamic_index_in_dim(density.reshape(nb, cores, sub, cols), r, 1, keepdims=False)
    own, touched, basis, points = lax.optimization_barrier((own, touched, basis, points))
    far = swap(own, near)
    near_sets = jnp.concatenate([touched] + [swap(touched, k) for k in range(1, near)], axis=0).reshape(-1)

    pts = points.shape[2]
    table = jnp.concatenate([blocks, counts[:, None]], axis=1).astype(jnp.float32)
    table = jnp.pad(table, ((0, 0), (0, pts - table.shape[1])))
    quads = jnp.concatenate([points, weights[:, None, :], table[:, None, :]], axis=1)
    quads_b = across(quads)
    basis_b = across(basis)
    quads = jnp.concatenate([quads, quads_b], axis=0)
    table = quads[:, 4, : TMAX + 1].astype(jnp.int32)
    slots, live = table[:, :TMAX], table[:, TMAX]
    order, lives = sort_by_count(live, math.gcd(live.shape[0], 4))

    own_set = touched[0]
    stored = lookup_owner(owner, own_set)
    kbs = jnp.bitwise_xor(stored // nb, i) * nb + stored % nb
    active = jnp.arange(TMAX, dtype=jnp.int32)[None, :] < live[:, None]
    hits = slots[:, :, None] == jnp.arange(UMAX, dtype=jnp.int32)
    kb = jnp.sum(jnp.where(hits, kbs, 0), axis=2)
    spare = nb * near
    col = jnp.where(active, slots, UMAX).reshape(-1)
    rows_near = jnp.where(active & (kb < spare), kb, spare).reshape(-1)
    rows_far = jnp.where(active & (kb >= spare), kb - spare, spare).reshape(-1)
    slots = slots.reshape(-1)

    shaped = jnp.concatenate([centers, (widths * widths)[None]], axis=0).reshape(4, block_count, cores, sub)
    shaped = lax.dynamic_index_in_dim(shaped, r, 2, keepdims=False)
    centre = jnp.take(shaped, own_set, axis=1)
    centre = jnp.broadcast_to(centre[..., None], (4, UMAX, sub, FB))

    near_sets, own, order = lax.optimization_barrier((near_sets, own, order))
    picked = pick(near_sets, own, near)
    parts = [picked[0]] + [swap(picked[k], k) for k in range(1, near)]
    picked = pick(near_sets, far, near)
    far_parts = [picked[0]] + [swap(picked[k], k) for k in range(1, near)]
    order, picked = lax.optimization_barrier((order, picked))

    common = (slots, (basis, basis_b), quads, centre)
    sums = batch_sums(order, lives, rows_near, col, *common, parts, False)
    far_sums = batch_sums(order, lives, rows_far, col, *common, far_parts, True)
    terms = [sums[0]] + [swap(sums[k], k) for k in range(1, near)]
    chunks = [[far_sums[b]] + [swap(far_sums[nb * k + b], k) for k in range(1, near)] for b in range(nb)]
    far_terms = [swap(merge(near_sets, chunk, cols), near) for chunk in chunks]
    keep, give = finish(near_sets, r.reshape(1), terms, far_terms)
    got = across(give)
    pair = jnp.where(r == 0, jnp.stack([keep, got], axis=1), jnp.stack([got, keep], axis=1))
    return pair.reshape(nb * FB, cols // cores)


def solution(mesh):
    in_specs = (
        P(("groups", "dom"), None),
        P("groups"),
        P(("groups", "dom"), None),
        P(("groups", "dom", "rows"), None),
        P(("groups", "dom", "rows")),
        P(("groups", "dom", "rows"), None, None),
        P(("groups", "dom", "rows"), None, None),
        P(("groups", "dom", "rows"), None),
        P(None, "groups"),
        P("groups"),
    )
    out_specs = P(("groups", "dom"), "rows")

    def run(*args):
        n, cores = mesh.shape["dom"], mesh.shape["rows"]
        rows_here = args[0].shape[0] // (mesh.shape["groups"] * n)
        split = rows_here % FB == 0 and cores == 2 and n >= 4 and n & (n - 1) == 0
        body = per_device if split else per_device_any
        return jax.shard_map(body, mesh=mesh, in_specs=in_specs, out_specs=out_specs, check_vma=False)(*args)

    return run
```

```python
import functools
import math

import jax
import jax.numpy as jnp
from jax import lax
from jax.experimental import pallas as pl
from jax.experimental.pallas import tpu as pltpu
from jax.sharding import PartitionSpec as P

FB = 128
TMAX = 4
UMAX = 8
MIB = 1024 * 1024


def coulomb(centre_x, centre_y, centre_z, spread, point_x, point_y, point_z):
    dist = (centre_x - point_x) ** 2 + (centre_y - point_y) ** 2 + (centre_z - point_z) ** 2
    return 1.0 / jnp.sqrt(dist + spread * spread)


def lookup_owner(owner, block_ids):
    match = block_ids[:, None] == jnp.arange(owner.shape[0], dtype=jnp.int32)[None, :]
    return jnp.sum(jnp.where(match, owner[None, :], 0), axis=1)


def answer_for(density, column_sets):
    rows_here = density.shape[0]
    sources, wanted = column_sets.shape
    blocked = density.reshape(rows_here, density.shape[1] // FB, FB)
    picked = jnp.take(blocked, column_sets.reshape(-1), axis=1)
    return picked.reshape(rows_here, sources, wanted * FB).transpose(1, 0, 2)


def spread_rows(terms, stored, block_count, sources):
    columns = terms.shape[1]
    expanded = jnp.zeros((block_count, FB, columns), jnp.float32)
    expanded = expanded.at[stored].set(terms.reshape(UMAX, FB, columns))
    return expanded.reshape(sources, block_count * FB // sources, columns)


def collect(returned, column_sets, block_count):
    sources, rows_here, columns = returned.shape
    wanted = column_sets.shape[1]
    pieces = returned.reshape(sources, rows_here, wanted, FB).transpose(1, 0, 2, 3)
    pieces = pieces.reshape(rows_here, sources * wanted, FB)
    total = jnp.zeros((rows_here, block_count, FB), jnp.float32)
    total = total.at[:, column_sets.reshape(-1)].add(pieces)
    return total.reshape(rows_here, block_count * FB)


def per_device_any(density, owner, touched, blocks, counts, basis, points, weights, centers, widths):
    rows_count = lax.axis_size("rows")
    rows_index = lax.axis_index("rows")
    batches = blocks.shape[0]
    block_count = owner.shape[0]
    width = TMAX * FB
    share = UMAX // rows_count
    own_set = touched[0]
    all_sets = lax.all_gather(touched, "dom", axis=0, tiled=True)
    sources = all_sets.shape[0]
    half_sets = lax.dynamic_slice_in_dim(all_sets, rows_index * share, share, 1)
    got = lax.all_to_all(
        answer_for(density, all_sets), "dom", split_axis=0, concat_axis=0, tiled=True
    )
    panel = got.reshape(block_count * FB, UMAX * FB)
    stored = lookup_owner(owner, own_set)
    tile = jnp.take(panel.reshape(block_count, FB, UMAX * FB), stored, axis=0).reshape(
        UMAX, FB, UMAX, FB
    )
    centre_blocks = centers.reshape(3, block_count, FB)
    spread_blocks = widths.reshape(block_count, FB)
    slot_ids = jnp.arange(TMAX, dtype=jnp.int32)
    group = math.gcd(batches, 8)
    turns = batches // group

    def work(total, item):
        slots, count, values, coords, quad = item
        gid = jnp.take(own_set, slots.reshape(-1), axis=0)
        active = (slot_ids[None, :] < count[:, None]).astype(jnp.float32)
        rowmask = jnp.repeat(active, FB, axis=1)[:, :, None]
        xmask = jnp.where(rowmask > 0, values, jnp.zeros_like(values))
        xweighted = (xmask.astype(jnp.float32) * quad[:, None, :]).astype(jnp.bfloat16)
        dloc = tile[slots[:, :, None], :, slots[:, None, :], :]
        dloc = dloc.transpose(0, 1, 3, 2, 4).reshape(group, width, width)
        centre = jnp.take(centre_blocks, gid, axis=1).reshape(3, group, width)
        spread = jnp.take(spread_blocks, gid, axis=0).reshape(group, width)
        vfac = coulomb(
            centre[0][:, :, None],
            centre[1][:, :, None],
            centre[2][:, :, None],
            spread[:, :, None],
            coords[:, 0][:, None, :],
            coords[:, 1][:, None, :],
            coords[:, 2][:, None, :],
        )
        gval = jnp.einsum("brc,bcg->brg", dloc, xmask, preferred_element_type=jnp.float32)
        fval = (gval * vfac * rowmask).astype(jnp.bfloat16)
        parts = jnp.einsum("brg,bcg->brc", fval, xweighted, preferred_element_type=jnp.float32)
        pieces = parts.reshape(group, TMAX, FB, TMAX, FB).transpose(0, 1, 3, 2, 4)
        total = total.at[slots[:, :, None], :, slots[:, None, :], :].add(pieces)
        return (total, None)

    items = (
        blocks.reshape(turns, group, TMAX),
        counts.reshape(turns, group),
        basis.reshape(turns, group, width, basis.shape[2]),
        points.reshape(turns, group, 3, points.shape[2]),
        weights.reshape(turns, group, weights.shape[1]),
    )
    start = jnp.zeros((UMAX, FB, UMAX, FB), jnp.float32)
    local_sum, _ = lax.scan(work, start, items)
    local_flat = local_sum.reshape(UMAX * FB, UMAX * FB)
    halved = lax.psum_scatter(local_flat, "rows", scatter_dimension=1, tiled=True)
    returned = lax.all_to_all(
        spread_rows(halved, stored, block_count, sources),
        "dom",
        split_axis=0,
        concat_axis=0,
        tiled=True,
    )
    gathered_terms = collect(returned, half_sets, block_count)
    summed = lax.psum_scatter(gathered_terms, "rows", scatter_dimension=1, tiled=True)
    return summed.astype(jnp.bfloat16)


def call(kernel, scalars, arrays, in_specs, out_shapes, out_specs, scratch, grid=(1,), cost=None, vmem=12):
    return pl.pallas_call(
        kernel,
        grid_spec=pltpu.PrefetchScalarGridSpec(
            num_scalar_prefetch=len(scalars),
            grid=grid,
            in_specs=in_specs,
            out_specs=out_specs,
            scratch_shapes=scratch,
        ),
        out_shape=out_shapes,
        cost_estimate=pl.CostEstimate(flops=cost[0], bytes_accessed=cost[1], transcendentals=0),
        compiler_params=pltpu.CompilerParams(vmem_limit_bytes=vmem * MIB),
    )(*scalars, *arrays)


def whole(shape):
    return pl.BlockSpec(shape, lambda *_: (0,) * len(shape))


def pick_kernel(peers, *refs):
    sets, full, outs = refs[:peers], refs[peers], refs[peers + 1 :]
    for k in range(peers):
        for q in range(UMAX):
            cols = pl.ds(pl.multiple_of(sets[k][0, q] * FB, FB), FB)
            outs[k][:, :, q * FB : (q + 1) * FB] = full[:, :, cols]


def pick(sets, full):
    nb, sub, cols = full.shape
    shape = (nb, sub, UMAX * FB)
    peers = len(sets)
    return call(
        functools.partial(pick_kernel, peers),
        sets,
        [full],
        [whole(full.shape)],
        [jax.ShapeDtypeStruct(shape, full.dtype)] * peers,
        [whole(shape)] * peers,
        [],
        cost=(0, 2 * nb * sub * (cols + peers * UMAX * FB)),
    )


def centre_kernel(own_set, core, centers, widths, out, turned):
    sub = out.shape[2]
    for p in range(UMAX):
        cols = pl.ds(pl.multiple_of(own_set[0, p] * FB, FB), FB)
        width = widths[:, cols]
        rows = jnp.concatenate([centers[:, cols], width * width, jnp.zeros((4, FB), jnp.float32)], axis=0)
        turned[...] = rows.T
        start = pl.multiple_of(core[0] * sub, sub)
        for c in range(4):
            out[c, p] = jnp.broadcast_to(turned[pl.ds(start, sub), c : c + 1], (sub, FB))


def centre_rows(own_set, core, centers, widths, sub):
    shape = (4, UMAX, sub, FB)
    return call(
        centre_kernel,
        [own_set, core],
        [centers, widths.reshape(1, -1)],
        [whole(centers.shape), whole((1, widths.shape[0]))],
        jax.ShapeDtypeStruct(shape, jnp.float32),
        whole(shape),
        [pltpu.VMEM((FB, 8), jnp.float32)],
        cost=(0, 2 * 4 * UMAX * sub * FB * 4),
    )


def table_kernel(nb, near, group, me, owner, own_set, blocks_a, blocks_b, counts_a, counts_b, *refs):
    order, lives, rows_near, rows_far, cols, slots, kbs, fill = refs
    half = counts_a.shape[0]
    spare = nb * near
    for p in range(UMAX):
        stored = owner[own_set[0, p]]
        kbs[p] = (lax.div(stored, nb) ^ me[0]) * nb + lax.rem(stored, nb)
    for c in range(TMAX + 1):
        fill[c] = 0

    def each(todo):
        for side, (blocks, counts) in enumerate(((blocks_a, counts_a), (blocks_b, counts_b))):

            @pl.loop(0, half)
            def _(b):
                todo(side, b, blocks, counts[b])

    def tally(side, b, blocks, count):
        fill[count] = fill[count] + 1

    each(tally)
    place = 0
    for c in range(TMAX, -1, -1):
        many = fill[c]
        fill[c] = place
        place = place + many

    def put(side, b, blocks, count):
        j = fill[count]
        fill[count] = j + 1
        order[j] = side * half + b

        @pl.when(lax.rem(j, group) == 0)
        def _():
            lives[lax.div(j, group)] = count

        for s in range(TMAX):
            pos = blocks[b, s]
            kb = kbs[pos]
            on = s < count
            at = j * TMAX + s
            slots[at] = pos
            cols[at] = jnp.where(on, pos, UMAX)
            rows_near[at] = jnp.where(on & (kb < spare), kb, spare)
            rows_far[at] = jnp.where(on & (kb >= spare), kb - spare, spare)

    each(put)


def batch_tables(me, owner, own_set, blocks, counts, nb, near):
    batches = 2 * counts[0].shape[0]
    group = math.gcd(batches, 4)
    sizes = (batches, batches // group) + (batches * TMAX,) * 4
    return call(
        functools.partial(table_kernel, nb, near, group),
        [me, owner, own_set, *blocks, *counts],
        [],
        [],
        [jax.ShapeDtypeStruct((size,), jnp.int32) for size in sizes],
        [pl.BlockSpec(memory_space=pltpu.SMEM)] * len(sizes),
        [pltpu.SMEM((UMAX,), jnp.int32), pltpu.SMEM((TMAX + 1,), jnp.int32)],
        cost=(0, 8 * batches * TMAX),
    )


def add_up(sets, terms, total):
    total[...] = jnp.zeros(total.shape, total.dtype)
    for k, term in enumerate(terms):
        for q in range(UMAX):
            cols = pl.ds(pl.multiple_of(sets[k][0, q] * FB, FB), FB)
            total[:, :, cols] += term[:, :, q * FB : (q + 1) * FB].astype(jnp.float32)


def merge_kernel(peers, *refs):
    sets, terms, out, total = refs[:peers], refs[peers : 2 * peers], refs[-2], refs[-1]
    add_up(sets, terms, total)
    out[...] = total[...].astype(out.dtype)


def merge(sets, terms, cols):
    nb, sub, wide = terms[0].shape
    shape = (nb, sub, cols)
    return call(
        functools.partial(merge_kernel, len(terms)),
        sets,
        terms,
        [whole(t.shape) for t in terms],
        jax.ShapeDtypeStruct(shape, jnp.bfloat16),
        whole(shape),
        [pltpu.VMEM(shape, jnp.float32)],
        cost=(0, 2 * nb * sub * (cols + 5 * wide)),
    )


def finish_kernel(peers, *refs):
    sets, core = refs[:peers], refs[peers]
    terms, fars = refs[peers + 1 : 2 * peers + 1], refs[2 * peers + 1 : -3]
    keep, give, total = refs[-3:]
    add_up(sets, terms, total)
    half = keep.shape[2]
    for out, side in ((keep, core[0]), (give, 1 - core[0])):
        cols = pl.ds(pl.multiple_of(side * half, FB), half)
        for b, far in enumerate(fars):
            out[b] = (total[b, :, cols] + far[0, :, cols].astype(jnp.float32)).astype(out.dtype)


def finish(sets, core, terms, fars):
    nb, sub, wide = terms[0].shape
    cols = fars[0].shape[2]
    shape = (nb, sub, cols // 2)
    return call(
        functools.partial(finish_kernel, len(terms)),
        [*sets, core],
        [*terms, *fars],
        [whole(t.shape) for t in (*terms, *fars)],
        [jax.ShapeDtypeStruct(shape, jnp.bfloat16)] * 2,
        [whole(shape)] * 2,
        [pltpu.VMEM((nb, sub, cols), jnp.float32)],
        cost=(0, 2 * nb * sub * (2 * cols + 5 * wide)),
    )


def batch_kernel(group, pieces, order, lives, rows, cols, poss, *refs):
    xs, coords, weights, centre = refs[0:2], refs[2:4], refs[4:6], refs[6]
    parts = refs[7 : 7 + pieces]
    outs = refs[7 + pieces : -8]
    dense, acc, xbuf, pbuf, wbuf, sems, xsems, qsems = refs[-8:]
    nb, sub, wide = parts[0].shape
    spare = nb * pieces
    batches, _, pts = xbuf.shape
    half = batches // 2

    def fetch(j, act):
        b = order[j]
        for side in (0, 1):

            @pl.when((b >= half) if side else (b < half))
            def _():
                act(pltpu.make_async_copy(xs[side].at[b - half * side], xbuf.at[j], xsems.at[j]))

    copies = [
        pltpu.make_async_copy(part, dense.at[pl.ds(nb * k, nb), :, pl.ds(0, wide)], sems.at[k])
        for k, part in enumerate(parts)
    ]
    for side in (0, 1):
        rest = pl.ds(half * side, half)
        copies.append(pltpu.make_async_copy(coords[side], pbuf.at[rest], qsems.at[side]))
        copies.append(pltpu.make_async_copy(weights[side], wbuf.at[rest], qsems.at[2 + side]))
    for copy in copies:
        copy.start()

    @pl.loop(0, batches)
    def _(j):
        fetch(j, lambda copy: copy.start())

    acc[...] = jnp.zeros(acc.shape, acc.dtype)
    dense[:, :, wide:] = jnp.zeros((spare + 1, sub, FB), dense.dtype)
    dense[spare, :, :wide] = jnp.zeros((sub, wide), dense.dtype)
    for copy in copies:
        copy.wait()

    def lanes(col):
        return jnp.concatenate([col] * (pts // FB), axis=1)

    def one(j, live):
        b = order[j]
        row = [rows[j * TMAX + s] for s in range(live)]
        col = [pl.ds(pl.multiple_of(cols[j * TMAX + s] * FB, FB), FB) for s in range(live)]
        pos = [poss[j * TMAX + s] for s in range(live)]
        x = xbuf[j, : live * FB, :]
        point = pbuf[b]
        d = jnp.concatenate(
            [
                jnp.concatenate([dense[row[s], :, col[t]] for t in range(live)], axis=1)
                for s in range(live)
            ],
            axis=0,
        )
        gval = jnp.dot(d, x, preferred_element_type=jnp.float32)
        fval = []
        for s in range(live):
            dist = None
            for axis in range(3):
                diff = lanes(centre[axis, pos[s]]) - point[axis : axis + 1, :]
                dist = diff * diff if dist is None else dist + diff * diff
            dist = dist + lanes(centre[3, pos[s]])
            fval.append((gval[s * sub : (s + 1) * sub] * lax.rsqrt(dist)).astype(jnp.bfloat16))
        fval = jnp.concatenate(fval, axis=0)
        xw = (x.astype(jnp.float32) * wbuf[pl.ds(b, 1), :]).astype(jnp.bfloat16)
        part = lax.dot_general(
            fval, xw, (((1,), (1,)), ((), ())), preferred_element_type=jnp.float32
        )
        return row, col, part

    @pl.loop(0, batches // group)
    def _(h):
        @pl.loop(0, group)
        def _(u):
            fetch(h * group + u, lambda copy: copy.wait())

        for live in range(2, TMAX + 1):

            @pl.when(lives[h] == live)
            def _():
                for row, col, part in [one(h * group + u, live) for u in range(group)]:
                    for s in range(live):
                        for t in range(live):
                            acc[row[s], :, col[t]] += part[s * sub : (s + 1) * sub, t * FB : (t + 1) * FB]

    for k, out in enumerate(outs):
        size = out.shape[0]
        out[...] = acc[size * k : size * (k + 1), :, :wide].astype(out.dtype)


def batch_sums(order, lives, rows, cols, poss, xs, coords, weights, centre, parts, split):
    _, width, pts = xs[0].shape
    batches = order.shape[0]
    group = batches // lives.shape[0]
    nb, sub, wide = parts[0].shape
    pieces = len(parts)
    size = 1 if split else nb
    out_shapes = [
        jax.ShapeDtypeStruct((size, sub, wide), jnp.bfloat16 if k else jnp.float32)
        for k in range(pieces)
        for _ in range(nb // size)
    ]
    flops = 2 * batches * 2 * width * (width // 2) * pts
    return call(
        functools.partial(batch_kernel, group, pieces),
        [order, lives, rows, cols, poss],
        [*xs, *coords, *weights, centre, *parts],
        [pl.BlockSpec(memory_space=pltpu.HBM)] * 2
        + [pl.BlockSpec(memory_space=pl.ANY)] * 4
        + [whole(centre.shape)]
        + [pl.BlockSpec(memory_space=pl.ANY)] * pieces,
        out_shapes,
        [whole((size, sub, wide))] * len(out_shapes),
        [
            pltpu.VMEM((nb * pieces + 1, sub, wide + FB), jnp.bfloat16),
            pltpu.VMEM((nb * pieces + 1, sub, wide + FB), jnp.float32),
            pltpu.VMEM((batches, width, pts), jnp.bfloat16),
            pltpu.VMEM((batches, 3, pts), jnp.float32),
            pltpu.VMEM((batches, pts), jnp.float32),
            pltpu.SemaphoreType.DMA((pieces,)),
            pltpu.SemaphoreType.DMA((batches,)),
            pltpu.SemaphoreType.DMA((4,)),
        ],
        cost=(flops, 2 * batches * width * pts),
        vmem=32,
    )


def per_device(density, owner, touched, blocks, counts, basis, points, weights, centers, widths):
    n = lax.axis_size("dom")
    cores = lax.axis_size("rows")
    i = lax.axis_index("dom")
    r = lax.axis_index("rows")
    nb = density.shape[0] // FB
    sub = FB // cores
    cols = density.shape[1]
    near = n // 2
    core = r.reshape(1)

    def swap(x, k):
        return lax.ppermute(x, "dom", [(a, a ^ k) for a in range(n)])

    def across(x):
        return lax.ppermute(x, "rows", [(a, cores - 1 - a) for a in range(cores)])

    own = lax.dynamic_index_in_dim(density.reshape(nb, cores, sub, cols), r, 1, keepdims=False)
    far = swap(own, near)
    sets = [touched] + [swap(touched, k) for k in range(1, near)]
    both = [(x, across(x)) for x in (basis, points, weights, blocks, counts)]
    tables = batch_tables(i.reshape(1), owner, touched, both[3], both[4], nb, near)
    order, lives, rows_near, rows_far, col, slots = tables
    centre = centre_rows(touched, core, centers, widths, sub)

    picked = pick(sets, own)
    parts = [picked[0]] + [swap(picked[k], k) for k in range(1, near)]
    picked = pick(sets, far)
    far_parts = [picked[0]] + [swap(picked[k], k) for k in range(1, near)]
    order, _ = lax.optimization_barrier((order, picked[0]))

    common = (slots, *both[:3], centre)
    sums = batch_sums(order, lives, rows_near, col, *common, parts, False)
    order, _ = lax.optimization_barrier((order, sums[0]))
    far_sums = batch_sums(order, lives, rows_far, col, *common, far_parts, True)
    terms = [sums[0]] + [swap(sums[k], k) for k in range(1, near)]
    chunks = [[far_sums[b]] + [swap(far_sums[nb * k + b], k) for k in range(1, near)] for b in range(nb)]
    far_terms = [swap(merge(sets, chunk, cols), near) for chunk in chunks]
    keep, give = finish(sets, core, terms, far_terms)
    got = across(give)
    pair = jnp.where(r == 0, jnp.stack([keep, got], axis=1), jnp.stack([got, keep], axis=1))
    return pair.reshape(nb * FB, cols // cores)


def solution(mesh):
    in_specs = (
        P(("groups", "dom"), None),
        P("groups"),
        P(("groups", "dom"), None),
        P(("groups", "dom", "rows"), None),
        P(("groups", "dom", "rows")),
        P(("groups", "dom", "rows"), None, None),
        P(("groups", "dom", "rows"), None, None),
        P(("groups", "dom", "rows"), None),
        P(None, "groups"),
        P("groups"),
    )
    out_specs = P(("groups", "dom"), "rows")

    def run(*args):
        n, cores = mesh.shape["dom"], mesh.shape["rows"]
        rows_here = args[0].shape[0] // (mesh.shape["groups"] * n)
        split = rows_here % FB == 0 and cores == 2 and n >= 4 and n & (n - 1) == 0
        body = per_device if split else per_device_any
        return jax.shard_map(body, mesh=mesh, in_specs=in_specs, out_specs=out_specs, check_vma=False)(*args)

    return run
```

```python
import functools
import math

import jax
import jax.numpy as jnp
from jax import lax
from jax.experimental import pallas as pl
from jax.experimental.pallas import tpu as pltpu
from jax.sharding import PartitionSpec as P

FB = 128
TMAX = 4
UMAX = 8
MIB = 1024 * 1024


def coulomb(centre_x, centre_y, centre_z, spread, point_x, point_y, point_z):
    dist = (centre_x - point_x) ** 2 + (centre_y - point_y) ** 2 + (centre_z - point_z) ** 2
    return 1.0 / jnp.sqrt(dist + spread * spread)


def lookup_owner(owner, block_ids):
    match = block_ids[:, None] == jnp.arange(owner.shape[0], dtype=jnp.int32)[None, :]
    return jnp.sum(jnp.where(match, owner[None, :], 0), axis=1)


def answer_for(density, column_sets):
    rows_here = density.shape[0]
    sources, wanted = column_sets.shape
    blocked = density.reshape(rows_here, density.shape[1] // FB, FB)
    picked = jnp.take(blocked, column_sets.reshape(-1), axis=1)
    return picked.reshape(rows_here, sources, wanted * FB).transpose(1, 0, 2)


def spread_rows(terms, stored, block_count, sources):
    columns = terms.shape[1]
    expanded = jnp.zeros((block_count, FB, columns), jnp.float32)
    expanded = expanded.at[stored].set(terms.reshape(UMAX, FB, columns))
    return expanded.reshape(sources, block_count * FB // sources, columns)


def collect(returned, column_sets, block_count):
    sources, rows_here, columns = returned.shape
    wanted = column_sets.shape[1]
    pieces = returned.reshape(sources, rows_here, wanted, FB).transpose(1, 0, 2, 3)
    pieces = pieces.reshape(rows_here, sources * wanted, FB)
    total = jnp.zeros((rows_here, block_count, FB), jnp.float32)
    total = total.at[:, column_sets.reshape(-1)].add(pieces)
    return total.reshape(rows_here, block_count * FB)


def per_device_any(density, owner, touched, blocks, counts, basis, points, weights, centers, widths):
    rows_count = lax.axis_size("rows")
    rows_index = lax.axis_index("rows")
    batches = blocks.shape[0]
    block_count = owner.shape[0]
    width = TMAX * FB
    share = UMAX // rows_count
    own_set = touched[0]
    all_sets = lax.all_gather(touched, "dom", axis=0, tiled=True)
    sources = all_sets.shape[0]
    half_sets = lax.dynamic_slice_in_dim(all_sets, rows_index * share, share, 1)
    got = lax.all_to_all(
        answer_for(density, all_sets), "dom", split_axis=0, concat_axis=0, tiled=True
    )
    panel = got.reshape(block_count * FB, UMAX * FB)
    stored = lookup_owner(owner, own_set)
    tile = jnp.take(panel.reshape(block_count, FB, UMAX * FB), stored, axis=0).reshape(
        UMAX, FB, UMAX, FB
    )
    centre_blocks = centers.reshape(3, block_count, FB)
    spread_blocks = widths.reshape(block_count, FB)
    slot_ids = jnp.arange(TMAX, dtype=jnp.int32)
    group = math.gcd(batches, 8)
    turns = batches // group

    def work(total, item):
        slots, count, values, coords, quad = item
        gid = jnp.take(own_set, slots.reshape(-1), axis=0)
        active = (slot_ids[None, :] < count[:, None]).astype(jnp.float32)
        rowmask = jnp.repeat(active, FB, axis=1)[:, :, None]
        xmask = jnp.where(rowmask > 0, values, jnp.zeros_like(values))
        xweighted = (xmask.astype(jnp.float32) * quad[:, None, :]).astype(jnp.bfloat16)
        dloc = tile[slots[:, :, None], :, slots[:, None, :], :]
        dloc = dloc.transpose(0, 1, 3, 2, 4).reshape(group, width, width)
        centre = jnp.take(centre_blocks, gid, axis=1).reshape(3, group, width)
        spread = jnp.take(spread_blocks, gid, axis=0).reshape(group, width)
        vfac = coulomb(
            centre[0][:, :, None],
            centre[1][:, :, None],
            centre[2][:, :, None],
            spread[:, :, None],
            coords[:, 0][:, None, :],
            coords[:, 1][:, None, :],
            coords[:, 2][:, None, :],
        )
        gval = jnp.einsum("brc,bcg->brg", dloc, xmask, preferred_element_type=jnp.float32)
        fval = (gval * vfac * rowmask).astype(jnp.bfloat16)
        parts = jnp.einsum("brg,bcg->brc", fval, xweighted, preferred_element_type=jnp.float32)
        pieces = parts.reshape(group, TMAX, FB, TMAX, FB).transpose(0, 1, 3, 2, 4)
        total = total.at[slots[:, :, None], :, slots[:, None, :], :].add(pieces)
        return (total, None)

    items = (
        blocks.reshape(turns, group, TMAX),
        counts.reshape(turns, group),
        basis.reshape(turns, group, width, basis.shape[2]),
        points.reshape(turns, group, 3, points.shape[2]),
        weights.reshape(turns, group, weights.shape[1]),
    )
    start = jnp.zeros((UMAX, FB, UMAX, FB), jnp.float32)
    local_sum, _ = lax.scan(work, start, items)
    local_flat = local_sum.reshape(UMAX * FB, UMAX * FB)
    halved = lax.psum_scatter(local_flat, "rows", scatter_dimension=1, tiled=True)
    returned = lax.all_to_all(
        spread_rows(halved, stored, block_count, sources),
        "dom",
        split_axis=0,
        concat_axis=0,
        tiled=True,
    )
    gathered_terms = collect(returned, half_sets, block_count)
    summed = lax.psum_scatter(gathered_terms, "rows", scatter_dimension=1, tiled=True)
    return summed.astype(jnp.bfloat16)


def call(kernel, scalars, arrays, in_specs, out_shapes, out_specs, scratch, grid=(1,), cost=None, vmem=44):
    return pl.pallas_call(
        kernel,
        grid_spec=pltpu.PrefetchScalarGridSpec(
            num_scalar_prefetch=len(scalars),
            grid=grid,
            in_specs=in_specs,
            out_specs=out_specs,
            scratch_shapes=scratch,
        ),
        out_shape=out_shapes,
        cost_estimate=pl.CostEstimate(flops=cost[0], bytes_accessed=cost[1], transcendentals=0),
        compiler_params=pltpu.CompilerParams(vmem_limit_bytes=vmem * MIB),
    )(*scalars, *arrays)


def whole(shape):
    return pl.BlockSpec(shape, lambda *_: (0,) * len(shape))


def pick_kernel(peers, *refs):
    sets, full, outs = refs[:peers], refs[peers], refs[peers + 1 :]
    for k in range(peers):
        for q in range(UMAX):
            cols = pl.ds(pl.multiple_of(sets[k][0, q] * FB, FB), FB)
            outs[k][:, :, q * FB : (q + 1) * FB] = full[:, :, cols]


def pick(sets, full):
    nb, sub, cols = full.shape
    shape = (nb, sub, UMAX * FB)
    peers = len(sets)
    return call(
        functools.partial(pick_kernel, peers),
        sets,
        [full],
        [whole(full.shape)],
        [jax.ShapeDtypeStruct(shape, full.dtype)] * peers,
        [whole(shape)] * peers,
        [],
        cost=(0, 2 * nb * sub * (cols + peers * UMAX * FB)),
    )


def centre_kernel(own_set, core, centers, widths, out, turned):
    sub = out.shape[2]
    for p in range(UMAX):
        cols = pl.ds(pl.multiple_of(own_set[0, p] * FB, FB), FB)
        width = widths[:, cols]
        rows = jnp.concatenate([centers[:, cols], width * width, jnp.zeros((4, FB), jnp.float32)], axis=0)
        turned[...] = rows.T
        start = pl.multiple_of(core[0] * sub, sub)
        for c in range(4):
            out[c, p] = jnp.broadcast_to(turned[pl.ds(start, sub), c : c + 1], (sub, FB))


def centre_rows(own_set, core, centers, widths, sub):
    shape = (4, UMAX, sub, FB)
    return call(
        centre_kernel,
        [own_set, core],
        [centers, widths],
        [whole(centers.shape), whole(widths.shape)],
        jax.ShapeDtypeStruct(shape, jnp.float32),
        whole(shape),
        [pltpu.VMEM((FB, 8), jnp.float32)],
        cost=(0, 2 * 4 * UMAX * sub * FB * 4),
    )


def table_kernel(nb, near, group, me, owner, own_set, blocks_a, blocks_b, counts_a, counts_b, out, kbs, fill):
    half = counts_a.shape[0]
    at_lives, at_near, at_far, at_col, at_pos = table_places(2 * half, group)
    spare = nb * near
    for p in range(UMAX):
        stored = owner[own_set[0, p]]
        kbs[p] = (lax.div(stored, nb) ^ me[0]) * nb + lax.rem(stored, nb)
    for c in range(TMAX + 1):
        fill[c] = 0

    def each(todo):
        for side, (blocks, counts) in enumerate(((blocks_a, counts_a), (blocks_b, counts_b))):

            @pl.loop(0, half)
            def _(b):
                todo(side, b, blocks, counts[b])

    def tally(side, b, blocks, count):
        fill[count] = fill[count] + 1

    each(tally)
    place = 0
    for c in range(TMAX, -1, -1):
        many = fill[c]
        fill[c] = place
        place = place + many

    def put(side, b, blocks, count):
        j = fill[count]
        fill[count] = j + 1
        out[j] = side * half + b

        @pl.when(lax.rem(j, group) == 0)
        def _():
            out[at_lives + lax.div(j, group)] = count

        for s in range(TMAX):
            pos = blocks[b, s]
            kb = kbs[pos]
            on = s < count
            at = j * TMAX + s
            out[at_pos + at] = pos
            out[at_col + at] = jnp.where(on, pos, UMAX)
            out[at_near + at] = jnp.where(on & (kb < spare), kb, spare)
            out[at_far + at] = jnp.where(on & (kb >= spare), kb - spare, spare)

    each(put)


def table_places(batches, group):
    lives = batches
    near = lives + batches // group
    return lives, near, near + batches * TMAX, near + 2 * batches * TMAX, near + 3 * batches * TMAX


def batch_tables(me, owner, own_set, blocks, counts, nb, near):
    batches = 2 * counts[0].shape[0]
    group = math.gcd(batches, 4)
    size = table_places(batches, group)[-1] + batches * TMAX
    return call(
        functools.partial(table_kernel, nb, near, group),
        [me, owner, own_set, *blocks, *counts],
        [],
        [],
        jax.ShapeDtypeStruct((size,), jnp.int32),
        pl.BlockSpec(memory_space=pltpu.SMEM),
        [pltpu.SMEM((UMAX,), jnp.int32), pltpu.SMEM((TMAX + 1,), jnp.int32)],
        cost=(0, 8 * batches * TMAX),
    )


def add_up(sets, terms, total):
    total[...] = jnp.zeros(total.shape, total.dtype)
    for k, term in enumerate(terms):
        for q in range(UMAX):
            cols = pl.ds(pl.multiple_of(sets[k][0, q] * FB, FB), FB)
            total[:, :, cols] += term[:, :, q * FB : (q + 1) * FB].astype(jnp.float32)


def merge_kernel(peers, *refs):
    sets, terms, out, total = refs[:peers], refs[peers : 2 * peers], refs[-2], refs[-1]
    add_up(sets, terms, total)
    out[...] = total[...].astype(out.dtype)


def merge(sets, terms, cols):
    nb, sub, wide = terms[0].shape
    shape = (nb, sub, cols)
    return call(
        functools.partial(merge_kernel, len(terms)),
        sets,
        terms,
        [whole(t.shape) for t in terms],
        jax.ShapeDtypeStruct(shape, jnp.bfloat16),
        whole(shape),
        [pltpu.VMEM(shape, jnp.float32)],
        cost=(0, 2 * nb * sub * (cols + 5 * wide)),
    )


def finish_kernel(peers, *refs):
    sets, core = refs[:peers], refs[peers]
    terms, fars = refs[peers + 1 : 2 * peers + 1], refs[2 * peers + 1 : -3]
    keep, give, total = refs[-3:]
    add_up(sets, terms, total)
    half = keep.shape[2]
    for out, side in ((keep, core[0]), (give, 1 - core[0])):
        cols = pl.ds(pl.multiple_of(side * half, FB), half)
        for b, far in enumerate(fars):
            out[b] = (total[b, :, cols] + far[0, :, cols].astype(jnp.float32)).astype(out.dtype)


def finish(sets, core, terms, fars):
    nb, sub, wide = terms[0].shape
    cols = fars[0].shape[2]
    shape = (nb, sub, cols // 2)
    return call(
        functools.partial(finish_kernel, len(terms)),
        [*sets, core],
        [*terms, *fars],
        [whole(t.shape) for t in (*terms, *fars)],
        [jax.ShapeDtypeStruct(shape, jnp.bfloat16)] * 2,
        [whole(shape)] * 2,
        [pltpu.VMEM((nb, sub, cols), jnp.float32)],
        cost=(0, 2 * nb * sub * (2 * cols + 5 * wide)),
    )


def batch_kernel(group, pieces, split, table, *refs):
    xs, coords, weights, centre = refs[0:2], refs[2:4], refs[4:6], refs[6]
    parts = refs[7 : 7 + pieces]
    outs = refs[7 + pieces : -8]
    dense, acc, xbuf, pbuf, wbuf, sems, xsems, qsems = refs[-8:]
    nb, sub, wide = parts[0].shape
    spare = nb * pieces
    batches, _, pts = xbuf.shape
    half = batches // 2
    at_lives, at_near, at_far, at_col, at_pos = table_places(batches, group)
    at_row = at_far if split else at_near

    def fetch(j, act):
        b = table[j]
        for side in (0, 1):

            @pl.when((b >= half) if side else (b < half))
            def _():
                act(pltpu.make_async_copy(xs[side].at[b - half * side], xbuf.at[j], xsems.at[j]))

    copies = [
        pltpu.make_async_copy(part, dense.at[pl.ds(nb * k, nb), :, pl.ds(0, wide)], sems.at[k])
        for k, part in enumerate(parts)
    ]
    for side in (0, 1):
        rest = pl.ds(half * side, half)
        copies.append(pltpu.make_async_copy(coords[side], pbuf.at[:, rest], qsems.at[side]))
        copies.append(pltpu.make_async_copy(weights[side], wbuf.at[rest], qsems.at[2 + side]))
    for copy in copies:
        copy.start()

    @pl.loop(0, batches)
    def _(j):
        fetch(j, lambda copy: copy.start())

    acc[...] = jnp.zeros(acc.shape, acc.dtype)
    dense[:, :, wide:] = jnp.zeros((spare + 1, sub, FB), dense.dtype)
    dense[spare, :, :wide] = jnp.zeros((sub, wide), dense.dtype)
    for copy in copies:
        copy.wait()

    def lanes(col):
        return jnp.concatenate([col] * (pts // FB), axis=1)

    def one(j, live):
        b = table[j]
        row = [table[at_row + j * TMAX + s] for s in range(live)]
        col = [pl.ds(pl.multiple_of(table[at_col + j * TMAX + s] * FB, FB), FB) for s in range(live)]
        pos = [table[at_pos + j * TMAX + s] for s in range(live)]
        x = xbuf[j, : live * FB, :]
        d = jnp.concatenate(
            [
                jnp.concatenate([dense[row[s], :, col[t]] for t in range(live)], axis=1)
                for s in range(live)
            ],
            axis=0,
        )
        gval = jnp.dot(d, x, preferred_element_type=jnp.float32)
        fval = []
        for s in range(live):
            dist = None
            for axis in range(3):
                diff = lanes(centre[axis, pos[s]]) - pbuf[axis, pl.ds(b, 1), :]
                dist = diff * diff if dist is None else dist + diff * diff
            dist = dist + lanes(centre[3, pos[s]])
            fval.append((gval[s * sub : (s + 1) * sub] * lax.rsqrt(dist)).astype(jnp.bfloat16))
        fval = jnp.concatenate(fval, axis=0)
        xw = (x.astype(jnp.float32) * wbuf[pl.ds(b, 1), :]).astype(jnp.bfloat16)
        part = lax.dot_general(
            fval, xw, (((1,), (1,)), ((), ())), preferred_element_type=jnp.float32
        )
        return row, col, part

    @pl.loop(0, batches // group)
    def _(h):
        @pl.loop(0, group)
        def _(u):
            fetch(h * group + u, lambda copy: copy.wait())

        for live in range(2, TMAX + 1):

            @pl.when(table[at_lives + h] == live)
            def _():
                for row, col, part in [one(h * group + u, live) for u in range(group)]:
                    for s in range(live):
                        for t in range(live):
                            acc[row[s], :, col[t]] += part[s * sub : (s + 1) * sub, t * FB : (t + 1) * FB]

    for k, out in enumerate(outs):
        size = out.shape[0]
        out[...] = acc[size * k : size * (k + 1), :, :wide].astype(out.dtype)


def batch_sums(table, xs, coords, weights, centre, parts, split):
    _, width, pts = xs[0].shape
    batches = 2 * xs[0].shape[0]
    group = math.gcd(batches, 4)
    nb, sub, wide = parts[0].shape
    pieces = len(parts)
    size = 1 if split else nb
    out_shapes = [
        jax.ShapeDtypeStruct((size, sub, wide), jnp.bfloat16 if k else jnp.float32)
        for k in range(pieces)
        for _ in range(nb // size)
    ]
    flops = 2 * batches * 2 * width * (width // 2) * pts
    return call(
        functools.partial(batch_kernel, group, pieces, split),
        [table],
        [*xs, *coords, *weights, centre, *parts],
        [pl.BlockSpec(memory_space=pltpu.HBM)] * 2
        + [pl.BlockSpec(memory_space=pl.ANY)] * 4
        + [whole(centre.shape)]
        + [pl.BlockSpec(memory_space=pl.ANY)] * pieces,
        out_shapes,
        [whole((size, sub, wide))] * len(out_shapes),
        [
            pltpu.VMEM((nb * pieces + 1, sub, wide + FB), jnp.bfloat16),
            pltpu.VMEM((nb * pieces + 1, sub, wide + FB), jnp.float32),
            pltpu.VMEM((batches, width, pts), jnp.bfloat16),
            pltpu.VMEM((3, batches, pts), jnp.float32),
            pltpu.VMEM((batches, pts), jnp.float32),
            pltpu.SemaphoreType.DMA((pieces,)),
            pltpu.SemaphoreType.DMA((batches,)),
            pltpu.SemaphoreType.DMA((4,)),
        ],
        cost=(flops, 2 * batches * width * pts),
    )


def per_device(density, owner, touched, blocks, counts, basis, points, weights, centers, widths):
    n = lax.axis_size("dom")
    cores = lax.axis_size("rows")
    i = lax.axis_index("dom")
    r = lax.axis_index("rows")
    nb = density.shape[0] // FB
    sub = FB // cores
    cols = density.shape[1]
    near = n // 2
    core = r.reshape(1)

    def swap(x, k):
        return lax.ppermute(x, "dom", [(a, a ^ k) for a in range(n)])

    def across(x):
        return lax.ppermute(x, "rows", [(a, cores - 1 - a) for a in range(cores)])

    def stay(x):
        return pltpu.with_memory_space_constraint(x, pltpu.HBM)

    own = lax.dynamic_index_in_dim(density.reshape(nb, cores, sub, cols), r, 1, keepdims=False)
    far = swap(own, near)
    sets = [touched] + [swap(touched, k) for k in range(1, near)]
    points = points.transpose(1, 0, 2)
    both = [(stay(x), across(x)) for x in (basis, points, weights, counts)] + [(blocks, across(blocks))]
    sets[0] = stay(touched)
    table = batch_tables(i.reshape(1), stay(owner), sets[0], both[4], both[3], nb, near)
    centre = centre_rows(sets[0], core, stay(centers), stay(widths.reshape(1, -1)), sub)

    picked = pick(sets, own)
    parts = [picked[0]] + [swap(picked[k], k) for k in range(1, near)]
    far, table, centre, own_part = lax.optimization_barrier((far, table, centre, picked[0]))
    picked = pick(sets, far)
    far_parts = [picked[0]] + [swap(picked[k], k) for k in range(1, near)]
    table, _ = lax.optimization_barrier((table, picked[0]))

    common = (*both[:3], centre)
    sums = batch_sums(table, *common, parts, False)
    table, _ = lax.optimization_barrier((table, sums[0]))
    far_sums = batch_sums(table, *common, far_parts, True)
    terms = [sums[0]] + [swap(sums[k], k) for k in range(1, near)]
    far_sums, terms = lax.optimization_barrier((far_sums, terms))
    chunks = [[far_sums[b]] + [swap(far_sums[nb * k + b], k) for k in range(1, near)] for b in range(nb)]
    far_terms = [swap(merge(sets, chunk, cols), near) for chunk in chunks]
    keep, give = finish(sets, core, terms, far_terms)
    got = across(give)
    pair = jnp.where(r == 0, jnp.stack([keep, got], axis=1), jnp.stack([got, keep], axis=1))
    return pair.reshape(nb * FB, cols // cores)


def solution(mesh):
    in_specs = (
        P(("groups", "dom"), None),
        P("groups"),
        P(("groups", "dom"), None),
        P(("groups", "dom", "rows"), None),
        P(("groups", "dom", "rows")),
        P(("groups", "dom", "rows"), None, None),
        P(("groups", "dom", "rows"), None, None),
        P(("groups", "dom", "rows"), None),
        P(None, "groups"),
        P("groups"),
    )
    out_specs = P(("groups", "dom"), "rows")

    def run(*args):
        n, cores = mesh.shape["dom"], mesh.shape["rows"]
        rows_here = args[0].shape[0] // (mesh.shape["groups"] * n)
        split = rows_here % FB == 0 and cores == 2 and n >= 4 and n & (n - 1) == 0
        body = per_device if split else per_device_any
        return jax.shard_map(body, mesh=mesh, in_specs=in_specs, out_specs=out_specs, check_vma=False)(*args)

    return run
```

```python
import functools
import math

import jax
import jax.numpy as jnp
from jax import lax
from jax.experimental import pallas as pl
from jax.experimental.pallas import tpu as pltpu
from jax.sharding import PartitionSpec as P

FB = 128
TMAX = 4
UMAX = 8
MIB = 1024 * 1024


def coulomb(centre_x, centre_y, centre_z, spread, point_x, point_y, point_z):
    dist = (centre_x - point_x) ** 2 + (centre_y - point_y) ** 2 + (centre_z - point_z) ** 2
    return 1.0 / jnp.sqrt(dist + spread * spread)


def lookup_owner(owner, block_ids):
    match = block_ids[:, None] == jnp.arange(owner.shape[0], dtype=jnp.int32)[None, :]
    return jnp.sum(jnp.where(match, owner[None, :], 0), axis=1)


def answer_for(density, column_sets):
    rows_here = density.shape[0]
    sources, wanted = column_sets.shape
    blocked = density.reshape(rows_here, density.shape[1] // FB, FB)
    picked = jnp.take(blocked, column_sets.reshape(-1), axis=1)
    return picked.reshape(rows_here, sources, wanted * FB).transpose(1, 0, 2)


def spread_rows(terms, stored, block_count, sources):
    columns = terms.shape[1]
    expanded = jnp.zeros((block_count, FB, columns), jnp.float32)
    expanded = expanded.at[stored].set(terms.reshape(UMAX, FB, columns))
    return expanded.reshape(sources, block_count * FB // sources, columns)


def collect(returned, column_sets, block_count):
    sources, rows_here, columns = returned.shape
    wanted = column_sets.shape[1]
    pieces = returned.reshape(sources, rows_here, wanted, FB).transpose(1, 0, 2, 3)
    pieces = pieces.reshape(rows_here, sources * wanted, FB)
    total = jnp.zeros((rows_here, block_count, FB), jnp.float32)
    total = total.at[:, column_sets.reshape(-1)].add(pieces)
    return total.reshape(rows_here, block_count * FB)


def per_device_any(density, owner, touched, blocks, counts, basis, points, weights, centers, widths):
    rows_count = lax.axis_size("rows")
    rows_index = lax.axis_index("rows")
    batches = blocks.shape[0]
    block_count = owner.shape[0]
    width = TMAX * FB
    share = UMAX // rows_count
    own_set = touched[0]
    all_sets = lax.all_gather(touched, "dom", axis=0, tiled=True)
    sources = all_sets.shape[0]
    half_sets = lax.dynamic_slice_in_dim(all_sets, rows_index * share, share, 1)
    got = lax.all_to_all(
        answer_for(density, all_sets), "dom", split_axis=0, concat_axis=0, tiled=True
    )
    panel = got.reshape(block_count * FB, UMAX * FB)
    stored = lookup_owner(owner, own_set)
    tile = jnp.take(panel.reshape(block_count, FB, UMAX * FB), stored, axis=0).reshape(
        UMAX, FB, UMAX, FB
    )
    centre_blocks = centers.reshape(3, block_count, FB)
    spread_blocks = widths.reshape(block_count, FB)
    slot_ids = jnp.arange(TMAX, dtype=jnp.int32)
    group = math.gcd(batches, 8)
    turns = batches // group

    def work(total, item):
        slots, count, values, coords, quad = item
        gid = jnp.take(own_set, slots.reshape(-1), axis=0)
        active = (slot_ids[None, :] < count[:, None]).astype(jnp.float32)
        rowmask = jnp.repeat(active, FB, axis=1)[:, :, None]
        xmask = jnp.where(rowmask > 0, values, jnp.zeros_like(values))
        xweighted = (xmask.astype(jnp.float32) * quad[:, None, :]).astype(jnp.bfloat16)
        dloc = tile[slots[:, :, None], :, slots[:, None, :], :]
        dloc = dloc.transpose(0, 1, 3, 2, 4).reshape(group, width, width)
        centre = jnp.take(centre_blocks, gid, axis=1).reshape(3, group, width)
        spread = jnp.take(spread_blocks, gid, axis=0).reshape(group, width)
        vfac = coulomb(
            centre[0][:, :, None],
            centre[1][:, :, None],
            centre[2][:, :, None],
            spread[:, :, None],
            coords[:, 0][:, None, :],
            coords[:, 1][:, None, :],
            coords[:, 2][:, None, :],
        )
        gval = jnp.einsum("brc,bcg->brg", dloc, xmask, preferred_element_type=jnp.float32)
        fval = (gval * vfac * rowmask).astype(jnp.bfloat16)
        parts = jnp.einsum("brg,bcg->brc", fval, xweighted, preferred_element_type=jnp.float32)
        pieces = parts.reshape(group, TMAX, FB, TMAX, FB).transpose(0, 1, 3, 2, 4)
        total = total.at[slots[:, :, None], :, slots[:, None, :], :].add(pieces)
        return (total, None)

    items = (
        blocks.reshape(turns, group, TMAX),
        counts.reshape(turns, group),
        basis.reshape(turns, group, width, basis.shape[2]),
        points.reshape(turns, group, 3, points.shape[2]),
        weights.reshape(turns, group, weights.shape[1]),
    )
    start = jnp.zeros((UMAX, FB, UMAX, FB), jnp.float32)
    local_sum, _ = lax.scan(work, start, items)
    local_flat = local_sum.reshape(UMAX * FB, UMAX * FB)
    halved = lax.psum_scatter(local_flat, "rows", scatter_dimension=1, tiled=True)
    returned = lax.all_to_all(
        spread_rows(halved, stored, block_count, sources),
        "dom",
        split_axis=0,
        concat_axis=0,
        tiled=True,
    )
    gathered_terms = collect(returned, half_sets, block_count)
    summed = lax.psum_scatter(gathered_terms, "rows", scatter_dimension=1, tiled=True)
    return summed.astype(jnp.bfloat16)


def call(kernel, scalars, arrays, in_specs, out_shapes, out_specs, scratch, grid=(1,), cost=None, vmem=44):
    return pl.pallas_call(
        kernel,
        grid_spec=pltpu.PrefetchScalarGridSpec(
            num_scalar_prefetch=len(scalars),
            grid=grid,
            in_specs=in_specs,
            out_specs=out_specs,
            scratch_shapes=scratch,
        ),
        out_shape=out_shapes,
        cost_estimate=pl.CostEstimate(flops=cost[0], bytes_accessed=cost[1], transcendentals=0),
        compiler_params=pltpu.CompilerParams(vmem_limit_bytes=vmem * MIB),
    )(*scalars, *arrays)


def whole(shape):
    return pl.BlockSpec(shape, lambda *_: (0,) * len(shape))


def pick_kernel(peers, *refs):
    sets, full, outs = refs[:peers], refs[peers], refs[peers + 1 :]
    for k in range(peers):
        for q in range(UMAX):
            cols = pl.ds(pl.multiple_of(sets[k][0, q] * FB, FB), FB)
            outs[k][:, :, q * FB : (q + 1) * FB] = full[:, :, cols]


def pick(sets, full):
    nb, sub, cols = full.shape
    shape = (nb, sub, UMAX * FB)
    peers = len(sets)
    return call(
        functools.partial(pick_kernel, peers),
        sets,
        [full],
        [whole(full.shape)],
        [jax.ShapeDtypeStruct(shape, full.dtype)] * peers,
        [whole(shape)] * peers,
        [],
        cost=(0, 2 * nb * sub * (cols + peers * UMAX * FB)),
    )


def centre_kernel(own_set, core, centers, widths, out, turned):
    sub = out.shape[2]
    for p in range(UMAX):
        cols = pl.ds(pl.multiple_of(own_set[0, p] * FB, FB), FB)
        width = widths[:, cols]
        rows = jnp.concatenate([centers[:, cols], width * width, jnp.zeros((4, FB), jnp.float32)], axis=0)
        turned[...] = rows.T
        start = pl.multiple_of(core[0] * sub, sub)
        for c in range(4):
            out[c, p] = jnp.broadcast_to(turned[pl.ds(start, sub), c : c + 1], (sub, FB))


def centre_rows(own_set, core, centers, widths, sub):
    shape = (4, UMAX, sub, FB)
    return call(
        centre_kernel,
        [own_set, core],
        [centers, widths],
        [whole(centers.shape), whole(widths.shape)],
        jax.ShapeDtypeStruct(shape, jnp.float32),
        whole(shape),
        [pltpu.VMEM((FB, 8), jnp.float32)],
        cost=(0, 2 * 4 * UMAX * sub * FB * 4),
    )


def table_kernel(nb, near, group, me, owner, own_set, blocks_a, blocks_b, counts_a, counts_b, out, kbs, fill):
    half = counts_a.shape[0]
    at_lives, at_near, at_far, at_col, at_pos = table_places(2 * half, group)
    spare = nb * near
    for p in range(UMAX):
        stored = owner[own_set[0, p]]
        kbs[p] = (lax.div(stored, nb) ^ me[0]) * nb + lax.rem(stored, nb)
    for c in range(TMAX + 1):
        fill[c] = 0

    def each(todo):
        for side, (blocks, counts) in enumerate(((blocks_a, counts_a), (blocks_b, counts_b))):

            @pl.loop(0, half)
            def _(b):
                todo(side, b, blocks, counts[b])

    def tally(side, b, blocks, count):
        fill[count] = fill[count] + 1

    each(tally)
    place = 0
    for c in range(TMAX, -1, -1):
        many = fill[c]
        fill[c] = place
        place = place + many

    def put(side, b, blocks, count):
        j = fill[count]
        fill[count] = j + 1
        out[j] = side * half + b

        @pl.when(lax.rem(j, group) == 0)
        def _():
            out[at_lives + lax.div(j, group)] = count

        for s in range(TMAX):
            pos = blocks[b, s]
            kb = kbs[pos]
            on = s < count
            at = j * TMAX + s
            out[at_pos + at] = pos
            out[at_col + at] = jnp.where(on, pos, UMAX)
            out[at_near + at] = jnp.where(on & (kb < spare), kb, spare)
            out[at_far + at] = jnp.where(on & (kb >= spare), kb - spare, spare)

    each(put)


def table_places(batches, group):
    lives = batches
    near = lives + batches // group
    return lives, near, near + batches * TMAX, near + 2 * batches * TMAX, near + 3 * batches * TMAX


def batch_tables(me, owner, own_set, blocks, counts, nb, near):
    batches = 2 * counts[0].shape[0]
    group = math.gcd(batches, 4)
    size = table_places(batches, group)[-1] + batches * TMAX
    return call(
        functools.partial(table_kernel, nb, near, group),
        [me, owner, own_set, *blocks, *counts],
        [],
        [],
        jax.ShapeDtypeStruct((size,), jnp.int32),
        pl.BlockSpec(memory_space=pltpu.SMEM),
        [pltpu.SMEM((UMAX,), jnp.int32), pltpu.SMEM((TMAX + 1,), jnp.int32)],
        cost=(0, 8 * batches * TMAX),
    )


def add_up(sets, terms, total):
    total[...] = jnp.zeros(total.shape, total.dtype)
    for k, term in enumerate(terms):
        for q in range(UMAX):
            cols = pl.ds(pl.multiple_of(sets[k][0, q] * FB, FB), FB)
            total[:, :, cols] += term[:, :, q * FB : (q + 1) * FB].astype(jnp.float32)


def merge_kernel(peers, *refs):
    sets, terms, out, total = refs[:peers], refs[peers : 2 * peers], refs[-2], refs[-1]
    add_up(sets, terms, total)
    out[...] = total[...].astype(out.dtype)


def merge(sets, terms, cols):
    nb, sub, wide = terms[0].shape
    shape = (nb, sub, cols)
    return call(
        functools.partial(merge_kernel, len(terms)),
        sets,
        terms,
        [whole(t.shape) for t in terms],
        jax.ShapeDtypeStruct(shape, jnp.bfloat16),
        whole(shape),
        [pltpu.VMEM(shape, jnp.float32)],
        cost=(0, 2 * nb * sub * (cols + 5 * wide)),
    )


def finish_kernel(peers, *refs):
    sets, core = refs[:peers], refs[peers]
    terms, fars = refs[peers + 1 : 2 * peers + 1], refs[2 * peers + 1 : -3]
    keep, give, total = refs[-3:]
    add_up(sets, terms, total)
    half = keep.shape[2]
    for out, side in ((keep, core[0]), (give, 1 - core[0])):
        cols = pl.ds(pl.multiple_of(side * half, FB), half)
        for b, far in enumerate(fars):
            out[b] = (total[b, :, cols] + far[0, :, cols].astype(jnp.float32)).astype(out.dtype)


def finish(sets, core, terms, fars):
    nb, sub, wide = terms[0].shape
    cols = fars[0].shape[2]
    shape = (nb, sub, cols // 2)
    return call(
        functools.partial(finish_kernel, len(terms)),
        [*sets, core],
        [*terms, *fars],
        [whole(t.shape) for t in (*terms, *fars)],
        [jax.ShapeDtypeStruct(shape, jnp.bfloat16)] * 2,
        [whole(shape)] * 2,
        [pltpu.VMEM((nb, sub, cols), jnp.float32)],
        cost=(0, 2 * nb * sub * (2 * cols + 5 * wide)),
    )


def batch_kernel(group, pieces, split, table, *refs):
    xs, coords, weights, centre = refs[0:2], refs[2:4], refs[4:6], refs[6]
    parts = refs[7 : 7 + pieces]
    outs = refs[7 + pieces : -8]
    dense, acc, xbuf, pbuf, wbuf, sems, xsems, qsems = refs[-8:]
    nb, sub, wide = parts[0].shape
    spare = nb * pieces
    batches, _, pts = xbuf.shape
    half = batches // 2
    at_lives, at_near, at_far, at_col, at_pos = table_places(batches, group)
    at_row = at_far if split else at_near

    def fetch(j, act):
        b = table[j]
        for side in (0, 1):

            @pl.when((b >= half) if side else (b < half))
            def _():
                act(pltpu.make_async_copy(xs[side].at[b - half * side], xbuf.at[j], xsems.at[j]))

    copies = [
        pltpu.make_async_copy(part, dense.at[pl.ds(nb * k, nb), :, pl.ds(0, wide)], sems.at[k])
        for k, part in enumerate(parts)
    ]
    for side in (0, 1):
        rest = pl.ds(half * side, half)
        copies.append(pltpu.make_async_copy(coords[side], pbuf.at[:, rest], qsems.at[side]))
        copies.append(pltpu.make_async_copy(weights[side], wbuf.at[rest], qsems.at[2 + side]))
    for copy in copies:
        copy.start()

    @pl.loop(0, batches)
    def _(j):
        fetch(j, lambda copy: copy.start())

    acc[...] = jnp.zeros(acc.shape, acc.dtype)
    dense[:, :, wide:] = jnp.zeros((spare + 1, sub, FB), dense.dtype)
    dense[spare, :, :wide] = jnp.zeros((sub, wide), dense.dtype)
    for copy in copies:
        copy.wait()

    def lanes(col):
        return jnp.concatenate([col] * (pts // FB), axis=1)

    def one(j, live):
        b = table[j]
        row = [table[at_row + j * TMAX + s] for s in range(live)]
        col = [pl.ds(pl.multiple_of(table[at_col + j * TMAX + s] * FB, FB), FB) for s in range(live)]
        pos = [table[at_pos + j * TMAX + s] for s in range(live)]
        x = xbuf[j, : live * FB, :]
        d = jnp.concatenate(
            [
                jnp.concatenate([dense[row[s], :, col[t]] for t in range(live)], axis=1)
                for s in range(live)
            ],
            axis=0,
        )
        gval = jnp.dot(d, x, preferred_element_type=jnp.float32)
        fval = []
        for s in range(live):
            dist = None
            for axis in range(3):
                diff = lanes(centre[axis, pos[s]]) - pbuf[axis, pl.ds(b, 1), :]
                dist = diff * diff if dist is None else dist + diff * diff
            dist = dist + lanes(centre[3, pos[s]])
            fval.append((gval[s * sub : (s + 1) * sub] * lax.rsqrt(dist)).astype(jnp.bfloat16))
        fval = jnp.concatenate(fval, axis=0)
        xw = (x.astype(jnp.float32) * wbuf[pl.ds(b, 1), :]).astype(jnp.bfloat16)
        part = lax.dot_general(
            fval, xw, (((1,), (1,)), ((), ())), preferred_element_type=jnp.float32
        )
        return row, col, part

    @pl.loop(0, batches // group)
    def _(h):
        @pl.loop(0, group)
        def _(u):
            fetch(h * group + u, lambda copy: copy.wait())

        for live in range(2, TMAX + 1):

            @pl.when(table[at_lives + h] == live)
            def _():
                for row, col, part in [one(h * group + u, live) for u in range(group)]:
                    for s in range(live):
                        for t in range(live):
                            acc[row[s], :, col[t]] += part[s * sub : (s + 1) * sub, t * FB : (t + 1) * FB]

    for k, out in enumerate(outs):
        size = out.shape[0]
        out[...] = acc[size * k : size * (k + 1), :, :wide].astype(out.dtype)


def batch_sums(table, xs, coords, weights, centre, parts, split):
    _, width, pts = xs[0].shape
    batches = 2 * xs[0].shape[0]
    group = math.gcd(batches, 4)
    nb, sub, wide = parts[0].shape
    pieces = len(parts)
    size = 1 if split else nb
    out_shapes = [
        jax.ShapeDtypeStruct((size, sub, wide), jnp.bfloat16 if k else jnp.float32)
        for k in range(pieces)
        for _ in range(nb // size)
    ]
    flops = 2 * batches * 2 * width * (width // 2) * pts
    return call(
        functools.partial(batch_kernel, group, pieces, split),
        [table],
        [*xs, *coords, *weights, centre, *parts],
        [pl.BlockSpec(memory_space=pltpu.HBM)] * 2
        + [pl.BlockSpec(memory_space=pl.ANY)] * 4
        + [whole(centre.shape)]
        + [pl.BlockSpec(memory_space=pl.ANY)] * pieces,
        out_shapes,
        [whole((size, sub, wide))] * len(out_shapes),
        [
            pltpu.VMEM((nb * pieces + 1, sub, wide + FB), jnp.bfloat16),
            pltpu.VMEM((nb * pieces + 1, sub, wide + FB), jnp.float32),
            pltpu.VMEM((batches, width, pts), jnp.bfloat16),
            pltpu.VMEM((3, batches, pts), jnp.float32),
            pltpu.VMEM((batches, pts), jnp.float32),
            pltpu.SemaphoreType.DMA((pieces,)),
            pltpu.SemaphoreType.DMA((batches,)),
            pltpu.SemaphoreType.DMA((4,)),
        ],
        cost=(flops, 2 * batches * width * pts),
    )


def per_device(density, owner, touched, blocks, counts, basis, points, weights, centers, widths):
    n = lax.axis_size("dom")
    cores = lax.axis_size("rows")
    i = lax.axis_index("dom")
    r = lax.axis_index("rows")
    nb = density.shape[0] // FB
    sub = FB // cores
    cols = density.shape[1]
    near = n // 2
    core = r.reshape(1)

    def swap(x, k):
        return lax.ppermute(x, "dom", [(a, a ^ k) for a in range(n)])

    def across(x):
        return lax.ppermute(x, "rows", [(a, cores - 1 - a) for a in range(cores)])

    def stay(x):
        return pltpu.with_memory_space_constraint(x, pltpu.HBM)

    own = lax.dynamic_index_in_dim(density.reshape(nb, cores, sub, cols), r, 1, keepdims=False)
    far = swap(own, near)
    sets = [touched] + [swap(touched, k) for k in range(1, near)]
    points = points.transpose(1, 0, 2)
    both = [(stay(x), across(x)) for x in (basis, points, weights, counts)] + [(blocks, across(blocks))]
    sets[0] = stay(touched)
    table = batch_tables(i.reshape(1), stay(owner), sets[0], both[4], both[3], nb, near)
    centre = centre_rows(sets[0], core, stay(centers), stay(widths.reshape(1, -1)), sub)

    own, table, centre, both = lax.optimization_barrier((own, table, centre, both))
    picked = pick(sets, own)
    parts = [picked[0]] + [swap(picked[k], k) for k in range(1, near)]
    far, _ = lax.optimization_barrier((far, picked[0]))
    picked = pick(sets, far)
    far_parts = [picked[0]] + [swap(picked[k], k) for k in range(1, near)]
    table, _ = lax.optimization_barrier((table, picked[0]))

    common = (*both[:3], centre)
    sums = batch_sums(table, *common, parts, False)
    table, _ = lax.optimization_barrier((table, sums[0]))
    far_sums = batch_sums(table, *common, far_parts, True)
    terms = [sums[0]] + [swap(sums[k], k) for k in range(1, near)]
    far_sums, terms = lax.optimization_barrier((far_sums, terms))
    far_terms = []
    for b in range(nb):
        chunk = [far_sums[b]] + [swap(far_sums[nb * k + b], k) for k in range(1, near)]
        merged = merge(sets, chunk, cols)
        far_sums, merged = lax.optimization_barrier((far_sums, merged))
        far_terms.append(swap(merged, near))
    keep, give = finish(sets, core, terms, far_terms)
    got = across(give)
    pair = jnp.where(r == 0, jnp.stack([keep, got], axis=1), jnp.stack([got, keep], axis=1))
    return pair.reshape(nb * FB, cols // cores)


def solution(mesh):
    in_specs = (
        P(("groups", "dom"), None),
        P("groups"),
        P(("groups", "dom"), None),
        P(("groups", "dom", "rows"), None),
        P(("groups", "dom", "rows")),
        P(("groups", "dom", "rows"), None, None),
        P(("groups", "dom", "rows"), None, None),
        P(("groups", "dom", "rows"), None),
        P(None, "groups"),
        P("groups"),
    )
    out_specs = P(("groups", "dom"), "rows")

    def run(*args):
        n, cores = mesh.shape["dom"], mesh.shape["rows"]
        rows_here = args[0].shape[0] // (mesh.shape["groups"] * n)
        split = rows_here % FB == 0 and cores == 2 and n >= 4 and n & (n - 1) == 0
        body = per_device if split else per_device_any
        return jax.shard_map(body, mesh=mesh, in_specs=in_specs, out_specs=out_specs, check_vma=False)(*args)

    return run
```

```python
import functools
import math

import jax
import jax.numpy as jnp
from jax import lax
from jax.experimental import pallas as pl
from jax.experimental.pallas import tpu as pltpu
from jax.sharding import PartitionSpec as P

FB = 128
TMAX = 4
UMAX = 8
MIB = 1024 * 1024


def coulomb(centre_x, centre_y, centre_z, spread, point_x, point_y, point_z):
    dist = (centre_x - point_x) ** 2 + (centre_y - point_y) ** 2 + (centre_z - point_z) ** 2
    return 1.0 / jnp.sqrt(dist + spread * spread)


def lookup_owner(owner, block_ids):
    match = block_ids[:, None] == jnp.arange(owner.shape[0], dtype=jnp.int32)[None, :]
    return jnp.sum(jnp.where(match, owner[None, :], 0), axis=1)


def answer_for(density, column_sets):
    rows_here = density.shape[0]
    sources, wanted = column_sets.shape
    blocked = density.reshape(rows_here, density.shape[1] // FB, FB)
    picked = jnp.take(blocked, column_sets.reshape(-1), axis=1)
    return picked.reshape(rows_here, sources, wanted * FB).transpose(1, 0, 2)


def spread_rows(terms, stored, block_count, sources):
    columns = terms.shape[1]
    expanded = jnp.zeros((block_count, FB, columns), jnp.float32)
    expanded = expanded.at[stored].set(terms.reshape(UMAX, FB, columns))
    return expanded.reshape(sources, block_count * FB // sources, columns)


def collect(returned, column_sets, block_count):
    sources, rows_here, columns = returned.shape
    wanted = column_sets.shape[1]
    pieces = returned.reshape(sources, rows_here, wanted, FB).transpose(1, 0, 2, 3)
    pieces = pieces.reshape(rows_here, sources * wanted, FB)
    total = jnp.zeros((rows_here, block_count, FB), jnp.float32)
    total = total.at[:, column_sets.reshape(-1)].add(pieces)
    return total.reshape(rows_here, block_count * FB)


def per_device_any(density, owner, touched, blocks, counts, basis, points, weights, centers, widths):
    rows_count = lax.axis_size("rows")
    rows_index = lax.axis_index("rows")
    batches = blocks.shape[0]
    block_count = owner.shape[0]
    width = TMAX * FB
    share = UMAX // rows_count
    own_set = touched[0]
    all_sets = lax.all_gather(touched, "dom", axis=0, tiled=True)
    sources = all_sets.shape[0]
    half_sets = lax.dynamic_slice_in_dim(all_sets, rows_index * share, share, 1)
    got = lax.all_to_all(
        answer_for(density, all_sets), "dom", split_axis=0, concat_axis=0, tiled=True
    )
    panel = got.reshape(block_count * FB, UMAX * FB)
    stored = lookup_owner(owner, own_set)
    tile = jnp.take(panel.reshape(block_count, FB, UMAX * FB), stored, axis=0).reshape(
        UMAX, FB, UMAX, FB
    )
    centre_blocks = centers.reshape(3, block_count, FB)
    spread_blocks = widths.reshape(block_count, FB)
    slot_ids = jnp.arange(TMAX, dtype=jnp.int32)
    group = math.gcd(batches, 8)
    turns = batches // group

    def work(total, item):
        slots, count, values, coords, quad = item
        gid = jnp.take(own_set, slots.reshape(-1), axis=0)
        active = (slot_ids[None, :] < count[:, None]).astype(jnp.float32)
        rowmask = jnp.repeat(active, FB, axis=1)[:, :, None]
        xmask = jnp.where(rowmask > 0, values, jnp.zeros_like(values))
        xweighted = (xmask.astype(jnp.float32) * quad[:, None, :]).astype(jnp.bfloat16)
        dloc = tile[slots[:, :, None], :, slots[:, None, :], :]
        dloc = dloc.transpose(0, 1, 3, 2, 4).reshape(group, width, width)
        centre = jnp.take(centre_blocks, gid, axis=1).reshape(3, group, width)
        spread = jnp.take(spread_blocks, gid, axis=0).reshape(group, width)
        vfac = coulomb(
            centre[0][:, :, None],
            centre[1][:, :, None],
            centre[2][:, :, None],
            spread[:, :, None],
            coords[:, 0][:, None, :],
            coords[:, 1][:, None, :],
            coords[:, 2][:, None, :],
        )
        gval = jnp.einsum("brc,bcg->brg", dloc, xmask, preferred_element_type=jnp.float32)
        fval = (gval * vfac * rowmask).astype(jnp.bfloat16)
        parts = jnp.einsum("brg,bcg->brc", fval, xweighted, preferred_element_type=jnp.float32)
        pieces = parts.reshape(group, TMAX, FB, TMAX, FB).transpose(0, 1, 3, 2, 4)
        total = total.at[slots[:, :, None], :, slots[:, None, :], :].add(pieces)
        return (total, None)

    items = (
        blocks.reshape(turns, group, TMAX),
        counts.reshape(turns, group),
        basis.reshape(turns, group, width, basis.shape[2]),
        points.reshape(turns, group, 3, points.shape[2]),
        weights.reshape(turns, group, weights.shape[1]),
    )
    start = jnp.zeros((UMAX, FB, UMAX, FB), jnp.float32)
    local_sum, _ = lax.scan(work, start, items)
    local_flat = local_sum.reshape(UMAX * FB, UMAX * FB)
    halved = lax.psum_scatter(local_flat, "rows", scatter_dimension=1, tiled=True)
    returned = lax.all_to_all(
        spread_rows(halved, stored, block_count, sources),
        "dom",
        split_axis=0,
        concat_axis=0,
        tiled=True,
    )
    gathered_terms = collect(returned, half_sets, block_count)
    summed = lax.psum_scatter(gathered_terms, "rows", scatter_dimension=1, tiled=True)
    return summed.astype(jnp.bfloat16)


def call(kernel, scalars, arrays, in_specs, out_shapes, out_specs, scratch, grid=(1,), cost=None, vmem=44):
    return pl.pallas_call(
        kernel,
        grid_spec=pltpu.PrefetchScalarGridSpec(
            num_scalar_prefetch=len(scalars),
            grid=grid,
            in_specs=in_specs,
            out_specs=out_specs,
            scratch_shapes=scratch,
        ),
        out_shape=out_shapes,
        cost_estimate=pl.CostEstimate(flops=cost[0], bytes_accessed=cost[1], transcendentals=0),
        compiler_params=pltpu.CompilerParams(vmem_limit_bytes=vmem * MIB),
    )(*scalars, *arrays)


def whole(shape):
    return pl.BlockSpec(shape, lambda *_: (0,) * len(shape))


def pick_kernel(peers, *refs):
    sets, full, outs = refs[:peers], refs[peers], refs[peers + 1 :]
    for k in range(peers):
        for q in range(UMAX):
            cols = pl.ds(pl.multiple_of(sets[k][0, q] * FB, FB), FB)
            outs[k][:, :, q * FB : (q + 1) * FB] = full[:, :, cols]


def pick(sets, full):
    nb, sub, cols = full.shape
    shape = (nb, sub, UMAX * FB)
    peers = len(sets)
    return call(
        functools.partial(pick_kernel, peers),
        sets,
        [full],
        [whole(full.shape)],
        [jax.ShapeDtypeStruct(shape, full.dtype)] * peers,
        [whole(shape)] * peers,
        [],
        cost=(0, 2 * nb * sub * (cols + peers * UMAX * FB)),
    )


def centre_kernel(own_set, core, centers, widths, out, turned):
    sub = out.shape[2]
    for p in range(UMAX):
        cols = pl.ds(pl.multiple_of(own_set[0, p] * FB, FB), FB)
        width = widths[:, cols]
        rows = jnp.concatenate([centers[:, cols], width * width, jnp.zeros((4, FB), jnp.float32)], axis=0)
        turned[...] = rows.T
        start = pl.multiple_of(core[0] * sub, sub)
        for c in range(4):
            out[c, p] = jnp.broadcast_to(turned[pl.ds(start, sub), c : c + 1], (sub, FB))


def centre_rows(own_set, core, centers, widths, sub):
    shape = (4, UMAX, sub, FB)
    return call(
        centre_kernel,
        [own_set, core],
        [centers, widths],
        [whole(centers.shape), whole(widths.shape)],
        jax.ShapeDtypeStruct(shape, jnp.float32),
        whole(shape),
        [pltpu.VMEM((FB, 8), jnp.float32)],
        cost=(0, 2 * 4 * UMAX * sub * FB * 4),
    )


def table_kernel(nb, near, group, me, owner, own_set, blocks_a, blocks_b, counts_a, counts_b, out, kbs, fill):
    half = counts_a.shape[0]
    at_lives, at_near, at_far, at_col, at_pos = table_places(2 * half, group)
    spare = nb * near
    for p in range(UMAX):
        stored = owner[own_set[0, p]]
        kbs[p] = (lax.div(stored, nb) ^ me[0]) * nb + lax.rem(stored, nb)
    for c in range(TMAX + 1):
        fill[c] = 0

    def each(todo):
        for side, (blocks, counts) in enumerate(((blocks_a, counts_a), (blocks_b, counts_b))):

            @pl.loop(0, half)
            def _(b):
                todo(side, b, blocks, counts[b])

    def tally(side, b, blocks, count):
        fill[count] = fill[count] + 1

    each(tally)
    place = 0
    for c in range(TMAX, -1, -1):
        many = fill[c]
        fill[c] = place
        place = place + many

    def put(side, b, blocks, count):
        j = fill[count]
        fill[count] = j + 1
        out[j] = side * half + b

        @pl.when(lax.rem(j, group) == 0)
        def _():
            out[at_lives + lax.div(j, group)] = count

        for s in range(TMAX):
            pos = blocks[b, s]
            kb = kbs[pos]
            on = s < count
            at = j * TMAX + s
            out[at_pos + at] = pos
            out[at_col + at] = jnp.where(on, pos, UMAX)
            out[at_near + at] = jnp.where(on & (kb < spare), kb, spare)
            out[at_far + at] = jnp.where(on & (kb >= spare), kb - spare, spare)

    each(put)


def table_places(batches, group):
    lives = batches
    near = lives + batches // group
    return lives, near, near + batches * TMAX, near + 2 * batches * TMAX, near + 3 * batches * TMAX


def batch_tables(me, owner, own_set, blocks, counts, nb, near):
    batches = 2 * counts[0].shape[0]
    group = math.gcd(batches, 4)
    size = table_places(batches, group)[-1] + batches * TMAX
    return call(
        functools.partial(table_kernel, nb, near, group),
        [me, owner, own_set, *blocks, *counts],
        [],
        [],
        jax.ShapeDtypeStruct((size,), jnp.int32),
        pl.BlockSpec(memory_space=pltpu.SMEM),
        [pltpu.SMEM((UMAX,), jnp.int32), pltpu.SMEM((TMAX + 1,), jnp.int32)],
        cost=(0, 8 * batches * TMAX),
    )


def add_up(sets, terms, total):
    total[...] = jnp.zeros(total.shape, total.dtype)
    for k, term in enumerate(terms):
        for q in range(UMAX):
            cols = pl.ds(pl.multiple_of(sets[k][0, q] * FB, FB), FB)
            total[:, :, cols] += term[:, :, q * FB : (q + 1) * FB].astype(jnp.float32)


def merge_kernel(peers, *refs):
    sets, core = refs[:peers], refs[peers]
    terms = refs[peers + 1 : 2 * peers + 1]
    keep, give, total = refs[-3:]
    add_up(sets, terms, total)
    half = keep.shape[2]
    for out, side in ((keep, core[0]), (give, 1 - core[0])):
        out[...] = total[:, :, pl.ds(pl.multiple_of(side * half, FB), half)].astype(out.dtype)


def merge(sets, core, terms, cols, dtype):
    nb, sub, wide = terms[0].shape
    shape = (nb, sub, cols // 2)
    return call(
        functools.partial(merge_kernel, len(terms)),
        [*sets, core],
        terms,
        [whole(t.shape) for t in terms],
        [jax.ShapeDtypeStruct(shape, dtype)] * 2,
        [whole(shape)] * 2,
        [pltpu.VMEM((nb, sub, cols), jnp.float32)],
        cost=(0, 2 * nb * sub * (cols + 5 * wide)),
    )


def finish_kernel(nb, core, *refs):
    out = refs[-1]
    for other in (0, 1):
        near, fars = refs[other], refs[2 + other * nb : 2 + (other + 1) * nb]
        side = (1 - core[0]) if other else core[0]
        for b in range(nb):
            out[b, side] = (near[b] + fars[b][0].astype(jnp.float32)).astype(out.dtype)


def finish(core, nears, fars):
    nb, sub, wide = nears[0].shape
    shape = (nb, 2, sub, wide)
    arrays = [*nears, *(far[0] for far in fars), *(far[1] for far in fars)]
    return call(
        functools.partial(finish_kernel, nb),
        [core],
        arrays,
        [whole(t.shape) for t in arrays],
        jax.ShapeDtypeStruct(shape, jnp.bfloat16),
        whole(shape),
        [],
        cost=(0, 16 * nb * sub * wide),
    )


def batch_kernel(group, pieces, split, table, *refs):
    xs, coords, weights, centre = refs[0:2], refs[2:4], refs[4:6], refs[6]
    parts = refs[7 : 7 + pieces]
    outs = refs[7 + pieces : -8]
    dense, acc, xbuf, pbuf, wbuf, sems, xsems, qsems = refs[-8:]
    nb, sub, wide = parts[0].shape
    spare = nb * pieces
    batches, _, pts = xbuf.shape
    half = batches // 2
    at_lives, at_near, at_far, at_col, at_pos = table_places(batches, group)
    at_row = at_far if split else at_near

    def fetch(j, act):
        b = table[j]
        for side in (0, 1):

            @pl.when((b >= half) if side else (b < half))
            def _():
                act(pltpu.make_async_copy(xs[side].at[b - half * side], xbuf.at[j], xsems.at[j]))

    copies = [
        pltpu.make_async_copy(part, dense.at[pl.ds(nb * k, nb), :, pl.ds(0, wide)], sems.at[k])
        for k, part in enumerate(parts)
    ]
    for side in (0, 1):
        rest = pl.ds(half * side, half)
        copies.append(pltpu.make_async_copy(coords[side], pbuf.at[:, rest], qsems.at[side]))
        copies.append(pltpu.make_async_copy(weights[side], wbuf.at[rest], qsems.at[2 + side]))
    for copy in copies:
        copy.start()

    @pl.loop(0, batches)
    def _(j):
        fetch(j, lambda copy: copy.start())

    acc[...] = jnp.zeros(acc.shape, acc.dtype)
    dense[:, :, wide:] = jnp.zeros((spare + 1, sub, FB), dense.dtype)
    dense[spare, :, :wide] = jnp.zeros((sub, wide), dense.dtype)
    for copy in copies:
        copy.wait()

    def lanes(col):
        return jnp.concatenate([col] * (pts // FB), axis=1)

    def one(j, live):
        b = table[j]
        row = [table[at_row + j * TMAX + s] for s in range(live)]
        col = [pl.ds(pl.multiple_of(table[at_col + j * TMAX + s] * FB, FB), FB) for s in range(live)]
        pos = [table[at_pos + j * TMAX + s] for s in range(live)]
        x = xbuf[j, : live * FB, :]
        d = jnp.concatenate(
            [
                jnp.concatenate([dense[row[s], :, col[t]] for t in range(live)], axis=1)
                for s in range(live)
            ],
            axis=0,
        )
        gval = jnp.dot(d, x, preferred_element_type=jnp.float32)
        fval = []
        for s in range(live):
            dist = None
            for axis in range(3):
                diff = lanes(centre[axis, pos[s]]) - pbuf[axis, pl.ds(b, 1), :]
                dist = diff * diff if dist is None else dist + diff * diff
            dist = dist + lanes(centre[3, pos[s]])
            fval.append((gval[s * sub : (s + 1) * sub] * lax.rsqrt(dist)).astype(jnp.bfloat16))
        fval = jnp.concatenate(fval, axis=0)
        xw = (x.astype(jnp.float32) * wbuf[pl.ds(b, 1), :]).astype(jnp.bfloat16)
        part = lax.dot_general(
            fval, xw, (((1,), (1,)), ((), ())), preferred_element_type=jnp.float32
        )
        return row, col, part

    @pl.loop(0, batches // group)
    def _(h):
        @pl.loop(0, group)
        def _(u):
            fetch(h * group + u, lambda copy: copy.wait())

        for live in range(2, TMAX + 1):

            @pl.when(table[at_lives + h] == live)
            def _():
                for row, col, part in [one(h * group + u, live) for u in range(group)]:
                    for s in range(live):
                        for t in range(live):
                            acc[row[s], :, col[t]] += part[s * sub : (s + 1) * sub, t * FB : (t + 1) * FB]

    for k, out in enumerate(outs):
        size = out.shape[0]
        out[...] = acc[size * k : size * (k + 1), :, :wide].astype(out.dtype)


def batch_sums(table, xs, coords, weights, centre, parts, split):
    _, width, pts = xs[0].shape
    batches = 2 * xs[0].shape[0]
    group = math.gcd(batches, 4)
    nb, sub, wide = parts[0].shape
    pieces = len(parts)
    size = 1 if split else nb
    out_shapes = [
        jax.ShapeDtypeStruct((size, sub, wide), jnp.bfloat16 if k else jnp.float32)
        for k in range(pieces)
        for _ in range(nb // size)
    ]
    flops = 2 * batches * 2 * width * (width // 2) * pts
    return call(
        functools.partial(batch_kernel, group, pieces, split),
        [table],
        [*xs, *coords, *weights, centre, *parts],
        [pl.BlockSpec(memory_space=pltpu.HBM)] * 2
        + [pl.BlockSpec(memory_space=pl.ANY)] * 4
        + [whole(centre.shape)]
        + [pl.BlockSpec(memory_space=pl.ANY)] * pieces,
        out_shapes,
        [whole((size, sub, wide))] * len(out_shapes),
        [
            pltpu.VMEM((nb * pieces + 1, sub, wide + FB), jnp.bfloat16),
            pltpu.VMEM((nb * pieces + 1, sub, wide + FB), jnp.float32),
            pltpu.VMEM((batches, width, pts), jnp.bfloat16),
            pltpu.VMEM((3, batches, pts), jnp.float32),
            pltpu.VMEM((batches, pts), jnp.float32),
            pltpu.SemaphoreType.DMA((pieces,)),
            pltpu.SemaphoreType.DMA((batches,)),
            pltpu.SemaphoreType.DMA((4,)),
        ],
        cost=(flops, 2 * batches * width * pts),
    )


def per_device(density, owner, touched, blocks, counts, basis, points, weights, centers, widths):
    n = lax.axis_size("dom")
    cores = lax.axis_size("rows")
    i = lax.axis_index("dom")
    r = lax.axis_index("rows")
    nb = density.shape[0] // FB
    sub = FB // cores
    cols = density.shape[1]
    near = n // 2
    core = r.reshape(1)

    def swap(x, k):
        return lax.ppermute(x, "dom", [(a, a ^ k) for a in range(n)])

    def across(x):
        return lax.ppermute(x, "rows", [(a, cores - 1 - a) for a in range(cores)])

    def swap_both(x):
        pairs = [(a, (a // cores ^ near) * cores + cores - 1 - a % cores) for a in range(n * cores)]
        return lax.ppermute(x, ("dom", "rows"), pairs)

    def stay(x):
        return pltpu.with_memory_space_constraint(x, pltpu.HBM)

    own = lax.dynamic_index_in_dim(density.reshape(nb, cores, sub, cols), r, 1, keepdims=False)
    sets = [touched] + [swap(touched, k) for k in range(1, near)]
    small = (points.transpose(1, 0, 2), weights, counts, blocks)
    small_b = [across(x) for x in small]
    own, sets, basis, small_b = lax.optimization_barrier((own, sets, basis, small_b))
    far = swap(own, near)
    sets[0] = stay(touched)
    picked = pick(sets, own)
    parts = [picked[0]] + [swap(picked[k], k) for k in range(1, near)]
    both = [(stay(basis), across(basis))] + [(stay(x), y) for x, y in zip(small[:3], small_b)]
    table = batch_tables(i.reshape(1), stay(owner), sets[0], (small[3], small_b[3]), both[3], nb, near)
    centre = centre_rows(sets[0], core, stay(centers), stay(widths.reshape(1, -1)), sub)

    far, table, centre = lax.optimization_barrier((far, table, centre))
    picked = pick(sets, far)
    far_parts = [picked[0]] + [swap(picked[k], k) for k in range(1, near)]
    table, _ = lax.optimization_barrier((table, picked[0]))

    common = (*both[:3], centre)
    sums = batch_sums(table, *common, parts, False)
    table, _ = lax.optimization_barrier((table, sums[0]))
    far_sums = batch_sums(table, *common, far_parts, True)
    terms = [sums[0]] + [swap(sums[k], k) for k in range(1, near)]
    far_sums, terms = lax.optimization_barrier((far_sums, terms))
    nears = merge(sets, core, terms, cols, jnp.float32)
    fars = []
    for b in range(nb):
        chunk = [far_sums[b]] + [swap(far_sums[nb * k + b], k) for k in range(1, near)]
        if b == 0:
            chunk, nears = lax.optimization_barrier((chunk, nears))
        else:
            chunk, fars[-1] = lax.optimization_barrier((chunk, fars[-1]))
        halves = merge(sets, core, chunk, cols, jnp.bfloat16)
        far_sums, halves, nears = lax.optimization_barrier((far_sums, halves, nears))
        fars.append((swap(halves[0], near), swap_both(halves[1])))
    nears = (nears[0], across(nears[1]))
    return finish(core, nears, fars).reshape(nb * FB, cols // cores)


def solution(mesh):
    in_specs = (
        P(("groups", "dom"), None),
        P("groups"),
        P(("groups", "dom"), None),
        P(("groups", "dom", "rows"), None),
        P(("groups", "dom", "rows")),
        P(("groups", "dom", "rows"), None, None),
        P(("groups", "dom", "rows"), None, None),
        P(("groups", "dom", "rows"), None),
        P(None, "groups"),
        P("groups"),
    )
    out_specs = P(("groups", "dom"), "rows")

    def run(*args):
        n, cores = mesh.shape["dom"], mesh.shape["rows"]
        rows_here = args[0].shape[0] // (mesh.shape["groups"] * n)
        split = rows_here % FB == 0 and cores == 2 and n >= 4 and n & (n - 1) == 0
        body = per_device if split else per_device_any
        return jax.shard_map(body, mesh=mesh, in_specs=in_specs, out_specs=out_specs, check_vma=False)(*args)

    return run
```

```python
import functools
import math

import jax
import jax.numpy as jnp
from jax import lax
from jax.experimental import pallas as pl
from jax.experimental.pallas import tpu as pltpu
from jax.sharding import PartitionSpec as P

FB = 128
TMAX = 4
UMAX = 8
GROUP = 6
MIB = 1024 * 1024


def coulomb(centre_x, centre_y, centre_z, spread, point_x, point_y, point_z):
    dist = (centre_x - point_x) ** 2 + (centre_y - point_y) ** 2 + (centre_z - point_z) ** 2
    return 1.0 / jnp.sqrt(dist + spread * spread)


def lookup_owner(owner, block_ids):
    match = block_ids[:, None] == jnp.arange(owner.shape[0], dtype=jnp.int32)[None, :]
    return jnp.sum(jnp.where(match, owner[None, :], 0), axis=1)


def answer_for(density, column_sets):
    rows_here = density.shape[0]
    sources, wanted = column_sets.shape
    blocked = density.reshape(rows_here, density.shape[1] // FB, FB)
    picked = jnp.take(blocked, column_sets.reshape(-1), axis=1)
    return picked.reshape(rows_here, sources, wanted * FB).transpose(1, 0, 2)


def spread_rows(terms, stored, block_count, sources):
    columns = terms.shape[1]
    expanded = jnp.zeros((block_count, FB, columns), jnp.float32)
    expanded = expanded.at[stored].set(terms.reshape(UMAX, FB, columns))
    return expanded.reshape(sources, block_count * FB // sources, columns)


def collect(returned, column_sets, block_count):
    sources, rows_here, columns = returned.shape
    wanted = column_sets.shape[1]
    pieces = returned.reshape(sources, rows_here, wanted, FB).transpose(1, 0, 2, 3)
    pieces = pieces.reshape(rows_here, sources * wanted, FB)
    total = jnp.zeros((rows_here, block_count, FB), jnp.float32)
    total = total.at[:, column_sets.reshape(-1)].add(pieces)
    return total.reshape(rows_here, block_count * FB)


def per_device_any(density, owner, touched, blocks, counts, basis, points, weights, centers, widths):
    rows_count = lax.axis_size("rows")
    rows_index = lax.axis_index("rows")
    batches = blocks.shape[0]
    block_count = owner.shape[0]
    width = TMAX * FB
    share = UMAX // rows_count
    own_set = touched[0]
    all_sets = lax.all_gather(touched, "dom", axis=0, tiled=True)
    sources = all_sets.shape[0]
    half_sets = lax.dynamic_slice_in_dim(all_sets, rows_index * share, share, 1)
    got = lax.all_to_all(
        answer_for(density, all_sets), "dom", split_axis=0, concat_axis=0, tiled=True
    )
    panel = got.reshape(block_count * FB, UMAX * FB)
    stored = lookup_owner(owner, own_set)
    tile = jnp.take(panel.reshape(block_count, FB, UMAX * FB), stored, axis=0).reshape(
        UMAX, FB, UMAX, FB
    )
    centre_blocks = centers.reshape(3, block_count, FB)
    spread_blocks = widths.reshape(block_count, FB)
    slot_ids = jnp.arange(TMAX, dtype=jnp.int32)
    group = math.gcd(batches, 8)
    turns = batches // group

    def work(total, item):
        slots, count, values, coords, quad = item
        gid = jnp.take(own_set, slots.reshape(-1), axis=0)
        active = (slot_ids[None, :] < count[:, None]).astype(jnp.float32)
        rowmask = jnp.repeat(active, FB, axis=1)[:, :, None]
        xmask = jnp.where(rowmask > 0, values, jnp.zeros_like(values))
        xweighted = (xmask.astype(jnp.float32) * quad[:, None, :]).astype(jnp.bfloat16)
        dloc = tile[slots[:, :, None], :, slots[:, None, :], :]
        dloc = dloc.transpose(0, 1, 3, 2, 4).reshape(group, width, width)
        centre = jnp.take(centre_blocks, gid, axis=1).reshape(3, group, width)
        spread = jnp.take(spread_blocks, gid, axis=0).reshape(group, width)
        vfac = coulomb(
            centre[0][:, :, None],
            centre[1][:, :, None],
            centre[2][:, :, None],
            spread[:, :, None],
            coords[:, 0][:, None, :],
            coords[:, 1][:, None, :],
            coords[:, 2][:, None, :],
        )
        gval = jnp.einsum("brc,bcg->brg", dloc, xmask, preferred_element_type=jnp.float32)
        fval = (gval * vfac * rowmask).astype(jnp.bfloat16)
        parts = jnp.einsum("brg,bcg->brc", fval, xweighted, preferred_element_type=jnp.float32)
        pieces = parts.reshape(group, TMAX, FB, TMAX, FB).transpose(0, 1, 3, 2, 4)
        total = total.at[slots[:, :, None], :, slots[:, None, :], :].add(pieces)
        return (total, None)

    items = (
        blocks.reshape(turns, group, TMAX),
        counts.reshape(turns, group),
        basis.reshape(turns, group, width, basis.shape[2]),
        points.reshape(turns, group, 3, points.shape[2]),
        weights.reshape(turns, group, weights.shape[1]),
    )
    start = jnp.zeros((UMAX, FB, UMAX, FB), jnp.float32)
    local_sum, _ = lax.scan(work, start, items)
    local_flat = local_sum.reshape(UMAX * FB, UMAX * FB)
    halved = lax.psum_scatter(local_flat, "rows", scatter_dimension=1, tiled=True)
    returned = lax.all_to_all(
        spread_rows(halved, stored, block_count, sources),
        "dom",
        split_axis=0,
        concat_axis=0,
        tiled=True,
    )
    gathered_terms = collect(returned, half_sets, block_count)
    summed = lax.psum_scatter(gathered_terms, "rows", scatter_dimension=1, tiled=True)
    return summed.astype(jnp.bfloat16)


def call(kernel, scalars, arrays, in_specs, out_shapes, out_specs, scratch, grid=(1,), cost=None, vmem=36):
    return pl.pallas_call(
        kernel,
        grid_spec=pltpu.PrefetchScalarGridSpec(
            num_scalar_prefetch=len(scalars),
            grid=grid,
            in_specs=in_specs,
            out_specs=out_specs,
            scratch_shapes=scratch,
        ),
        out_shape=out_shapes,
        cost_estimate=pl.CostEstimate(flops=cost[0], bytes_accessed=cost[1], transcendentals=0),
        compiler_params=pltpu.CompilerParams(vmem_limit_bytes=vmem * MIB),
    )(*scalars, *arrays)


def whole(shape):
    return pl.BlockSpec(shape, lambda *_: (0,) * len(shape))


def pick_kernel(peers, *refs):
    sets, full, outs = refs[:peers], refs[peers], refs[peers + 1 :]
    for k in range(peers):
        for q in range(UMAX):
            cols = pl.ds(pl.multiple_of(sets[k][0, q] * FB, FB), FB)
            outs[k][:, :, q * FB : (q + 1) * FB] = full[:, :, cols]


def pick(sets, full):
    nb, sub, cols = full.shape
    shape = (nb, sub, UMAX * FB)
    peers = len(sets)
    return call(
        functools.partial(pick_kernel, peers),
        sets,
        [full],
        [whole(full.shape)],
        [jax.ShapeDtypeStruct(shape, full.dtype)] * peers,
        [whole(shape)] * peers,
        [],
        cost=(0, 2 * nb * sub * (cols + peers * UMAX * FB)),
    )


def centre_kernel(own_set, core, centers, widths, out, turned):
    sub = out.shape[2]
    for p in range(UMAX):
        cols = pl.ds(pl.multiple_of(own_set[0, p] * FB, FB), FB)
        width = widths[:, cols]
        rows = jnp.concatenate([centers[:, cols], width * width, jnp.zeros((4, FB), jnp.float32)], axis=0)
        turned[...] = rows.T
        start = pl.multiple_of(core[0] * sub, sub)
        for c in range(4):
            out[c, p] = jnp.broadcast_to(turned[pl.ds(start, sub), c : c + 1], (sub, FB))


def centre_rows(own_set, core, centers, widths, sub):
    shape = (4, UMAX, sub, FB)
    return call(
        centre_kernel,
        [own_set, core],
        [centers, widths],
        [whole(centers.shape), whole(widths.shape)],
        jax.ShapeDtypeStruct(shape, jnp.float32),
        whole(shape),
        [pltpu.VMEM((FB, 8), jnp.float32)],
        cost=(0, 2 * 4 * UMAX * sub * FB * 4),
    )


def table_places(batches, group):
    lives = batches
    rows = lives + batches // group
    slots = batches * TMAX
    return lives, rows, rows + slots, rows + 2 * slots, rows + 3 * slots


def table_kernel(nb, group, me, owner, own_set, blocks, packed, counts, out, kbs, fill, bundle, sem):
    copy = pltpu.make_async_copy(packed.at[TMAX], bundle, sem)
    copy.start()
    half = counts.shape[0]
    at_lives, at_row, at_pos, at_col, _ = table_places(2 * half, group)
    spare = owner.shape[0]
    for p in range(UMAX):
        stored = owner[own_set[0, p]]
        kbs[p] = (lax.div(stored, nb) ^ me[0]) * nb + lax.rem(stored, nb)
    for c in range(TMAX + 1):
        fill[c] = 0
    copy.wait()

    def count_of(side, b):
        return bundle[b, TMAX].astype(jnp.int32) if side else counts[b]

    for side in (0, 1):

        @pl.loop(0, half)
        def _(b):
            count = count_of(side, b)
            fill[count] = fill[count] + 1

    place = 0
    for c in range(TMAX, -1, -1):
        many = fill[c]
        fill[c] = place
        place = place + many

    for side in (0, 1):

        @pl.loop(0, half)
        def _(b):
            count = count_of(side, b)
            j = fill[count]
            fill[count] = j + 1
            out[j] = side * half + b

            @pl.when(lax.rem(j, group) == 0)
            def _():
                out[at_lives + lax.div(j, group)] = count

            for s in range(TMAX):
                pos = bundle[b, s].astype(jnp.int32) if side else blocks[s, b]
                on = s < count
                at = j * TMAX + s
                out[at_pos + at] = pos
                out[at_col + at] = jnp.where(on, pos, UMAX)
                out[at_row + at] = jnp.where(on, kbs[pos], spare)


def batch_tables(me, owner, own_set, blocks, packed, counts, nb):
    batches = 2 * counts.shape[0]
    group = math.gcd(batches, GROUP)
    size = table_places(batches, group)[-1]
    return call(
        functools.partial(table_kernel, nb, group),
        [me, owner, own_set, blocks],
        [packed, counts],
        [pl.BlockSpec(memory_space=pl.ANY), pl.BlockSpec(memory_space=pltpu.SMEM)],
        jax.ShapeDtypeStruct((size,), jnp.int32),
        pl.BlockSpec(memory_space=pltpu.SMEM),
        [
            pltpu.SMEM((UMAX,), jnp.int32),
            pltpu.SMEM((TMAX + 1,), jnp.int32),
            pltpu.SMEM(packed.shape[1:], packed.dtype),
            pltpu.SemaphoreType.DMA,
        ],
        cost=(0, 8 * batches * TMAX),
    )


def pack_kernel(points, weights, blocks, counts, out):
    batches, pts = weights.shape
    out[0:3] = points[...]
    out[3] = weights[...]
    lane = lax.broadcasted_iota(jnp.int32, (1, pts), 1)

    @pl.loop(0, batches)
    def _(b):
        row = jnp.where(lane == TMAX, counts[b], 0)
        for s in range(TMAX):
            row = jnp.where(lane == s, blocks[s, b], row)
        out[4, pl.ds(b, 1), :] = row.astype(jnp.float32)


def pack(points, weights, blocks, counts):
    shape = (5, *weights.shape)
    return call(
        pack_kernel,
        [],
        [points, weights, blocks, counts],
        [whole(points.shape), whole(weights.shape)] + [pl.BlockSpec(memory_space=pltpu.SMEM)] * 2,
        jax.ShapeDtypeStruct(shape, jnp.float32),
        whole(shape),
        [],
        cost=(0, 10 * 4 * weights.size),
    )


def add_up(sets, terms, total):
    total[...] = jnp.zeros(total.shape, total.dtype)
    for k, term in enumerate(terms):
        for q in range(UMAX):
            cols = pl.ds(pl.multiple_of(sets[k][0, q] * FB, FB), FB)
            total[:, :, cols] += term[:, :, q * FB : (q + 1) * FB].astype(jnp.float32)


def merge_kernel(peers, *refs):
    sets, terms, out, total = refs[:peers], refs[peers : 2 * peers], refs[-2], refs[-1]
    add_up(sets, terms, total)
    out[...] = total[...].astype(out.dtype)


def merge(sets, terms, cols):
    nb, sub, wide = terms[0].shape
    shape = (nb, sub, cols)
    return call(
        functools.partial(merge_kernel, len(terms)),
        sets,
        terms,
        [whole(t.shape) for t in terms],
        jax.ShapeDtypeStruct(shape, jnp.bfloat16),
        whole(shape),
        [pltpu.VMEM(shape, jnp.float32)],
        cost=(0, 2 * nb * sub * (cols + 5 * wide)),
    )


def finish_kernel(peers, *refs):
    sets, core = refs[:peers], refs[peers]
    terms, fars = refs[peers + 1 : 2 * peers + 1], refs[2 * peers + 1 : -3]
    keep, give, total = refs[-3:]
    add_up(sets, terms, total)
    half = keep.shape[2]
    for out, side in ((keep, core[0]), (give, 1 - core[0])):
        cols = pl.ds(pl.multiple_of(side * half, FB), half)
        for b, far in enumerate(fars):
            out[b] = (total[b, :, cols] + far[0, :, cols].astype(jnp.float32)).astype(out.dtype)


def finish(sets, core, terms, fars):
    nb, sub, wide = terms[0].shape
    cols = fars[0].shape[2]
    shape = (nb, sub, cols // 2)
    return call(
        functools.partial(finish_kernel, len(terms)),
        [*sets, core],
        [*terms, *fars],
        [whole(t.shape) for t in (*terms, *fars)],
        [jax.ShapeDtypeStruct(shape, jnp.bfloat16)] * 2,
        [whole(shape)] * 2,
        [pltpu.VMEM((nb, sub, cols), jnp.float32)],
        cost=(0, 2 * nb * sub * (2 * cols + 5 * wide)),
    )


def batch_kernel(group, pieces, table, *refs):
    xs, quads, centre_in = refs[0:2], refs[2:4], refs[4]
    parts = refs[5 : 5 + pieces]
    outs = refs[5 + pieces : -7]
    dense, acc, xbuf, qbuf, centre, sems, xsems = refs[-7:]
    nb, sub, wide = parts[0].shape
    spare = nb * pieces
    batches, _, pts = xbuf.shape
    half = batches // 2
    at_lives, at_row, at_pos, at_col, _ = table_places(batches, group)

    def fetch(j, act):
        b = table[j]
        for side in (0, 1):

            @pl.when((b >= half) if side else (b < half))
            def _():
                act(pltpu.make_async_copy(xs[side].at[b - half * side], xbuf.at[j], xsems.at[j]))

    copies = [
        pltpu.make_async_copy(part, dense.at[pl.ds(nb * k, nb), :, pl.ds(0, wide)], sems.at[k])
        for k, part in enumerate(parts)
    ]
    copies.append(pltpu.make_async_copy(centre_in, centre, sems.at[pieces]))
    for side in (0, 1):
        quad = qbuf.at[:, pl.ds(half * side, half)]
        copies.append(pltpu.make_async_copy(quads[side].at[pl.ds(0, 4)], quad, sems.at[pieces + 1 + side]))
    for copy in copies:
        copy.start()

    @pl.loop(0, batches)
    def _(j):
        fetch(j, lambda copy: copy.start())

    acc[...] = jnp.zeros(acc.shape, acc.dtype)
    dense[:, :, wide:] = jnp.zeros((spare + 1, sub, FB), dense.dtype)
    dense[spare, :, :wide] = jnp.zeros((sub, wide), dense.dtype)
    for copy in copies:
        copy.wait()

    def lanes(col):
        return jnp.concatenate([col] * (pts // FB), axis=1)

    def one(j, live):
        b = table[j]
        row = [table[at_row + j * TMAX + s] for s in range(live)]
        pos = [table[at_pos + j * TMAX + s] for s in range(live)]
        col = [pl.ds(pl.multiple_of(table[at_col + j * TMAX + s] * FB, FB), FB) for s in range(live)]
        x = xbuf[j, : live * FB, :]
        d = jnp.concatenate(
            [jnp.concatenate([dense[r, :, c] for c in col], axis=1) for r in row], axis=0
        )
        gval = jnp.dot(d, x, preferred_element_type=jnp.float32)
        fval = []
        for s in range(live):
            dist = None
            for axis in range(3):
                diff = lanes(centre[axis, pos[s]]) - qbuf[axis, pl.ds(b, 1), :]
                dist = diff * diff if dist is None else dist + diff * diff
            dist = dist + lanes(centre[3, pos[s]])
            fval.append((gval[s * sub : (s + 1) * sub] * lax.rsqrt(dist)).astype(jnp.bfloat16))
        fval = jnp.concatenate(fval, axis=0)
        xw = (x.astype(jnp.float32) * qbuf[3, pl.ds(b, 1), :]).astype(jnp.bfloat16)
        part = lax.dot_general(
            fval, xw, (((1,), (1,)), ((), ())), preferred_element_type=jnp.float32
        )
        return row, col, part

    @pl.loop(0, batches // group)
    def _(h):
        @pl.loop(0, group)
        def _(u):
            fetch(h * group + u, lambda copy: copy.wait())

        for live in range(2, TMAX + 1):

            @pl.when(table[at_lives + h] == live)
            def _():
                for row, col, part in [one(h * group + u, live) for u in range(group)]:
                    for s in range(live):
                        for t in range(live):
                            acc[row[s], :, col[t]] += part[s * sub : (s + 1) * sub, t * FB : (t + 1) * FB]

    start = 0
    for out in outs:
        rows = out.shape[0]
        out[...] = acc[start : start + rows, :, :wide].astype(out.dtype)
        start += rows


def batch_sums(table, xs, quads, centre, parts):
    _, width, pts = xs[0].shape
    batches = 2 * xs[0].shape[0]
    group = math.gcd(batches, GROUP)
    nb, sub, wide = parts[0].shape
    pieces = len(parts)
    near = pieces // 2
    out_shapes = [
        jax.ShapeDtypeStruct((nb if k < near else 1, sub, wide), jnp.bfloat16 if k % near else jnp.float32)
        for k in range(pieces)
        for _ in range(1 if k < near else nb)
    ]
    flops = 2 * batches * 2 * width * (width // 2) * pts
    return call(
        functools.partial(batch_kernel, group, pieces),
        [table],
        [*xs, *quads, centre, *parts],
        [pl.BlockSpec(memory_space=pl.ANY)] * (5 + pieces),
        out_shapes,
        [whole(out.shape) for out in out_shapes],
        [
            pltpu.VMEM((nb * pieces + 1, sub, wide + FB), jnp.bfloat16),
            pltpu.VMEM((nb * pieces + 1, sub, wide + FB), jnp.float32),
            pltpu.VMEM((batches, width, pts), jnp.bfloat16),
            pltpu.VMEM((4, batches, pts), jnp.float32),
            pltpu.VMEM(centre.shape, jnp.float32),
            pltpu.SemaphoreType.DMA((pieces + 3,)),
            pltpu.SemaphoreType.DMA((batches,)),
        ],
        cost=(flops, 2 * batches * width * pts),
    )


def per_device(density, owner, touched, blocks, counts, basis, points, weights, centers, widths):
    n = lax.axis_size("dom")
    cores = lax.axis_size("rows")
    i = lax.axis_index("dom")
    r = lax.axis_index("rows")
    nb = density.shape[0] // FB
    sub = FB // cores
    cols = density.shape[1]
    near = n // 2
    core = r.reshape(1)

    def swap(x, k):
        return lax.ppermute(x, "dom", [(a, a ^ k) for a in range(n)])

    def across(x):
        return lax.ppermute(x, "rows", [(a, cores - 1 - a) for a in range(cores)])

    def stay(x):
        return pltpu.with_memory_space_constraint(x, pltpu.HBM)

    own = lax.dynamic_index_in_dim(density.reshape(nb, cores, sub, cols), r, 1, keepdims=False)
    sets = [touched] + [swap(touched, k) for k in range(1, near)]
    own, sets = lax.optimization_barrier((own, sets))
    far = swap(own, near)
    sets[0] = stay(touched)
    picked = pick(sets, own)
    parts = [picked[0]] + [swap(picked[k], k) for k in range(1, near)]
    xs = (stay(basis), across(basis))
    far, parts = lax.optimization_barrier((far, parts))
    picked = pick(sets, far)
    small = (points.transpose(1, 0, 2), weights, blocks.T, counts)
    small, centers, widths, picked = lax.optimization_barrier((small, centers, widths, picked))
    parts += [picked[0]] + [swap(picked[k], k) for k in range(1, near)]

    small = [stay(x) for x in small]
    packed = pack(*small)
    packed_b = across(packed)
    table = batch_tables(i.reshape(1), stay(owner), sets[0], small[2], packed_b, small[3], nb)
    centre = centre_rows(sets[0], core, stay(centers), stay(widths.reshape(1, -1)), sub)
    parts, table, centre = lax.optimization_barrier((parts, table, centre))

    sums = batch_sums(table, xs, (packed, packed_b), centre, parts)
    sums, far_sums = sums[:near], sums[near:]
    far_terms = []
    for b in range(nb):
        chunk = [far_sums[b]] + [swap(far_sums[nb * k + b], k) for k in range(1, near)]
        merged = merge(sets, chunk, cols)
        sums, far_sums, merged = lax.optimization_barrier((sums, far_sums, merged))
        far_terms.append(swap(merged, near))
    sums, far_terms[0] = lax.optimization_barrier((sums, far_terms[0]))
    terms = [sums[0]] + [swap(sums[k], k) for k in range(1, near)]
    keep, give = finish(sets, core, terms, far_terms)
    got = across(give)
    pair = jnp.where(r == 0, jnp.stack([keep, got], axis=1), jnp.stack([got, keep], axis=1))
    return pair.reshape(nb * FB, cols // cores)


def solution(mesh):
    in_specs = (
        P(("groups", "dom"), None),
        P("groups"),
        P(("groups", "dom"), None),
        P(("groups", "dom", "rows"), None),
        P(("groups", "dom", "rows")),
        P(("groups", "dom", "rows"), None, None),
        P(("groups", "dom", "rows"), None, None),
        P(("groups", "dom", "rows"), None),
        P(None, "groups"),
        P("groups"),
    )
    out_specs = P(("groups", "dom"), "rows")

    def run(*args):
        n, cores = mesh.shape["dom"], mesh.shape["rows"]
        rows_here = args[0].shape[0] // (mesh.shape["groups"] * n)
        split = rows_here % FB == 0 and cores == 2 and n >= 4 and n & (n - 1) == 0
        body = per_device if split else per_device_any
        return jax.shard_map(body, mesh=mesh, in_specs=in_specs, out_specs=out_specs, check_vma=False)(*args)

    return run
```

```python
import functools
import math

import jax
import jax.numpy as jnp
from jax import lax
from jax.experimental import pallas as pl
from jax.experimental.pallas import tpu as pltpu
from jax.sharding import PartitionSpec as P

FB = 128
TMAX = 4
UMAX = 8
GROUP = 6
MIB = 1024 * 1024


def coulomb(centre_x, centre_y, centre_z, spread, point_x, point_y, point_z):
    dist = (centre_x - point_x) ** 2 + (centre_y - point_y) ** 2 + (centre_z - point_z) ** 2
    return 1.0 / jnp.sqrt(dist + spread * spread)


def lookup_owner(owner, block_ids):
    match = block_ids[:, None] == jnp.arange(owner.shape[0], dtype=jnp.int32)[None, :]
    return jnp.sum(jnp.where(match, owner[None, :], 0), axis=1)


def answer_for(density, column_sets):
    rows_here = density.shape[0]
    sources, wanted = column_sets.shape
    blocked = density.reshape(rows_here, density.shape[1] // FB, FB)
    picked = jnp.take(blocked, column_sets.reshape(-1), axis=1)
    return picked.reshape(rows_here, sources, wanted * FB).transpose(1, 0, 2)


def spread_rows(terms, stored, block_count, sources):
    columns = terms.shape[1]
    expanded = jnp.zeros((block_count, FB, columns), jnp.float32)
    expanded = expanded.at[stored].set(terms.reshape(UMAX, FB, columns))
    return expanded.reshape(sources, block_count * FB // sources, columns)


def collect(returned, column_sets, block_count):
    sources, rows_here, columns = returned.shape
    wanted = column_sets.shape[1]
    pieces = returned.reshape(sources, rows_here, wanted, FB).transpose(1, 0, 2, 3)
    pieces = pieces.reshape(rows_here, sources * wanted, FB)
    total = jnp.zeros((rows_here, block_count, FB), jnp.float32)
    total = total.at[:, column_sets.reshape(-1)].add(pieces)
    return total.reshape(rows_here, block_count * FB)


def per_device_any(density, owner, touched, blocks, counts, basis, points, weights, centers, widths):
    rows_count = lax.axis_size("rows")
    rows_index = lax.axis_index("rows")
    batches = blocks.shape[0]
    block_count = owner.shape[0]
    width = TMAX * FB
    share = UMAX // rows_count
    own_set = touched[0]
    all_sets = lax.all_gather(touched, "dom", axis=0, tiled=True)
    sources = all_sets.shape[0]
    half_sets = lax.dynamic_slice_in_dim(all_sets, rows_index * share, share, 1)
    got = lax.all_to_all(
        answer_for(density, all_sets), "dom", split_axis=0, concat_axis=0, tiled=True
    )
    panel = got.reshape(block_count * FB, UMAX * FB)
    stored = lookup_owner(owner, own_set)
    tile = jnp.take(panel.reshape(block_count, FB, UMAX * FB), stored, axis=0).reshape(
        UMAX, FB, UMAX, FB
    )
    centre_blocks = centers.reshape(3, block_count, FB)
    spread_blocks = widths.reshape(block_count, FB)
    slot_ids = jnp.arange(TMAX, dtype=jnp.int32)
    group = math.gcd(batches, 8)
    turns = batches // group

    def work(total, item):
        slots, count, values, coords, quad = item
        gid = jnp.take(own_set, slots.reshape(-1), axis=0)
        active = (slot_ids[None, :] < count[:, None]).astype(jnp.float32)
        rowmask = jnp.repeat(active, FB, axis=1)[:, :, None]
        xmask = jnp.where(rowmask > 0, values, jnp.zeros_like(values))
        xweighted = (xmask.astype(jnp.float32) * quad[:, None, :]).astype(jnp.bfloat16)
        dloc = tile[slots[:, :, None], :, slots[:, None, :], :]
        dloc = dloc.transpose(0, 1, 3, 2, 4).reshape(group, width, width)
        centre = jnp.take(centre_blocks, gid, axis=1).reshape(3, group, width)
        spread = jnp.take(spread_blocks, gid, axis=0).reshape(group, width)
        vfac = coulomb(
            centre[0][:, :, None],
            centre[1][:, :, None],
            centre[2][:, :, None],
            spread[:, :, None],
            coords[:, 0][:, None, :],
            coords[:, 1][:, None, :],
            coords[:, 2][:, None, :],
        )
        gval = jnp.einsum("brc,bcg->brg", dloc, xmask, preferred_element_type=jnp.float32)
        fval = (gval * vfac * rowmask).astype(jnp.bfloat16)
        parts = jnp.einsum("brg,bcg->brc", fval, xweighted, preferred_element_type=jnp.float32)
        pieces = parts.reshape(group, TMAX, FB, TMAX, FB).transpose(0, 1, 3, 2, 4)
        total = total.at[slots[:, :, None], :, slots[:, None, :], :].add(pieces)
        return (total, None)

    items = (
        blocks.reshape(turns, group, TMAX),
        counts.reshape(turns, group),
        basis.reshape(turns, group, width, basis.shape[2]),
        points.reshape(turns, group, 3, points.shape[2]),
        weights.reshape(turns, group, weights.shape[1]),
    )
    start = jnp.zeros((UMAX, FB, UMAX, FB), jnp.float32)
    local_sum, _ = lax.scan(work, start, items)
    local_flat = local_sum.reshape(UMAX * FB, UMAX * FB)
    halved = lax.psum_scatter(local_flat, "rows", scatter_dimension=1, tiled=True)
    returned = lax.all_to_all(
        spread_rows(halved, stored, block_count, sources),
        "dom",
        split_axis=0,
        concat_axis=0,
        tiled=True,
    )
    gathered_terms = collect(returned, half_sets, block_count)
    summed = lax.psum_scatter(gathered_terms, "rows", scatter_dimension=1, tiled=True)
    return summed.astype(jnp.bfloat16)


def call(kernel, scalars, arrays, in_specs, out_shapes, out_specs, scratch, grid=(1,), cost=None, vmem=36):
    return pl.pallas_call(
        kernel,
        grid_spec=pltpu.PrefetchScalarGridSpec(
            num_scalar_prefetch=len(scalars),
            grid=grid,
            in_specs=in_specs,
            out_specs=out_specs,
            scratch_shapes=scratch,
        ),
        out_shape=out_shapes,
        cost_estimate=pl.CostEstimate(flops=cost[0], bytes_accessed=cost[1], transcendentals=0),
        compiler_params=pltpu.CompilerParams(vmem_limit_bytes=vmem * MIB),
    )(*scalars, *arrays)


def whole(shape):
    return pl.BlockSpec(shape, lambda *_: (0,) * len(shape))


def pick_kernel(peers, *refs):
    sets, fulls, outs = refs[:peers], refs[peers:-peers], refs[-peers:]
    for k in range(peers):
        for q in range(UMAX):
            cols = pl.ds(pl.multiple_of(sets[k][0, q] * FB, FB), FB)
            picked = fulls[0][:, :, cols]
            for full in fulls[1:]:
                picked = picked + full[:, :, cols]
            outs[k][:, :, q * FB : (q + 1) * FB] = picked


def pick(sets, fulls):
    nb, sub, cols = fulls[0].shape
    shape = (nb, sub, UMAX * FB)
    peers = len(sets)
    return call(
        functools.partial(pick_kernel, peers),
        sets,
        fulls,
        [whole(full.shape) for full in fulls],
        [jax.ShapeDtypeStruct(shape, fulls[0].dtype)] * peers,
        [whole(shape)] * peers,
        [],
        cost=(0, 2 * nb * sub * (cols * len(fulls) + peers * UMAX * FB)),
    )


def centre_kernel(own_set, core, centers, widths, out, turned):
    sub = out.shape[2]
    for p in range(UMAX):
        cols = pl.ds(pl.multiple_of(own_set[0, p] * FB, FB), FB)
        width = widths[:, cols]
        rows = jnp.concatenate([centers[:, cols], width * width, jnp.zeros((4, FB), jnp.float32)], axis=0)
        turned[...] = rows.T
        start = pl.multiple_of(core[0] * sub, sub)
        for c in range(4):
            out[c, p] = jnp.broadcast_to(turned[pl.ds(start, sub), c : c + 1], (sub, FB))


def centre_rows(own_set, core, centers, widths, sub):
    shape = (4, UMAX, sub, FB)
    return call(
        centre_kernel,
        [own_set, core],
        [centers, widths],
        [whole(centers.shape), whole(widths.shape)],
        jax.ShapeDtypeStruct(shape, jnp.float32),
        whole(shape),
        [pltpu.VMEM((FB, 8), jnp.float32)],
        cost=(0, 2 * 4 * UMAX * sub * FB * 4),
    )


def table_places(batches, group):
    lives = batches
    rows = lives + batches // group
    slots = batches * TMAX
    return lives, rows, rows + slots, rows + 2 * slots, rows + 3 * slots


def table_kernel(nb, group, me, owner, own_set, blocks, packed, counts, out, kbs, fill, bundle, sem):
    copy = pltpu.make_async_copy(packed.at[TMAX], bundle, sem)
    copy.start()
    half = counts.shape[0]
    at_lives, at_row, at_pos, at_col, _ = table_places(2 * half, group)
    spare = owner.shape[0]
    for p in range(UMAX):
        stored = owner[own_set[0, p]]
        kbs[p] = (lax.div(stored, nb) ^ me[0]) * nb + lax.rem(stored, nb)
    for c in range(TMAX + 1):
        fill[c] = 0
    copy.wait()

    def count_of(side, b):
        return bundle[b, TMAX].astype(jnp.int32) if side else counts[b]

    for side in (0, 1):

        @pl.loop(0, half)
        def _(b):
            count = count_of(side, b)
            fill[count] = fill[count] + 1

    place = 0
    for c in range(TMAX, -1, -1):
        many = fill[c]
        fill[c] = place
        place = place + many

    for side in (0, 1):

        @pl.loop(0, half)
        def _(b):
            count = count_of(side, b)
            j = fill[count]
            fill[count] = j + 1
            out[j] = side * half + b

            @pl.when(lax.rem(j, group) == 0)
            def _():
                out[at_lives + lax.div(j, group)] = count

            for s in range(TMAX):
                pos = bundle[b, s].astype(jnp.int32) if side else blocks[s, b]
                on = s < count
                at = j * TMAX + s
                out[at_pos + at] = pos
                out[at_col + at] = jnp.where(on, pos, UMAX)
                out[at_row + at] = jnp.where(on, kbs[pos], spare)


def batch_tables(me, owner, own_set, blocks, packed, counts, nb):
    batches = 2 * counts.shape[0]
    group = math.gcd(batches, GROUP)
    size = table_places(batches, group)[-1]
    return call(
        functools.partial(table_kernel, nb, group),
        [me, owner, own_set, blocks],
        [packed, counts],
        [pl.BlockSpec(memory_space=pl.ANY), pl.BlockSpec(memory_space=pltpu.SMEM)],
        jax.ShapeDtypeStruct((size,), jnp.int32),
        pl.BlockSpec(memory_space=pltpu.SMEM),
        [
            pltpu.SMEM((UMAX,), jnp.int32),
            pltpu.SMEM((TMAX + 1,), jnp.int32),
            pltpu.SMEM(packed.shape[1:], packed.dtype),
            pltpu.SemaphoreType.DMA,
        ],
        cost=(0, 8 * batches * TMAX),
    )


def pack_kernel(points, weights, blocks, counts, out):
    batches, pts = weights.shape
    out[0:3] = points[...]
    out[3] = weights[...]
    lane = lax.broadcasted_iota(jnp.int32, (1, pts), 1)

    @pl.loop(0, batches)
    def _(b):
        row = jnp.where(lane == TMAX, counts[b], 0)
        for s in range(TMAX):
            row = jnp.where(lane == s, blocks[s, b], row)
        out[4, pl.ds(b, 1), :] = row.astype(jnp.float32)


def pack(points, weights, blocks, counts):
    shape = (5, *weights.shape)
    return call(
        pack_kernel,
        [],
        [points, weights, blocks, counts],
        [whole(points.shape), whole(weights.shape)] + [pl.BlockSpec(memory_space=pltpu.SMEM)] * 2,
        jax.ShapeDtypeStruct(shape, jnp.float32),
        whole(shape),
        [],
        cost=(0, 10 * 4 * weights.size),
    )


def add_up(sets, terms, total):
    total[...] = jnp.zeros(total.shape, total.dtype)
    for k, term in enumerate(terms):
        for q in range(UMAX):
            cols = pl.ds(pl.multiple_of(sets[k][0, q] * FB, FB), FB)
            total[:, :, cols] += term[:, :, q * FB : (q + 1) * FB].astype(jnp.float32)


def merge_kernel(peers, *refs):
    sets, terms, out, total = refs[:peers], refs[peers : 2 * peers], refs[-2], refs[-1]
    add_up(sets, terms, total)
    out[...] = total[...].astype(out.dtype)


def merge(sets, terms, cols):
    nb, sub, wide = terms[0].shape
    shape = (nb, sub, cols)
    return call(
        functools.partial(merge_kernel, len(terms)),
        sets,
        terms,
        [whole(t.shape) for t in terms],
        jax.ShapeDtypeStruct(shape, jnp.bfloat16),
        whole(shape),
        [pltpu.VMEM(shape, jnp.float32)],
        cost=(0, 2 * nb * sub * (cols + 5 * wide)),
    )


def finish_kernel(peers, *refs):
    sets, core = refs[:peers], refs[peers]
    terms, fars = refs[peers + 1 : 2 * peers + 1], refs[2 * peers + 1 : -3]
    keep, give, total = refs[-3:]
    add_up(sets, terms, total)
    half = keep.shape[2]
    for out, side in ((keep, core[0]), (give, 1 - core[0])):
        cols = pl.ds(pl.multiple_of(side * half, FB), half)
        here = total[:, :, cols]
        for far in fars:
            here = here + far[:, :, cols].astype(jnp.float32)
        out[...] = here.astype(out.dtype)


def finish(sets, core, terms, fars):
    nb, sub, wide = terms[0].shape
    cols = fars[0].shape[2]
    shape = (nb, sub, cols // 2)
    return call(
        functools.partial(finish_kernel, len(terms)),
        [*sets, core],
        [*terms, *fars],
        [whole(t.shape) for t in (*terms, *fars)],
        [jax.ShapeDtypeStruct(shape, jnp.bfloat16)] * 2,
        [whole(shape)] * 2,
        [pltpu.VMEM((nb, sub, cols), jnp.float32)],
        cost=(0, 2 * nb * sub * (2 * cols + 5 * wide)),
    )


def batch_kernel(group, pieces, table, *refs):
    xs, quads, centre_in = refs[0:2], refs[2:4], refs[4]
    parts = refs[5 : 5 + pieces]
    outs = refs[5 + pieces : -7]
    dense, acc, xbuf, qbuf, centre, sems, xsems = refs[-7:]
    nb, sub, wide = parts[0].shape
    spare = nb * pieces
    batches, _, pts = xbuf.shape
    half = batches // 2
    at_lives, at_row, at_pos, at_col, _ = table_places(batches, group)

    def fetch(j, act):
        b = table[j]
        for side in (0, 1):

            @pl.when((b >= half) if side else (b < half))
            def _():
                act(pltpu.make_async_copy(xs[side].at[b - half * side], xbuf.at[j], xsems.at[j]))

    copies = [
        pltpu.make_async_copy(part, dense.at[pl.ds(nb * k, nb), :, pl.ds(0, wide)], sems.at[k])
        for k, part in enumerate(parts)
    ]
    copies.append(pltpu.make_async_copy(centre_in, centre, sems.at[pieces]))
    for side in (0, 1):
        quad = qbuf.at[:, pl.ds(half * side, half)]
        copies.append(pltpu.make_async_copy(quads[side].at[pl.ds(0, 4)], quad, sems.at[pieces + 1 + side]))
    for copy in copies:
        copy.start()

    @pl.loop(0, batches)
    def _(j):
        fetch(j, lambda copy: copy.start())

    acc[...] = jnp.zeros(acc.shape, acc.dtype)
    dense[:, :, wide:] = jnp.zeros((spare + 1, sub, FB), dense.dtype)
    dense[spare, :, :wide] = jnp.zeros((sub, wide), dense.dtype)
    for copy in copies:
        copy.wait()

    def lanes(col):
        return jnp.concatenate([col] * (pts // FB), axis=1)

    def one(j, live):
        b = table[j]
        row = [table[at_row + j * TMAX + s] for s in range(live)]
        pos = [table[at_pos + j * TMAX + s] for s in range(live)]
        col = [pl.ds(pl.multiple_of(table[at_col + j * TMAX + s] * FB, FB), FB) for s in range(live)]
        x = xbuf[j, : live * FB, :]
        d = jnp.concatenate(
            [jnp.concatenate([dense[r, :, c] for c in col], axis=1) for r in row], axis=0
        )
        gval = jnp.dot(d, x, preferred_element_type=jnp.float32)
        fval = []
        for s in range(live):
            dist = None
            for axis in range(3):
                diff = lanes(centre[axis, pos[s]]) - qbuf[axis, pl.ds(b, 1), :]
                dist = diff * diff if dist is None else dist + diff * diff
            dist = dist + lanes(centre[3, pos[s]])
            fval.append((gval[s * sub : (s + 1) * sub] * lax.rsqrt(dist)).astype(jnp.bfloat16))
        fval = jnp.concatenate(fval, axis=0)
        xw = (x.astype(jnp.float32) * qbuf[3, pl.ds(b, 1), :]).astype(jnp.bfloat16)
        part = lax.dot_general(
            fval, xw, (((1,), (1,)), ((), ())), preferred_element_type=jnp.float32
        )
        return row, col, part

    @pl.loop(0, batches // group)
    def _(h):
        @pl.loop(0, group)
        def _(u):
            fetch(h * group + u, lambda copy: copy.wait())

        for live in range(2, TMAX + 1):

            @pl.when(table[at_lives + h] == live)
            def _():
                for row, col, part in [one(h * group + u, live) for u in range(group)]:
                    for s in range(live):
                        for t in range(live):
                            acc[row[s], :, col[t]] += part[s * sub : (s + 1) * sub, t * FB : (t + 1) * FB]

    start = 0
    for out in outs:
        rows = out.shape[0]
        out[...] = acc[start : start + rows, :, :wide].astype(out.dtype)
        start += rows


def batch_sums(table, xs, quads, centre, parts):
    _, width, pts = xs[0].shape
    batches = 2 * xs[0].shape[0]
    group = math.gcd(batches, GROUP)
    nb, sub, wide = parts[0].shape
    pieces = len(parts)
    near = pieces // 2
    out_shapes = [
        jax.ShapeDtypeStruct((nb, sub, wide), jnp.bfloat16 if k % near else jnp.float32) for k in range(pieces)
    ]
    flops = 2 * batches * 2 * width * (width // 2) * pts
    return call(
        functools.partial(batch_kernel, group, pieces),
        [table],
        [*xs, *quads, centre, *parts],
        [pl.BlockSpec(memory_space=pl.ANY)] * (5 + pieces),
        out_shapes,
        [whole(out.shape) for out in out_shapes],
        [
            pltpu.VMEM((nb * pieces + 1, sub, wide + FB), jnp.bfloat16),
            pltpu.VMEM((nb * pieces + 1, sub, wide + FB), jnp.float32),
            pltpu.VMEM((batches, width, pts), jnp.bfloat16),
            pltpu.VMEM((4, batches, pts), jnp.float32),
            pltpu.VMEM(centre.shape, jnp.float32),
            pltpu.SemaphoreType.DMA((pieces + 3,)),
            pltpu.SemaphoreType.DMA((batches,)),
        ],
        cost=(flops, 2 * batches * width * pts),
    )


def per_device(density, owner, touched, blocks, counts, basis, points, weights, centers, widths):
    n = lax.axis_size("dom")
    cores = lax.axis_size("rows")
    i = lax.axis_index("dom")
    r = lax.axis_index("rows")
    nb = density.shape[0] // FB
    sub = FB // cores
    cols = density.shape[1]
    near = n // 2
    core = r.reshape(1)

    def swap(x, k):
        return lax.ppermute(x, "dom", [(a, a ^ k) for a in range(n)])

    def across(x):
        return lax.ppermute(x, "rows", [(a, cores - 1 - a) for a in range(cores)])

    def stay(x):
        return pltpu.with_memory_space_constraint(x, pltpu.HBM)

    own = lax.dynamic_index_in_dim(density.reshape(nb, cores, sub, cols), r, 1, keepdims=False)
    def mirror(x, meanwhile):
        goes = ([], [])
        for a in range(n):
            inner = (a & (near // 2) != 0) != (a & near != 0)
            goes[inner].append((a, a ^ near))
        first = lax.ppermute(x, "dom", goes[0])
        x, first, meanwhile = lax.optimization_barrier((x, first, meanwhile))
        return [first, lax.ppermute(x, "dom", goes[1])], meanwhile

    sets = [touched] + [swap(touched, k) for k in range(1, near)]
    own, sets = lax.optimization_barrier((own, sets))
    sets[0] = stay(touched)
    fars, picked = mirror(own, pick(sets, [own]))
    parts = [picked[0]] + [swap(picked[k], k) for k in range(1, near)]
    xs = (stay(basis), across(basis))
    fars, parts = lax.optimization_barrier((fars, parts))
    picked = pick(sets, fars)
    small = (points.transpose(1, 0, 2), weights, blocks.T, counts)
    small, centers, widths, picked = lax.optimization_barrier((small, centers, widths, picked))
    parts += [picked[0]] + [swap(picked[k], k) for k in range(1, near)]

    small = [stay(x) for x in small]
    packed = pack(*small)
    packed_b = across(packed)
    table = batch_tables(i.reshape(1), stay(owner), sets[0], small[2], packed_b, small[3], nb)
    centre = centre_rows(sets[0], core, stay(centers), stay(widths.reshape(1, -1)), sub)
    parts, table, centre = lax.optimization_barrier((parts, table, centre))

    sums = batch_sums(table, xs, (packed, packed_b), centre, parts)
    far_terms = [sums[near]] + [swap(sums[near + k], k) for k in range(1, near)]
    merged = merge(sets, far_terms, cols)
    sums, merged = lax.optimization_barrier((sums, merged))
    fars, sums = mirror(merged, sums)
    terms = [sums[0]] + [swap(sums[k], k) for k in range(1, near)]
    keep, give = finish(sets, core, terms, fars)
    got = across(give)
    pair = jnp.where(r == 0, jnp.stack([keep, got], axis=1), jnp.stack([got, keep], axis=1))
    return pair.reshape(nb * FB, cols // cores)


def solution(mesh):
    in_specs = (
        P(("groups", "dom"), None),
        P("groups"),
        P(("groups", "dom"), None),
        P(("groups", "dom", "rows"), None),
        P(("groups", "dom", "rows")),
        P(("groups", "dom", "rows"), None, None),
        P(("groups", "dom", "rows"), None, None),
        P(("groups", "dom", "rows"), None),
        P(None, "groups"),
        P("groups"),
    )
    out_specs = P(("groups", "dom"), "rows")

    def run(*args):
        n, cores = mesh.shape["dom"], mesh.shape["rows"]
        rows_here = args[0].shape[0] // (mesh.shape["groups"] * n)
        split = rows_here % FB == 0 and cores == 2 and n >= 4 and n & (n - 1) == 0
        body = per_device if split else per_device_any
        return jax.shard_map(body, mesh=mesh, in_specs=in_specs, out_specs=out_specs, check_vma=False)(*args)

    return run
```

```python
import functools
import math

import jax
import jax.numpy as jnp
from jax import lax
from jax.experimental import pallas as pl
from jax.experimental.pallas import tpu as pltpu
from jax.sharding import PartitionSpec as P

FB = 128
TMAX = 4
UMAX = 8
GROUP = 6
MIB = 1024 * 1024


def coulomb(centre_x, centre_y, centre_z, spread, point_x, point_y, point_z):
    dist = (centre_x - point_x) ** 2 + (centre_y - point_y) ** 2 + (centre_z - point_z) ** 2
    return 1.0 / jnp.sqrt(dist + spread * spread)


def lookup_owner(owner, block_ids):
    match = block_ids[:, None] == jnp.arange(owner.shape[0], dtype=jnp.int32)[None, :]
    return jnp.sum(jnp.where(match, owner[None, :], 0), axis=1)


def answer_for(density, column_sets):
    rows_here = density.shape[0]
    sources, wanted = column_sets.shape
    blocked = density.reshape(rows_here, density.shape[1] // FB, FB)
    picked = jnp.take(blocked, column_sets.reshape(-1), axis=1)
    return picked.reshape(rows_here, sources, wanted * FB).transpose(1, 0, 2)


def spread_rows(terms, stored, block_count, sources):
    columns = terms.shape[1]
    expanded = jnp.zeros((block_count, FB, columns), jnp.float32)
    expanded = expanded.at[stored].set(terms.reshape(UMAX, FB, columns))
    return expanded.reshape(sources, block_count * FB // sources, columns)


def collect(returned, column_sets, block_count):
    sources, rows_here, columns = returned.shape
    wanted = column_sets.shape[1]
    pieces = returned.reshape(sources, rows_here, wanted, FB).transpose(1, 0, 2, 3)
    pieces = pieces.reshape(rows_here, sources * wanted, FB)
    total = jnp.zeros((rows_here, block_count, FB), jnp.float32)
    total = total.at[:, column_sets.reshape(-1)].add(pieces)
    return total.reshape(rows_here, block_count * FB)


def per_device_any(density, owner, touched, blocks, counts, basis, points, weights, centers, widths):
    rows_count = lax.axis_size("rows")
    rows_index = lax.axis_index("rows")
    batches = blocks.shape[0]
    block_count = owner.shape[0]
    width = TMAX * FB
    share = UMAX // rows_count
    own_set = touched[0]
    all_sets = lax.all_gather(touched, "dom", axis=0, tiled=True)
    sources = all_sets.shape[0]
    half_sets = lax.dynamic_slice_in_dim(all_sets, rows_index * share, share, 1)
    got = lax.all_to_all(
        answer_for(density, all_sets), "dom", split_axis=0, concat_axis=0, tiled=True
    )
    panel = got.reshape(block_count * FB, UMAX * FB)
    stored = lookup_owner(owner, own_set)
    tile = jnp.take(panel.reshape(block_count, FB, UMAX * FB), stored, axis=0).reshape(
        UMAX, FB, UMAX, FB
    )
    centre_blocks = centers.reshape(3, block_count, FB)
    spread_blocks = widths.reshape(block_count, FB)
    slot_ids = jnp.arange(TMAX, dtype=jnp.int32)
    group = math.gcd(batches, 8)
    turns = batches // group

    def work(total, item):
        slots, count, values, coords, quad = item
        gid = jnp.take(own_set, slots.reshape(-1), axis=0)
        active = (slot_ids[None, :] < count[:, None]).astype(jnp.float32)
        rowmask = jnp.repeat(active, FB, axis=1)[:, :, None]
        xmask = jnp.where(rowmask > 0, values, jnp.zeros_like(values))
        xweighted = (xmask.astype(jnp.float32) * quad[:, None, :]).astype(jnp.bfloat16)
        dloc = tile[slots[:, :, None], :, slots[:, None, :], :]
        dloc = dloc.transpose(0, 1, 3, 2, 4).reshape(group, width, width)
        centre = jnp.take(centre_blocks, gid, axis=1).reshape(3, group, width)
        spread = jnp.take(spread_blocks, gid, axis=0).reshape(group, width)
        vfac = coulomb(
            centre[0][:, :, None],
            centre[1][:, :, None],
            centre[2][:, :, None],
            spread[:, :, None],
            coords[:, 0][:, None, :],
            coords[:, 1][:, None, :],
            coords[:, 2][:, None, :],
        )
        gval = jnp.einsum("brc,bcg->brg", dloc, xmask, preferred_element_type=jnp.float32)
        fval = (gval * vfac * rowmask).astype(jnp.bfloat16)
        parts = jnp.einsum("brg,bcg->brc", fval, xweighted, preferred_element_type=jnp.float32)
        pieces = parts.reshape(group, TMAX, FB, TMAX, FB).transpose(0, 1, 3, 2, 4)
        total = total.at[slots[:, :, None], :, slots[:, None, :], :].add(pieces)
        return (total, None)

    items = (
        blocks.reshape(turns, group, TMAX),
        counts.reshape(turns, group),
        basis.reshape(turns, group, width, basis.shape[2]),
        points.reshape(turns, group, 3, points.shape[2]),
        weights.reshape(turns, group, weights.shape[1]),
    )
    start = jnp.zeros((UMAX, FB, UMAX, FB), jnp.float32)
    local_sum, _ = lax.scan(work, start, items)
    local_flat = local_sum.reshape(UMAX * FB, UMAX * FB)
    halved = lax.psum_scatter(local_flat, "rows", scatter_dimension=1, tiled=True)
    returned = lax.all_to_all(
        spread_rows(halved, stored, block_count, sources),
        "dom",
        split_axis=0,
        concat_axis=0,
        tiled=True,
    )
    gathered_terms = collect(returned, half_sets, block_count)
    summed = lax.psum_scatter(gathered_terms, "rows", scatter_dimension=1, tiled=True)
    return summed.astype(jnp.bfloat16)


def call(kernel, scalars, arrays, in_specs, out_shapes, out_specs, scratch, grid=(1,), cost=None, vmem=36):
    return pl.pallas_call(
        kernel,
        grid_spec=pltpu.PrefetchScalarGridSpec(
            num_scalar_prefetch=len(scalars),
            grid=grid,
            in_specs=in_specs,
            out_specs=out_specs,
            scratch_shapes=scratch,
        ),
        out_shape=out_shapes,
        cost_estimate=pl.CostEstimate(flops=cost[0], bytes_accessed=cost[1], transcendentals=0),
        compiler_params=pltpu.CompilerParams(vmem_limit_bytes=vmem * MIB),
    )(*scalars, *arrays)


def whole(shape):
    return pl.BlockSpec(shape, lambda *_: (0,) * len(shape))


def pick_kernel(peers, *refs):
    sets, fulls, outs = refs[:peers], refs[peers:-peers], refs[-peers:]
    for k in range(peers):
        for q in range(UMAX):
            cols = pl.ds(pl.multiple_of(sets[k][0, q] * FB, FB), FB)
            row = 0
            for full in fulls:
                rows = full.shape[0]
                outs[k][row : row + rows, :, q * FB : (q + 1) * FB] = full[:, :, cols]
                row += rows


def pick(sets, fulls):
    rows = sum(full.shape[0] for full in fulls)
    _, sub, cols = fulls[0].shape
    shape = (rows, sub, UMAX * FB)
    peers = len(sets)
    return call(
        functools.partial(pick_kernel, peers),
        sets,
        fulls,
        [whole(full.shape) for full in fulls],
        [jax.ShapeDtypeStruct(shape, fulls[0].dtype)] * peers,
        [whole(shape)] * peers,
        [],
        cost=(0, 2 * rows * sub * (cols + peers * UMAX * FB)),
    )


def centre_kernel(own_set, core, centers, widths, out, turned):
    sub = out.shape[2]
    for p in range(UMAX):
        cols = pl.ds(pl.multiple_of(own_set[0, p] * FB, FB), FB)
        width = widths[:, cols]
        rows = jnp.concatenate([centers[:, cols], width * width, jnp.zeros((4, FB), jnp.float32)], axis=0)
        turned[...] = rows.T
        start = pl.multiple_of(core[0] * sub, sub)
        for c in range(4):
            out[c, p] = jnp.broadcast_to(turned[pl.ds(start, sub), c : c + 1], (sub, FB))


def centre_rows(own_set, core, centers, widths, sub):
    shape = (4, UMAX, sub, FB)
    return call(
        centre_kernel,
        [own_set, core],
        [centers, widths],
        [whole(centers.shape), whole(widths.shape)],
        jax.ShapeDtypeStruct(shape, jnp.float32),
        whole(shape),
        [pltpu.VMEM((FB, 8), jnp.float32)],
        cost=(0, 2 * 4 * UMAX * sub * FB * 4),
    )


def table_places(batches, group):
    lives = batches
    rows = lives + batches // group
    slots = batches * TMAX
    return lives, rows, rows + slots, rows + 2 * slots, rows + 3 * slots, rows + 4 * slots


def table_kernel(nb, near, group, me, owner, own_set, blocks, packed, counts, out, kbs, fill, bundle, sem):
    copy = pltpu.make_async_copy(packed.at[TMAX], bundle, sem)
    copy.start()
    half = counts.shape[0]
    at_lives, at_near, at_far, at_pos, at_col, _ = table_places(2 * half, group)
    spare = nb * near
    for p in range(UMAX):
        stored = owner[own_set[0, p]]
        kbs[p] = (lax.div(stored, nb) ^ me[0]) * nb + lax.rem(stored, nb)
    for c in range(TMAX + 1):
        fill[c] = 0
    copy.wait()

    def count_of(side, b):
        return bundle[b, TMAX].astype(jnp.int32) if side else counts[b]

    for side in (0, 1):

        @pl.loop(0, half)
        def _(b):
            count = count_of(side, b)
            fill[count] = fill[count] + 1

    place = 0
    for c in range(TMAX, -1, -1):
        many = fill[c]
        fill[c] = place
        place = place + many

    for side in (0, 1):

        @pl.loop(0, half)
        def _(b):
            count = count_of(side, b)
            j = fill[count]
            fill[count] = j + 1
            out[j] = side * half + b

            @pl.when(lax.rem(j, group) == 0)
            def _():
                out[at_lives + lax.div(j, group)] = count

            for s in range(TMAX):
                pos = bundle[b, s].astype(jnp.int32) if side else blocks[s, b]
                on = s < count
                at = j * TMAX + s
                out[at_pos + at] = pos
                out[at_col + at] = jnp.where(on, pos, UMAX)
                kb = kbs[pos]
                out[at_near + at] = jnp.where(on & (kb < spare), kb, spare)
                out[at_far + at] = jnp.where(on & (kb >= spare), kb - spare, spare)


def batch_tables(me, owner, own_set, blocks, packed, counts, nb, near):
    batches = 2 * counts.shape[0]
    group = math.gcd(batches, GROUP)
    size = table_places(batches, group)[-1]
    return call(
        functools.partial(table_kernel, nb, near, group),
        [me, owner, own_set, blocks],
        [packed, counts],
        [pl.BlockSpec(memory_space=pl.ANY), pl.BlockSpec(memory_space=pltpu.SMEM)],
        jax.ShapeDtypeStruct((size,), jnp.int32),
        pl.BlockSpec(memory_space=pltpu.SMEM),
        [
            pltpu.SMEM((UMAX,), jnp.int32),
            pltpu.SMEM((TMAX + 1,), jnp.int32),
            pltpu.SMEM(packed.shape[1:], packed.dtype),
            pltpu.SemaphoreType.DMA,
        ],
        cost=(0, 8 * batches * TMAX),
    )


def pack_kernel(points, weights, blocks, counts, out):
    batches, pts = weights.shape
    out[0:3] = points[...]
    out[3] = weights[...]
    lane = lax.broadcasted_iota(jnp.int32, (1, pts), 1)

    @pl.loop(0, batches)
    def _(b):
        row = jnp.where(lane == TMAX, counts[b], 0)
        for s in range(TMAX):
            row = jnp.where(lane == s, blocks[s, b], row)
        out[4, pl.ds(b, 1), :] = row.astype(jnp.float32)


def pack(points, weights, blocks, counts):
    shape = (5, *weights.shape)
    return call(
        pack_kernel,
        [],
        [points, weights, blocks, counts],
        [whole(points.shape), whole(weights.shape)] + [pl.BlockSpec(memory_space=pltpu.SMEM)] * 2,
        jax.ShapeDtypeStruct(shape, jnp.float32),
        whole(shape),
        [],
        cost=(0, 10 * 4 * weights.size),
    )


def add_up(sets, terms, total):
    total[...] = jnp.zeros(total.shape, total.dtype)
    for k, term in enumerate(terms):
        for q in range(UMAX):
            cols = pl.ds(pl.multiple_of(sets[k][0, q] * FB, FB), FB)
            total[:, :, cols] += term[:, :, q * FB : (q + 1) * FB].astype(jnp.float32)


def merge_kernel(peers, *refs):
    sets, terms, out, total = refs[:peers], refs[peers : 2 * peers], refs[-2], refs[-1]
    add_up(sets, terms, total)
    out[...] = total[...].astype(out.dtype)


def merge(sets, terms, cols):
    nb, sub, wide = terms[0].shape
    shape = (nb, sub, cols)
    return call(
        functools.partial(merge_kernel, len(terms)),
        sets,
        terms,
        [whole(t.shape) for t in terms],
        jax.ShapeDtypeStruct(shape, jnp.bfloat16),
        whole(shape),
        [pltpu.VMEM(shape, jnp.float32)],
        cost=(0, 2 * nb * sub * (cols + 5 * wide)),
    )


def finish_kernel(peers, *refs):
    sets, core = refs[:peers], refs[peers]
    terms, fars = refs[peers + 1 : 2 * peers + 1], refs[2 * peers + 1 : -3]
    keep, give, total = refs[-3:]
    add_up(sets, terms, total)
    half = keep.shape[2]
    for out, side in ((keep, core[0]), (give, 1 - core[0])):
        cols = pl.ds(pl.multiple_of(side * half, FB), half)
        for b, far in enumerate(fars):
            out[b] = (total[b, :, cols] + far[0, :, cols].astype(jnp.float32)).astype(out.dtype)


def finish(sets, core, terms, fars):
    nb, sub, wide = terms[0].shape
    cols = fars[0].shape[2]
    shape = (nb, sub, cols // 2)
    return call(
        functools.partial(finish_kernel, len(terms)),
        [*sets, core],
        [*terms, *fars],
        [whole(t.shape) for t in (*terms, *fars)],
        [jax.ShapeDtypeStruct(shape, jnp.bfloat16)] * 2,
        [whole(shape)] * 2,
        [pltpu.VMEM((nb, sub, cols), jnp.float32)],
        cost=(0, 2 * nb * sub * (2 * cols + 5 * wide)),
    )


def batch_kernel(group, nb, places, split, table, *refs):
    xs, quads, centre_in = refs[0:2], refs[2:4], refs[4]
    parts = refs[5 : 5 + len(places)]
    outs = refs[5 + len(places) : -7]
    dense, acc, xbuf, qbuf, centre, sems, xsems = refs[-7:]
    _, sub, wide = parts[0].shape
    pieces = sum(len(where) for where in places)
    spare = nb * pieces
    batches, _, pts = xbuf.shape
    half = batches // 2
    at_lives, at_near, at_far, at_pos, at_col, _ = table_places(batches, group)
    at_row = at_far if split else at_near

    def fetch(j, act):
        b = table[j]
        for side in (0, 1):

            @pl.when((b >= half) if side else (b < half))
            def _():
                act(pltpu.make_async_copy(xs[side].at[b - half * side], xbuf.at[j], xsems.at[j]))

    copies = []
    for part, where in zip(parts, places):
        for j, piece in enumerate(where):
            block = dense.at[pl.ds(nb * piece, nb), :, pl.ds(0, wide)]
            copies.append(pltpu.make_async_copy(part.at[pl.ds(nb * j, nb)], block, sems.at[piece]))
    copies.append(pltpu.make_async_copy(centre_in, centre, sems.at[pieces]))
    for side in (0, 1):
        quad = qbuf.at[:, pl.ds(half * side, half)]
        copies.append(pltpu.make_async_copy(quads[side].at[pl.ds(0, 4)], quad, sems.at[pieces + 1 + side]))
    for copy in copies:
        copy.start()

    @pl.loop(0, batches)
    def _(j):
        fetch(j, lambda copy: copy.start())

    acc[...] = jnp.zeros(acc.shape, acc.dtype)
    dense[:, :, wide:] = jnp.zeros((spare + 1, sub, FB), dense.dtype)
    dense[spare, :, :wide] = jnp.zeros((sub, wide), dense.dtype)
    for copy in copies:
        copy.wait()

    def lanes(col):
        return jnp.concatenate([col] * (pts // FB), axis=1)

    def one(j, live):
        b = table[j]
        row = [table[at_row + j * TMAX + s] for s in range(live)]
        pos = [table[at_pos + j * TMAX + s] for s in range(live)]
        col = [pl.ds(pl.multiple_of(table[at_col + j * TMAX + s] * FB, FB), FB) for s in range(live)]
        x = xbuf[j, : live * FB, :]
        d = jnp.concatenate(
            [jnp.concatenate([dense[r, :, c] for c in col], axis=1) for r in row], axis=0
        )
        gval = jnp.dot(d, x, preferred_element_type=jnp.float32)
        fval = []
        for s in range(live):
            dist = None
            for axis in range(3):
                diff = lanes(centre[axis, pos[s]]) - qbuf[axis, pl.ds(b, 1), :]
                dist = diff * diff if dist is None else dist + diff * diff
            dist = dist + lanes(centre[3, pos[s]])
            fval.append((gval[s * sub : (s + 1) * sub] * lax.rsqrt(dist)).astype(jnp.bfloat16))
        fval = jnp.concatenate(fval, axis=0)
        xw = (x.astype(jnp.float32) * qbuf[3, pl.ds(b, 1), :]).astype(jnp.bfloat16)
        part = lax.dot_general(
            fval, xw, (((1,), (1,)), ((), ())), preferred_element_type=jnp.float32
        )
        return row, col, part

    @pl.loop(0, batches // group)
    def _(h):
        @pl.loop(0, group)
        def _(u):
            fetch(h * group + u, lambda copy: copy.wait())

        for live in range(2, TMAX + 1):

            @pl.when(table[at_lives + h] == live)
            def _():
                for row, col, part in [one(h * group + u, live) for u in range(group)]:
                    for s in range(live):
                        for t in range(live):
                            acc[row[s], :, col[t]] += part[s * sub : (s + 1) * sub, t * FB : (t + 1) * FB]

    start = 0
    for out in outs:
        rows = out.shape[0]
        out[...] = acc[start : start + rows, :, :wide].astype(out.dtype)
        start += rows


def batch_sums(table, xs, quads, centre, parts, places, nb, split):
    _, width, pts = xs[0].shape
    batches = 2 * xs[0].shape[0]
    group = math.gcd(batches, GROUP)
    _, sub, wide = parts[0].shape
    pieces = sum(len(where) for where in places)
    size = 1 if split else nb
    out_shapes = [
        jax.ShapeDtypeStruct((size, sub, wide), jnp.bfloat16 if piece else jnp.float32)
        for piece in range(pieces)
        for _ in range(nb // size)
    ]
    flops = 2 * batches * 2 * width * (width // 2) * pts
    return call(
        functools.partial(batch_kernel, group, nb, places, split),
        [table],
        [*xs, *quads, centre, *parts],
        [pl.BlockSpec(memory_space=pl.ANY)] * (5 + len(parts)),
        out_shapes,
        [whole(out.shape) for out in out_shapes],
        [
            pltpu.VMEM((nb * pieces + 1, sub, wide + FB), jnp.bfloat16),
            pltpu.VMEM((nb * pieces + 1, sub, wide + FB), jnp.float32),
            pltpu.VMEM((batches, width, pts), jnp.bfloat16),
            pltpu.VMEM((4, batches, pts), jnp.float32),
            pltpu.VMEM(centre.shape, jnp.float32),
            pltpu.SemaphoreType.DMA((pieces + 3,)),
            pltpu.SemaphoreType.DMA((batches,)),
        ],
        cost=(flops, 2 * batches * width * pts),
    )


def per_device(density, owner, touched, blocks, counts, basis, points, weights, centers, widths):
    n = lax.axis_size("dom")
    cores = lax.axis_size("rows")
    i = lax.axis_index("dom")
    r = lax.axis_index("rows")
    nb = density.shape[0] // FB
    sub = FB // cores
    cols = density.shape[1]
    near = n // 2
    core = r.reshape(1)

    def swap(x, k):
        return lax.ppermute(x, "dom", [(a, a ^ k) for a in range(n)])

    def across(x):
        return lax.ppermute(x, "rows", [(a, cores - 1 - a) for a in range(cores)])

    def stay(x):
        return pltpu.with_memory_space_constraint(x, pltpu.HBM)

    own = lax.dynamic_index_in_dim(density.reshape(nb, cores, sub, cols), r, 1, keepdims=False)
    side = near // 2
    sets = [touched] + [swap(touched, k) for k in range(1, near)]
    packed = pack(stay(points.transpose(1, 0, 2)), stay(weights), stay(blocks.T), stay(counts))
    packed_b = across(packed)
    sets[0] = stay(touched)
    table = batch_tables(i.reshape(1), stay(owner), sets[0], stay(blocks.T), packed_b, stay(counts), nb, near)
    centre = centre_rows(sets[0], core, stay(centers), stay(widths.reshape(1, -1)), sub)
    beside = swap(own, side)
    fars = []
    for b in range(nb):
        if fars:
            own, beside, sets, table, centre, fars[-1] = lax.optimization_barrier(
                (own, beside, sets, table, centre, fars[-1])
            )
        fars.append(swap(own[b : b + 1], near))
    peers = range(1, side)
    picked = pick([sets[0]] + [sets[k] for k in peers], [own, beside])
    parts = [picked[0]] + [swap(picked[1 + j], k) for j, k in enumerate(peers)]
    places = [(0, side)] + [(k, k + side) for k in peers]
    basis, fars[0] = lax.optimization_barrier((basis, fars[0]))
    xs = (stay(basis), across(basis))
    picked = pick(sets, fars)
    table, picked = lax.optimization_barrier((table, picked))
    far_parts = [picked[0]] + [swap(picked[k], k) for k in range(1, near)]

    common = (xs, (packed, packed_b), centre)
    sums = batch_sums(table, *common, parts, places, nb, False)
    table, sums = lax.optimization_barrier((table, sums))
    far_sums = batch_sums(table, *common, far_parts, [(k,) for k in range(near)], nb, True)
    terms = [sums[0]] + [swap(sums[k], k) for k in range(1, near)]
    far_sums, terms = lax.optimization_barrier((far_sums, terms))
    far_terms = []
    for b in range(nb):
        chunk = [far_sums[b]] + [swap(far_sums[nb * k + b], k) for k in range(1, near)]
        merged = merge(sets, chunk, cols)
        far_sums, merged = lax.optimization_barrier((far_sums, merged))
        far_terms.append(swap(merged, near))
    keep, give = finish(sets, core, terms, far_terms)
    got = across(give)
    pair = jnp.where(r == 0, jnp.stack([keep, got], axis=1), jnp.stack([got, keep], axis=1))
    return pair.reshape(nb * FB, cols // cores)


def solution(mesh):
    in_specs = (
        P(("groups", "dom"), None),
        P("groups"),
        P(("groups", "dom"), None),
        P(("groups", "dom", "rows"), None),
        P(("groups", "dom", "rows")),
        P(("groups", "dom", "rows"), None, None),
        P(("groups", "dom", "rows"), None, None),
        P(("groups", "dom", "rows"), None),
        P(None, "groups"),
        P("groups"),
    )
    out_specs = P(("groups", "dom"), "rows")

    def run(*args):
        n, cores = mesh.shape["dom"], mesh.shape["rows"]
        rows_here = args[0].shape[0] // (mesh.shape["groups"] * n)
        split = rows_here % FB == 0 and cores == 2 and n >= 4 and n & (n - 1) == 0
        body = per_device if split else per_device_any
        return jax.shard_map(body, mesh=mesh, in_specs=in_specs, out_specs=out_specs, check_vma=False)(*args)

    return run
```

```python
import functools
import math

import jax
import jax.numpy as jnp
from jax import lax
from jax.experimental import pallas as pl
from jax.experimental.pallas import tpu as pltpu
from jax.sharding import PartitionSpec as P

FB = 128
TMAX = 4
UMAX = 8
GROUP = 6
MIB = 1024 * 1024


def coulomb(centre_x, centre_y, centre_z, spread, point_x, point_y, point_z):
    dist = (centre_x - point_x) ** 2 + (centre_y - point_y) ** 2 + (centre_z - point_z) ** 2
    return 1.0 / jnp.sqrt(dist + spread * spread)


def lookup_owner(owner, block_ids):
    match = block_ids[:, None] == jnp.arange(owner.shape[0], dtype=jnp.int32)[None, :]
    return jnp.sum(jnp.where(match, owner[None, :], 0), axis=1)


def answer_for(density, column_sets):
    rows_here = density.shape[0]
    sources, wanted = column_sets.shape
    blocked = density.reshape(rows_here, density.shape[1] // FB, FB)
    picked = jnp.take(blocked, column_sets.reshape(-1), axis=1)
    return picked.reshape(rows_here, sources, wanted * FB).transpose(1, 0, 2)


def spread_rows(terms, stored, block_count, sources):
    columns = terms.shape[1]
    expanded = jnp.zeros((block_count, FB, columns), jnp.float32)
    expanded = expanded.at[stored].set(terms.reshape(UMAX, FB, columns))
    return expanded.reshape(sources, block_count * FB // sources, columns)


def collect(returned, column_sets, block_count):
    sources, rows_here, columns = returned.shape
    wanted = column_sets.shape[1]
    pieces = returned.reshape(sources, rows_here, wanted, FB).transpose(1, 0, 2, 3)
    pieces = pieces.reshape(rows_here, sources * wanted, FB)
    total = jnp.zeros((rows_here, block_count, FB), jnp.float32)
    total = total.at[:, column_sets.reshape(-1)].add(pieces)
    return total.reshape(rows_here, block_count * FB)


def per_device_any(density, owner, touched, blocks, counts, basis, points, weights, centers, widths):
    rows_count = lax.axis_size("rows")
    rows_index = lax.axis_index("rows")
    batches = blocks.shape[0]
    block_count = owner.shape[0]
    width = TMAX * FB
    share = UMAX // rows_count
    own_set = touched[0]
    all_sets = lax.all_gather(touched, "dom", axis=0, tiled=True)
    sources = all_sets.shape[0]
    half_sets = lax.dynamic_slice_in_dim(all_sets, rows_index * share, share, 1)
    got = lax.all_to_all(
        answer_for(density, all_sets), "dom", split_axis=0, concat_axis=0, tiled=True
    )
    panel = got.reshape(block_count * FB, UMAX * FB)
    stored = lookup_owner(owner, own_set)
    tile = jnp.take(panel.reshape(block_count, FB, UMAX * FB), stored, axis=0).reshape(
        UMAX, FB, UMAX, FB
    )
    centre_blocks = centers.reshape(3, block_count, FB)
    spread_blocks = widths.reshape(block_count, FB)
    slot_ids = jnp.arange(TMAX, dtype=jnp.int32)
    group = math.gcd(batches, 8)
    turns = batches // group

    def work(total, item):
        slots, count, values, coords, quad = item
        gid = jnp.take(own_set, slots.reshape(-1), axis=0)
        active = (slot_ids[None, :] < count[:, None]).astype(jnp.float32)
        rowmask = jnp.repeat(active, FB, axis=1)[:, :, None]
        xmask = jnp.where(rowmask > 0, values, jnp.zeros_like(values))
        xweighted = (xmask.astype(jnp.float32) * quad[:, None, :]).astype(jnp.bfloat16)
        dloc = tile[slots[:, :, None], :, slots[:, None, :], :]
        dloc = dloc.transpose(0, 1, 3, 2, 4).reshape(group, width, width)
        centre = jnp.take(centre_blocks, gid, axis=1).reshape(3, group, width)
        spread = jnp.take(spread_blocks, gid, axis=0).reshape(group, width)
        vfac = coulomb(
            centre[0][:, :, None],
            centre[1][:, :, None],
            centre[2][:, :, None],
            spread[:, :, None],
            coords[:, 0][:, None, :],
            coords[:, 1][:, None, :],
            coords[:, 2][:, None, :],
        )
        gval = jnp.einsum("brc,bcg->brg", dloc, xmask, preferred_element_type=jnp.float32)
        fval = (gval * vfac * rowmask).astype(jnp.bfloat16)
        parts = jnp.einsum("brg,bcg->brc", fval, xweighted, preferred_element_type=jnp.float32)
        pieces = parts.reshape(group, TMAX, FB, TMAX, FB).transpose(0, 1, 3, 2, 4)
        total = total.at[slots[:, :, None], :, slots[:, None, :], :].add(pieces)
        return (total, None)

    items = (
        blocks.reshape(turns, group, TMAX),
        counts.reshape(turns, group),
        basis.reshape(turns, group, width, basis.shape[2]),
        points.reshape(turns, group, 3, points.shape[2]),
        weights.reshape(turns, group, weights.shape[1]),
    )
    start = jnp.zeros((UMAX, FB, UMAX, FB), jnp.float32)
    local_sum, _ = lax.scan(work, start, items)
    local_flat = local_sum.reshape(UMAX * FB, UMAX * FB)
    halved = lax.psum_scatter(local_flat, "rows", scatter_dimension=1, tiled=True)
    returned = lax.all_to_all(
        spread_rows(halved, stored, block_count, sources),
        "dom",
        split_axis=0,
        concat_axis=0,
        tiled=True,
    )
    gathered_terms = collect(returned, half_sets, block_count)
    summed = lax.psum_scatter(gathered_terms, "rows", scatter_dimension=1, tiled=True)
    return summed.astype(jnp.bfloat16)


def call(kernel, scalars, arrays, in_specs, out_shapes, out_specs, scratch, grid=(1,), cost=None, vmem=44):
    return pl.pallas_call(
        kernel,
        grid_spec=pltpu.PrefetchScalarGridSpec(
            num_scalar_prefetch=len(scalars),
            grid=grid,
            in_specs=in_specs,
            out_specs=out_specs,
            scratch_shapes=scratch,
        ),
        out_shape=out_shapes,
        cost_estimate=pl.CostEstimate(flops=cost[0], bytes_accessed=cost[1], transcendentals=0),
        compiler_params=pltpu.CompilerParams(vmem_limit_bytes=vmem * MIB),
    )(*scalars, *arrays)


def whole(shape):
    return pl.BlockSpec(shape, lambda *_: (0,) * len(shape))


def pick_kernel(peers, *refs):
    sets, full, outs = refs[:peers], refs[peers], refs[peers + 1 :]
    for k in range(peers):
        for q in range(UMAX):
            cols = pl.ds(pl.multiple_of(sets[k][0, q] * FB, FB), FB)
            outs[k][:, :, q * FB : (q + 1) * FB] = full[:, :, cols]


def pick(sets, full):
    nb, sub, cols = full.shape
    shape = (nb, sub, UMAX * FB)
    peers = len(sets)
    return call(
        functools.partial(pick_kernel, peers),
        sets,
        [full],
        [whole(full.shape)],
        [jax.ShapeDtypeStruct(shape, full.dtype)] * peers,
        [whole(shape)] * peers,
        [],
        cost=(0, 2 * nb * sub * (cols + peers * UMAX * FB)),
    )


def centre_kernel(own_set, core, centers, widths, out, turned):
    sub = out.shape[2]
    for p in range(UMAX):
        cols = pl.ds(pl.multiple_of(own_set[0, p] * FB, FB), FB)
        width = widths[:, cols]
        rows = jnp.concatenate([centers[:, cols], width * width, jnp.zeros((4, FB), jnp.float32)], axis=0)
        turned[...] = rows.T
        start = pl.multiple_of(core[0] * sub, sub)
        for c in range(4):
            out[c, p] = jnp.broadcast_to(turned[pl.ds(start, sub), c : c + 1], (sub, FB))


def centre_rows(own_set, core, centers, widths, sub):
    shape = (4, UMAX, sub, FB)
    return call(
        centre_kernel,
        [own_set, core],
        [centers, widths],
        [whole(centers.shape), whole(widths.shape)],
        jax.ShapeDtypeStruct(shape, jnp.float32),
        whole(shape),
        [pltpu.VMEM((FB, 8), jnp.float32)],
        cost=(0, 2 * 4 * UMAX * sub * FB * 4),
    )


def table_places(batches, group):
    lives = batches
    rows = lives + batches // group
    slots = batches * TMAX
    return lives, rows, rows + slots, rows + 2 * slots, rows + 3 * slots, rows + 4 * slots


def table_kernel(nb, near, group, me, owner, own_set, blocks, packed, counts, out, kbs, fill, bundle, sem):
    copy = pltpu.make_async_copy(packed.at[TMAX], bundle, sem)
    copy.start()
    half = counts.shape[0]
    at_lives, at_near, at_far, at_pos, at_col, _ = table_places(2 * half, group)
    spare = nb * near
    for p in range(UMAX):
        stored = owner[own_set[0, p]]
        kbs[p] = (lax.div(stored, nb) ^ me[0]) * nb + lax.rem(stored, nb)
    for c in range(TMAX + 1):
        fill[c] = 0
    copy.wait()

    def count_of(side, b):
        return bundle[b, TMAX].astype(jnp.int32) if side else counts[b]

    for side in (0, 1):

        @pl.loop(0, half)
        def _(b):
            count = count_of(side, b)
            fill[count] = fill[count] + 1

    place = 0
    for c in range(TMAX, -1, -1):
        many = fill[c]
        fill[c] = place
        place = place + many

    for side in (0, 1):

        @pl.loop(0, half)
        def _(b):
            count = count_of(side, b)
            j = fill[count]
            fill[count] = j + 1
            out[j] = side * half + b

            @pl.when(lax.rem(j, group) == 0)
            def _():
                out[at_lives + lax.div(j, group)] = count

            for s in range(TMAX):
                pos = bundle[b, s].astype(jnp.int32) if side else blocks[s, b]
                on = s < count
                at = j * TMAX + s
                out[at_pos + at] = pos
                out[at_col + at] = jnp.where(on, pos, UMAX)
                kb = kbs[pos]
                out[at_near + at] = jnp.where(on & (kb < spare), kb, spare)
                out[at_far + at] = jnp.where(on & (kb >= spare), kb - spare, spare)


def batch_tables(me, owner, own_set, blocks, packed, counts, nb, near):
    batches = 2 * counts.shape[0]
    group = math.gcd(batches, GROUP)
    size = table_places(batches, group)[-1]
    return call(
        functools.partial(table_kernel, nb, near, group),
        [me, owner, own_set, blocks],
        [packed, counts],
        [pl.BlockSpec(memory_space=pl.ANY), pl.BlockSpec(memory_space=pltpu.SMEM)],
        jax.ShapeDtypeStruct((size,), jnp.int32),
        pl.BlockSpec(memory_space=pltpu.SMEM),
        [
            pltpu.SMEM((UMAX,), jnp.int32),
            pltpu.SMEM((TMAX + 1,), jnp.int32),
            pltpu.SMEM(packed.shape[1:], packed.dtype),
            pltpu.SemaphoreType.DMA,
        ],
        cost=(0, 8 * batches * TMAX),
    )


def pack_kernel(points, weights, blocks, counts, out):
    batches, pts = weights.shape
    out[0:3] = points[...]
    out[3] = weights[...]
    lane = lax.broadcasted_iota(jnp.int32, (1, pts), 1)

    @pl.loop(0, batches)
    def _(b):
        row = jnp.where(lane == TMAX, counts[b], 0)
        for s in range(TMAX):
            row = jnp.where(lane == s, blocks[s, b], row)
        out[4, pl.ds(b, 1), :] = row.astype(jnp.float32)


def pack(points, weights, blocks, counts):
    shape = (5, *weights.shape)
    return call(
        pack_kernel,
        [],
        [points, weights, blocks, counts],
        [whole(points.shape), whole(weights.shape)] + [pl.BlockSpec(memory_space=pltpu.SMEM)] * 2,
        jax.ShapeDtypeStruct(shape, jnp.float32),
        whole(shape),
        [],
        cost=(0, 10 * 4 * weights.size),
    )


def add_up(sets, terms, total):
    total[...] = jnp.zeros(total.shape, total.dtype)
    for k, term in enumerate(terms):
        for q in range(UMAX):
            cols = pl.ds(pl.multiple_of(sets[k][0, q] * FB, FB), FB)
            total[:, :, cols] += term[:, :, q * FB : (q + 1) * FB].astype(jnp.float32)


def merge_kernel(peers, *refs):
    sets, terms, out, total = refs[:peers], refs[peers : 2 * peers], refs[-2], refs[-1]
    add_up(sets, terms, total)
    out[...] = total[...].astype(out.dtype)


def merge(sets, terms, cols):
    nb, sub, wide = terms[0].shape
    shape = (nb, sub, cols)
    return call(
        functools.partial(merge_kernel, len(terms)),
        sets,
        terms,
        [whole(t.shape) for t in terms],
        jax.ShapeDtypeStruct(shape, jnp.bfloat16),
        whole(shape),
        [pltpu.VMEM(shape, jnp.float32)],
        cost=(0, 2 * nb * sub * (cols + 5 * wide)),
    )


def finish_kernel(peers, *refs):
    sets, core = refs[:peers], refs[peers]
    terms, fars = refs[peers + 1 : 2 * peers + 1], refs[2 * peers + 1 : -3]
    keep, give, total = refs[-3:]
    add_up(sets, terms, total)
    half = keep.shape[2]
    for out, side in ((keep, core[0]), (give, 1 - core[0])):
        cols = pl.ds(pl.multiple_of(side * half, FB), half)
        for b, far in enumerate(fars):
            out[b] = (total[b, :, cols] + far[0, :, cols].astype(jnp.float32)).astype(out.dtype)


def finish(sets, core, terms, fars):
    nb, sub, wide = terms[0].shape
    cols = fars[0].shape[2]
    shape = (nb, sub, cols // 2)
    return call(
        functools.partial(finish_kernel, len(terms)),
        [*sets, core],
        [*terms, *fars],
        [whole(t.shape) for t in (*terms, *fars)],
        [jax.ShapeDtypeStruct(shape, jnp.bfloat16)] * 2,
        [whole(shape)] * 2,
        [pltpu.VMEM((nb, sub, cols), jnp.float32)],
        cost=(0, 2 * nb * sub * (2 * cols + 5 * wide)),
    )


def batch_kernel(group, pieces, split, table, *refs):
    xs, quads, centre_in = refs[0:2], refs[2:4], refs[4]
    parts = refs[5 : 5 + pieces]
    outs = refs[5 + pieces : -7]
    dense, acc, xbuf, qbuf, centre, sems, xsems = refs[-7:]
    nb, sub, wide = parts[0].shape
    spare = nb * pieces
    batches, _, pts = xbuf.shape
    half = batches // 2
    at_lives, at_near, at_far, at_pos, at_col, _ = table_places(batches, group)
    at_row = at_far if split else at_near

    def fetch(j, act):
        b = table[j]
        for side in (0, 1):

            @pl.when((b >= half) if side else (b < half))
            def _():
                act(pltpu.make_async_copy(xs[side].at[b - half * side], xbuf.at[j], xsems.at[j]))

    copies = [
        pltpu.make_async_copy(part, dense.at[pl.ds(nb * k, nb), :, pl.ds(0, wide)], sems.at[k])
        for k, part in enumerate(parts)
    ]
    copies.append(pltpu.make_async_copy(centre_in, centre, sems.at[pieces]))
    for side in (0, 1):
        quad = qbuf.at[:, pl.ds(half * side, half)]
        copies.append(pltpu.make_async_copy(quads[side].at[pl.ds(0, 4)], quad, sems.at[pieces + 1 + side]))
    for copy in copies:
        copy.start()

    @pl.loop(0, batches)
    def _(j):
        fetch(j, lambda copy: copy.start())

    acc[...] = jnp.zeros(acc.shape, acc.dtype)
    dense[:, :, wide:] = jnp.zeros((spare + 1, sub, FB), dense.dtype)
    dense[spare, :, :wide] = jnp.zeros((sub, wide), dense.dtype)
    for copy in copies:
        copy.wait()

    def lanes(col):
        return jnp.concatenate([col] * (pts // FB), axis=1)

    def one(j, live):
        b = table[j]
        row = [table[at_row + j * TMAX + s] for s in range(live)]
        pos = [table[at_pos + j * TMAX + s] for s in range(live)]
        col = [pl.ds(pl.multiple_of(table[at_col + j * TMAX + s] * FB, FB), FB) for s in range(live)]
        x = xbuf[j, : live * FB, :]
        d = jnp.concatenate(
            [jnp.concatenate([dense[r, :, c] for c in col], axis=1) for r in row], axis=0
        )
        gval = jnp.dot(d, x, preferred_element_type=jnp.float32)
        fval = []
        for s in range(live):
            dist = None
            for axis in range(3):
                diff = lanes(centre[axis, pos[s]]) - qbuf[axis, pl.ds(b, 1), :]
                dist = diff * diff if dist is None else dist + diff * diff
            dist = dist + lanes(centre[3, pos[s]])
            fval.append((gval[s * sub : (s + 1) * sub] * lax.rsqrt(dist)).astype(jnp.bfloat16))
        fval = jnp.concatenate(fval, axis=0)
        xw = (x.astype(jnp.float32) * qbuf[3, pl.ds(b, 1), :]).astype(jnp.bfloat16)
        part = lax.dot_general(
            fval, xw, (((1,), (1,)), ((), ())), preferred_element_type=jnp.float32
        )
        return row, col, part

    @pl.loop(0, batches // group)
    def _(h):
        @pl.loop(0, group)
        def _(u):
            fetch(h * group + u, lambda copy: copy.wait())

        for live in range(2, TMAX + 1):

            @pl.when(table[at_lives + h] == live)
            def _():
                for row, col, part in [one(h * group + u, live) for u in range(group)]:
                    for s in range(live):
                        for t in range(live):
                            acc[row[s], :, col[t]] += part[s * sub : (s + 1) * sub, t * FB : (t + 1) * FB]

    start = 0
    for out in outs:
        rows = out.shape[0]
        out[...] = acc[start : start + rows, :, :wide].astype(out.dtype)
        start += rows


def batch_sums(table, xs, quads, centre, parts, split):
    _, width, pts = xs[0].shape
    batches = 2 * xs[0].shape[0]
    group = math.gcd(batches, GROUP)
    nb, sub, wide = parts[0].shape
    pieces = len(parts)
    size = 1 if split else nb
    out_shapes = [
        jax.ShapeDtypeStruct((size, sub, wide), jnp.bfloat16 if k else jnp.float32)
        for k in range(pieces)
        for _ in range(nb // size)
    ]
    flops = 2 * batches * 2 * width * (width // 2) * pts
    return call(
        functools.partial(batch_kernel, group, pieces, split),
        [table],
        [*xs, *quads, centre, *parts],
        [pl.BlockSpec(memory_space=pl.ANY)] * (5 + pieces),
        out_shapes,
        [whole(out.shape) for out in out_shapes],
        [
            pltpu.VMEM((nb * pieces + 1, sub, wide + FB), jnp.bfloat16),
            pltpu.VMEM((nb * pieces + 1, sub, wide + FB), jnp.float32),
            pltpu.VMEM((batches, width, pts), jnp.bfloat16),
            pltpu.VMEM((4, batches, pts), jnp.float32),
            pltpu.VMEM(centre.shape, jnp.float32),
            pltpu.SemaphoreType.DMA((pieces + 3,)),
            pltpu.SemaphoreType.DMA((batches,)),
        ],
        cost=(flops, 2 * batches * width * pts),
    )


def per_device(density, owner, touched, blocks, counts, basis, points, weights, centers, widths):
    n = lax.axis_size("dom")
    cores = lax.axis_size("rows")
    i = lax.axis_index("dom")
    r = lax.axis_index("rows")
    nb = density.shape[0] // FB
    sub = FB // cores
    cols = density.shape[1]
    near = n // 2
    core = r.reshape(1)

    def swap(x, k):
        return lax.ppermute(x, "dom", [(a, a ^ k) for a in range(n)])

    def across(x):
        return lax.ppermute(x, "rows", [(a, cores - 1 - a) for a in range(cores)])

    def stay(x):
        return pltpu.with_memory_space_constraint(x, pltpu.HBM)

    own = lax.dynamic_index_in_dim(density.reshape(nb, cores, sub, cols), r, 1, keepdims=False)
    sets = [touched] + [swap(touched, k) for k in range(1, near)]
    packed = pack(stay(points.transpose(1, 0, 2)), stay(weights), stay(blocks.T), stay(counts))
    packed_b = across(packed)
    own, sets, basis, packed_b = lax.optimization_barrier((own, sets, basis, packed_b))
    far = swap(own, near)
    sets[0] = stay(touched)
    picked = pick(sets, own)
    parts = [picked[0]] + [swap(picked[k], k) for k in range(1, near)]
    xs = (stay(basis), across(basis))
    quads = (packed, packed_b)
    table = batch_tables(i.reshape(1), stay(owner), sets[0], stay(blocks.T), packed_b, stay(counts), nb, near)
    centre = centre_rows(sets[0], core, stay(centers), stay(widths.reshape(1, -1)), sub)

    far, table, centre = lax.optimization_barrier((far, table, centre))
    picked = pick(sets, far)
    far_parts = [picked[0]] + [swap(picked[k], k) for k in range(1, near)]
    table, _ = lax.optimization_barrier((table, picked[0]))

    common = (xs, quads, centre)
    sums = batch_sums(table, *common, parts, False)
    table, _ = lax.optimization_barrier((table, sums[0]))
    far_sums = batch_sums(table, *common, far_parts, True)
    terms = [sums[0]] + [swap(sums[k], k) for k in range(1, near)]
    far_sums, terms = lax.optimization_barrier((far_sums, terms))
    far_terms = []
    for b in range(nb):
        chunk = [far_sums[b]] + [swap(far_sums[nb * k + b], k) for k in range(1, near)]
        merged = merge(sets, chunk, cols)
        far_sums, merged = lax.optimization_barrier((far_sums, merged))
        far_terms.append(swap(merged, near))
    keep, give = finish(sets, core, terms, far_terms)
    got = across(give)
    pair = jnp.where(r == 0, jnp.stack([keep, got], axis=1), jnp.stack([got, keep], axis=1))
    return pair.reshape(nb * FB, cols // cores)


def solution(mesh):
    in_specs = (
        P(("groups", "dom"), None),
        P("groups"),
        P(("groups", "dom"), None),
        P(("groups", "dom", "rows"), None),
        P(("groups", "dom", "rows")),
        P(("groups", "dom", "rows"), None, None),
        P(("groups", "dom", "rows"), None, None),
        P(("groups", "dom", "rows"), None),
        P(None, "groups"),
        P("groups"),
    )
    out_specs = P(("groups", "dom"), "rows")

    def run(*args):
        n, cores = mesh.shape["dom"], mesh.shape["rows"]
        rows_here = args[0].shape[0] // (mesh.shape["groups"] * n)
        split = rows_here % FB == 0 and cores == 2 and n >= 4 and n & (n - 1) == 0
        body = per_device if split else per_device_any
        return jax.shard_map(body, mesh=mesh, in_specs=in_specs, out_specs=out_specs, check_vma=False)(*args)

    return run
```

```python
import functools
import math

import jax
import jax.numpy as jnp
from jax import lax
from jax.experimental import pallas as pl
from jax.experimental.pallas import tpu as pltpu
from jax.sharding import PartitionSpec as P

FB = 128
TMAX = 4
UMAX = 8
GROUP = 6
MIB = 1024 * 1024


def coulomb(centre_x, centre_y, centre_z, spread, point_x, point_y, point_z):
    dist = (centre_x - point_x) ** 2 + (centre_y - point_y) ** 2 + (centre_z - point_z) ** 2
    return 1.0 / jnp.sqrt(dist + spread * spread)


def lookup_owner(owner, block_ids):
    match = block_ids[:, None] == jnp.arange(owner.shape[0], dtype=jnp.int32)[None, :]
    return jnp.sum(jnp.where(match, owner[None, :], 0), axis=1)


def answer_for(density, column_sets):
    rows_here = density.shape[0]
    sources, wanted = column_sets.shape
    blocked = density.reshape(rows_here, density.shape[1] // FB, FB)
    picked = jnp.take(blocked, column_sets.reshape(-1), axis=1)
    return picked.reshape(rows_here, sources, wanted * FB).transpose(1, 0, 2)


def spread_rows(terms, stored, block_count, sources):
    columns = terms.shape[1]
    expanded = jnp.zeros((block_count, FB, columns), jnp.float32)
    expanded = expanded.at[stored].set(terms.reshape(UMAX, FB, columns))
    return expanded.reshape(sources, block_count * FB // sources, columns)


def collect(returned, column_sets, block_count):
    sources, rows_here, columns = returned.shape
    wanted = column_sets.shape[1]
    pieces = returned.reshape(sources, rows_here, wanted, FB).transpose(1, 0, 2, 3)
    pieces = pieces.reshape(rows_here, sources * wanted, FB)
    total = jnp.zeros((rows_here, block_count, FB), jnp.float32)
    total = total.at[:, column_sets.reshape(-1)].add(pieces)
    return total.reshape(rows_here, block_count * FB)


def per_device_any(density, owner, touched, blocks, counts, basis, points, weights, centers, widths):
    rows_count = lax.axis_size("rows")
    rows_index = lax.axis_index("rows")
    batches = blocks.shape[0]
    block_count = owner.shape[0]
    width = TMAX * FB
    share = UMAX // rows_count
    own_set = touched[0]
    all_sets = lax.all_gather(touched, "dom", axis=0, tiled=True)
    sources = all_sets.shape[0]
    half_sets = lax.dynamic_slice_in_dim(all_sets, rows_index * share, share, 1)
    got = lax.all_to_all(
        answer_for(density, all_sets), "dom", split_axis=0, concat_axis=0, tiled=True
    )
    panel = got.reshape(block_count * FB, UMAX * FB)
    stored = lookup_owner(owner, own_set)
    tile = jnp.take(panel.reshape(block_count, FB, UMAX * FB), stored, axis=0).reshape(
        UMAX, FB, UMAX, FB
    )
    centre_blocks = centers.reshape(3, block_count, FB)
    spread_blocks = widths.reshape(block_count, FB)
    slot_ids = jnp.arange(TMAX, dtype=jnp.int32)
    group = math.gcd(batches, 8)
    turns = batches // group

    def work(total, item):
        slots, count, values, coords, quad = item
        gid = jnp.take(own_set, slots.reshape(-1), axis=0)
        active = (slot_ids[None, :] < count[:, None]).astype(jnp.float32)
        rowmask = jnp.repeat(active, FB, axis=1)[:, :, None]
        xmask = jnp.where(rowmask > 0, values, jnp.zeros_like(values))
        xweighted = (xmask.astype(jnp.float32) * quad[:, None, :]).astype(jnp.bfloat16)
        dloc = tile[slots[:, :, None], :, slots[:, None, :], :]
        dloc = dloc.transpose(0, 1, 3, 2, 4).reshape(group, width, width)
        centre = jnp.take(centre_blocks, gid, axis=1).reshape(3, group, width)
        spread = jnp.take(spread_blocks, gid, axis=0).reshape(group, width)
        vfac = coulomb(
            centre[0][:, :, None],
            centre[1][:, :, None],
            centre[2][:, :, None],
            spread[:, :, None],
            coords[:, 0][:, None, :],
            coords[:, 1][:, None, :],
            coords[:, 2][:, None, :],
        )
        gval = jnp.einsum("brc,bcg->brg", dloc, xmask, preferred_element_type=jnp.float32)
        fval = (gval * vfac * rowmask).astype(jnp.bfloat16)
        parts = jnp.einsum("brg,bcg->brc", fval, xweighted, preferred_element_type=jnp.float32)
        pieces = parts.reshape(group, TMAX, FB, TMAX, FB).transpose(0, 1, 3, 2, 4)
        total = total.at[slots[:, :, None], :, slots[:, None, :], :].add(pieces)
        return (total, None)

    items = (
        blocks.reshape(turns, group, TMAX),
        counts.reshape(turns, group),
        basis.reshape(turns, group, width, basis.shape[2]),
        points.reshape(turns, group, 3, points.shape[2]),
        weights.reshape(turns, group, weights.shape[1]),
    )
    start = jnp.zeros((UMAX, FB, UMAX, FB), jnp.float32)
    local_sum, _ = lax.scan(work, start, items)
    local_flat = local_sum.reshape(UMAX * FB, UMAX * FB)
    halved = lax.psum_scatter(local_flat, "rows", scatter_dimension=1, tiled=True)
    returned = lax.all_to_all(
        spread_rows(halved, stored, block_count, sources),
        "dom",
        split_axis=0,
        concat_axis=0,
        tiled=True,
    )
    gathered_terms = collect(returned, half_sets, block_count)
    summed = lax.psum_scatter(gathered_terms, "rows", scatter_dimension=1, tiled=True)
    return summed.astype(jnp.bfloat16)


def call(kernel, scalars, arrays, in_specs, out_shapes, out_specs, scratch, grid=(1,), cost=None, vmem=44):
    return pl.pallas_call(
        kernel,
        grid_spec=pltpu.PrefetchScalarGridSpec(
            num_scalar_prefetch=len(scalars),
            grid=grid,
            in_specs=in_specs,
            out_specs=out_specs,
            scratch_shapes=scratch,
        ),
        out_shape=out_shapes,
        cost_estimate=pl.CostEstimate(flops=cost[0], bytes_accessed=cost[1], transcendentals=0),
        compiler_params=pltpu.CompilerParams(vmem_limit_bytes=vmem * MIB),
    )(*scalars, *arrays)


def whole(shape):
    return pl.BlockSpec(shape, lambda *_: (0,) * len(shape))


def pick_kernel(peers, *refs):
    sets, full, outs = refs[:peers], refs[peers], refs[peers + 1 :]
    for k in range(peers):
        for q in range(UMAX):
            cols = pl.ds(pl.multiple_of(sets[k][0, q] * FB, FB), FB)
            outs[k][:, :, q * FB : (q + 1) * FB] = full[:, :, cols]


def pick(sets, full):
    nb, sub, cols = full.shape
    shape = (nb, sub, UMAX * FB)
    peers = len(sets)
    return call(
        functools.partial(pick_kernel, peers),
        sets,
        [full],
        [whole(full.shape)],
        [jax.ShapeDtypeStruct(shape, full.dtype)] * peers,
        [whole(shape)] * peers,
        [],
        cost=(0, 2 * nb * sub * (cols + peers * UMAX * FB)),
    )


def centre_kernel(own_set, core, centers, widths, out, turned):
    sub = out.shape[2]
    for p in range(UMAX):
        cols = pl.ds(pl.multiple_of(own_set[0, p] * FB, FB), FB)
        width = widths[:, cols]
        rows = jnp.concatenate([centers[:, cols], width * width, jnp.zeros((4, FB), jnp.float32)], axis=0)
        turned[...] = rows.T
        start = pl.multiple_of(core[0] * sub, sub)
        for c in range(4):
            out[c, p] = jnp.broadcast_to(turned[pl.ds(start, sub), c : c + 1], (sub, FB))


def centre_rows(own_set, core, centers, widths, sub):
    shape = (4, UMAX, sub, FB)
    return call(
        centre_kernel,
        [own_set, core],
        [centers, widths],
        [whole(centers.shape), whole(widths.shape)],
        jax.ShapeDtypeStruct(shape, jnp.float32),
        whole(shape),
        [pltpu.VMEM((FB, 8), jnp.float32)],
        cost=(0, 2 * 4 * UMAX * sub * FB * 4),
    )


def table_places(batches, group):
    lives = batches
    rows = lives + batches // group
    slots = batches * TMAX
    return lives, rows, rows + slots, rows + 2 * slots, rows + 3 * slots, rows + 4 * slots


def table_kernel(nb, near, group, me, owner, own_set, blocks, packed, counts, out, kbs, fill, bundle, sem):
    copy = pltpu.make_async_copy(packed.at[TMAX], bundle, sem)
    copy.start()
    half = counts.shape[0]
    at_lives, at_near, at_far, at_pos, at_col, _ = table_places(2 * half, group)
    spare = nb * near
    for p in range(UMAX):
        stored = owner[own_set[0, p]]
        kbs[p] = (lax.div(stored, nb) ^ me[0]) * nb + lax.rem(stored, nb)
    for c in range(TMAX + 1):
        fill[c] = 0
    copy.wait()

    def count_of(side, b):
        return bundle[b, TMAX].astype(jnp.int32) if side else counts[b]

    for side in (0, 1):

        @pl.loop(0, half)
        def _(b):
            count = count_of(side, b)
            fill[count] = fill[count] + 1

    place = 0
    for c in range(TMAX, -1, -1):
        many = fill[c]
        fill[c] = place
        place = place + many

    for side in (0, 1):

        @pl.loop(0, half)
        def _(b):
            count = count_of(side, b)
            j = fill[count]
            fill[count] = j + 1
            out[j] = side * half + b

            @pl.when(lax.rem(j, group) == 0)
            def _():
                out[at_lives + lax.div(j, group)] = count

            for s in range(TMAX):
                pos = bundle[b, s].astype(jnp.int32) if side else blocks[s, b]
                on = s < count
                at = j * TMAX + s
                out[at_pos + at] = pos
                out[at_col + at] = jnp.where(on, pos, UMAX)
                kb = kbs[pos]
                out[at_near + at] = jnp.where(on & (kb < spare), kb, spare)
                out[at_far + at] = jnp.where(on & (kb >= spare), kb - spare, spare)


def batch_tables(me, owner, own_set, blocks, packed, counts, nb, near):
    batches = 2 * counts.shape[0]
    group = math.gcd(batches, GROUP)
    size = table_places(batches, group)[-1]
    return call(
        functools.partial(table_kernel, nb, near, group),
        [me, owner, own_set, blocks],
        [packed, counts],
        [pl.BlockSpec(memory_space=pl.ANY), pl.BlockSpec(memory_space=pltpu.SMEM)],
        jax.ShapeDtypeStruct((size,), jnp.int32),
        pl.BlockSpec(memory_space=pltpu.SMEM),
        [
            pltpu.SMEM((UMAX,), jnp.int32),
            pltpu.SMEM((TMAX + 1,), jnp.int32),
            pltpu.SMEM(packed.shape[1:], packed.dtype),
            pltpu.SemaphoreType.DMA,
        ],
        cost=(0, 8 * batches * TMAX),
    )


def pack_kernel(points, weights, blocks, counts, out):
    batches, pts = weights.shape
    out[0:3] = points[...]
    out[3] = weights[...]
    lane = lax.broadcasted_iota(jnp.int32, (1, pts), 1)

    @pl.loop(0, batches)
    def _(b):
        row = jnp.where(lane == TMAX, counts[b], 0)
        for s in range(TMAX):
            row = jnp.where(lane == s, blocks[s, b], row)
        out[4, pl.ds(b, 1), :] = row.astype(jnp.float32)


def pack(points, weights, blocks, counts):
    shape = (5, *weights.shape)
    return call(
        pack_kernel,
        [],
        [points, weights, blocks, counts],
        [whole(points.shape), whole(weights.shape)] + [pl.BlockSpec(memory_space=pltpu.SMEM)] * 2,
        jax.ShapeDtypeStruct(shape, jnp.float32),
        whole(shape),
        [],
        cost=(0, 10 * 4 * weights.size),
    )


def add_up(sets, terms, total):
    total[...] = jnp.zeros(total.shape, total.dtype)
    for k, term in enumerate(terms):
        for q in range(UMAX):
            cols = pl.ds(pl.multiple_of(sets[k][0, q] * FB, FB), FB)
            total[:, :, cols] += term[:, :, q * FB : (q + 1) * FB].astype(jnp.float32)


def merge_kernel(peers, *refs):
    sets, terms, out, total = refs[:peers], refs[peers : 2 * peers], refs[-2], refs[-1]
    add_up(sets, terms, total)
    out[...] = total[...].astype(out.dtype)


def merge(sets, terms, cols):
    nb, sub, wide = terms[0].shape
    shape = (nb, sub, cols)
    return call(
        functools.partial(merge_kernel, len(terms)),
        sets,
        terms,
        [whole(t.shape) for t in terms],
        jax.ShapeDtypeStruct(shape, jnp.bfloat16),
        whole(shape),
        [pltpu.VMEM(shape, jnp.float32)],
        cost=(0, 2 * nb * sub * (cols + 5 * wide)),
    )


def finish_kernel(peers, *refs):
    sets, core = refs[:peers], refs[peers]
    terms, fars = refs[peers + 1 : 2 * peers + 1], refs[2 * peers + 1 : -3]
    keep, give, total = refs[-3:]
    add_up(sets, terms, total)
    half = keep.shape[2]
    for out, side in ((keep, core[0]), (give, 1 - core[0])):
        cols = pl.ds(pl.multiple_of(side * half, FB), half)
        for b, far in enumerate(fars):
            out[b] = (total[b, :, cols] + far[0, :, cols].astype(jnp.float32)).astype(out.dtype)


def finish(sets, core, terms, fars):
    nb, sub, wide = terms[0].shape
    cols = fars[0].shape[2]
    shape = (nb, sub, cols // 2)
    return call(
        functools.partial(finish_kernel, len(terms)),
        [*sets, core],
        [*terms, *fars],
        [whole(t.shape) for t in (*terms, *fars)],
        [jax.ShapeDtypeStruct(shape, jnp.bfloat16)] * 2,
        [whole(shape)] * 2,
        [pltpu.VMEM((nb, sub, cols), jnp.float32)],
        cost=(0, 2 * nb * sub * (2 * cols + 5 * wide)),
    )


def batch_kernel(group, pieces, split, table, *refs):
    xs, quads, centre_in = refs[0:2], refs[2:4], refs[4]
    parts = refs[5 : 5 + pieces]
    outs = refs[5 + pieces : -7]
    dense, acc, xbuf, qbuf, centre, sems, xsems = refs[-7:]
    nb, sub, wide = parts[0].shape
    spare = nb * pieces
    batches, _, pts = xbuf.shape
    half = batches // 2
    at_lives, at_near, at_far, at_pos, at_col, _ = table_places(batches, group)
    at_row = at_far if split else at_near

    def fetch(j, sem):
        b = table[j]
        for side in (0, 1):

            @pl.when((b >= half) if side else (b < half))
            def _():
                pltpu.make_async_copy(xs[side].at[b - half * side], xbuf.at[j], sem).start()

    copies = [
        pltpu.make_async_copy(part, dense.at[pl.ds(nb * k, nb), :, pl.ds(0, wide)], sems.at[k])
        for k, part in enumerate(parts)
    ]
    copies.append(pltpu.make_async_copy(centre_in, centre, sems.at[pieces]))
    for side in (0, 1):
        quad = qbuf.at[:, pl.ds(half * side, half)]
        copies.append(pltpu.make_async_copy(quads[side].at[pl.ds(0, 4)], quad, sems.at[pieces + 1 + side]))
    for copy in copies:
        copy.start()

    @pl.loop(0, batches // group)
    def _(h):
        for u in range(group):
            fetch(h * group + u, xsems.at[h])

    acc[...] = jnp.zeros(acc.shape, acc.dtype)
    dense[:, :, wide:] = jnp.zeros((spare + 1, sub, FB), dense.dtype)
    dense[spare, :, :wide] = jnp.zeros((sub, wide), dense.dtype)
    for copy in copies:
        copy.wait()

    def lanes(col):
        return jnp.concatenate([col] * (pts // FB), axis=1)

    def one(j, live):
        b = table[j]
        row = [table[at_row + j * TMAX + s] for s in range(live)]
        pos = [table[at_pos + j * TMAX + s] for s in range(live)]
        col = [pl.ds(pl.multiple_of(table[at_col + j * TMAX + s] * FB, FB), FB) for s in range(live)]
        x = xbuf[j, : live * FB, :]
        d = jnp.concatenate(
            [jnp.concatenate([dense[r, :, c] for c in col], axis=1) for r in row], axis=0
        )
        gval = jnp.dot(d, x, preferred_element_type=jnp.float32)
        fval = []
        for s in range(live):
            dist = None
            for axis in range(3):
                diff = lanes(centre[axis, pos[s]]) - qbuf[axis, pl.ds(b, 1), :]
                dist = diff * diff if dist is None else dist + diff * diff
            dist = dist + lanes(centre[3, pos[s]])
            fval.append((gval[s * sub : (s + 1) * sub] * lax.rsqrt(dist)).astype(jnp.bfloat16))
        fval = jnp.concatenate(fval, axis=0)
        xw = (x.astype(jnp.float32) * qbuf[3, pl.ds(b, 1), :]).astype(jnp.bfloat16)
        part = lax.dot_general(
            fval, xw, (((1,), (1,)), ((), ())), preferred_element_type=jnp.float32
        )
        return row, col, part

    @pl.loop(0, batches // group)
    def _(h):
        arrived = xbuf.at[pl.ds(h * group, group)]
        pltpu.make_async_copy(arrived, arrived, xsems.at[h]).wait()
        for live in range(2, TMAX + 1):

            @pl.when(table[at_lives + h] == live)
            def _():
                for row, col, part in [one(h * group + u, live) for u in range(group)]:
                    for s in range(live):
                        for t in range(live):
                            acc[row[s], :, col[t]] += part[s * sub : (s + 1) * sub, t * FB : (t + 1) * FB]

    start = 0
    for out in outs:
        rows = out.shape[0]
        out[...] = acc[start : start + rows, :, :wide].astype(out.dtype)
        start += rows


def batch_sums(table, xs, quads, centre, parts, split):
    _, width, pts = xs[0].shape
    batches = 2 * xs[0].shape[0]
    group = math.gcd(batches, GROUP)
    nb, sub, wide = parts[0].shape
    pieces = len(parts)
    size = 1 if split else nb
    out_shapes = [
        jax.ShapeDtypeStruct((size, sub, wide), jnp.bfloat16 if k else jnp.float32)
        for k in range(pieces)
        for _ in range(nb // size)
    ]
    flops = 2 * batches * 2 * width * (width // 2) * pts
    return call(
        functools.partial(batch_kernel, group, pieces, split),
        [table],
        [*xs, *quads, centre, *parts],
        [pl.BlockSpec(memory_space=pl.ANY)] * (5 + pieces),
        out_shapes,
        [whole(out.shape) for out in out_shapes],
        [
            pltpu.VMEM((nb * pieces + 1, sub, wide + FB), jnp.bfloat16),
            pltpu.VMEM((nb * pieces + 1, sub, wide + FB), jnp.float32),
            pltpu.VMEM((batches, width, pts), jnp.bfloat16),
            pltpu.VMEM((4, batches, pts), jnp.float32),
            pltpu.VMEM(centre.shape, jnp.float32),
            pltpu.SemaphoreType.DMA((pieces + 3,)),
            pltpu.SemaphoreType.DMA((batches // group,)),
        ],
        cost=(flops, 2 * batches * width * pts),
    )


def per_device(density, owner, touched, blocks, counts, basis, points, weights, centers, widths):
    n = lax.axis_size("dom")
    cores = lax.axis_size("rows")
    i = lax.axis_index("dom")
    r = lax.axis_index("rows")
    nb = density.shape[0] // FB
    sub = FB // cores
    cols = density.shape[1]
    near = n // 2
    core = r.reshape(1)

    def swap(x, k):
        return lax.ppermute(x, "dom", [(a, a ^ k) for a in range(n)])

    def across(x):
        return lax.ppermute(x, "rows", [(a, cores - 1 - a) for a in range(cores)])

    def stay(x):
        return pltpu.with_memory_space_constraint(x, pltpu.HBM)

    own = lax.dynamic_index_in_dim(density.reshape(nb, cores, sub, cols), r, 1, keepdims=False)
    sets = [touched] + [swap(touched, k) for k in range(1, near)]
    packed = pack(stay(points.transpose(1, 0, 2)), stay(weights), stay(blocks.T), stay(counts))
    packed_b = across(packed)
    own, sets, basis, packed_b = lax.optimization_barrier((own, sets, basis, packed_b))
    far = swap(own, near)
    sets[0] = stay(touched)
    picked = pick(sets, own)
    parts = [picked[0]] + [swap(picked[k], k) for k in range(1, near)]
    xs = (stay(basis), across(basis))
    quads = (packed, packed_b)
    table = batch_tables(i.reshape(1), stay(owner), sets[0], stay(blocks.T), packed_b, stay(counts), nb, near)
    centre = centre_rows(sets[0], core, stay(centers), stay(widths.reshape(1, -1)), sub)

    far, table, centre = lax.optimization_barrier((far, table, centre))
    picked = pick(sets, far)
    far_parts = [picked[0]] + [swap(picked[k], k) for k in range(1, near)]
    table, _ = lax.optimization_barrier((table, picked[0]))

    common = (xs, quads, centre)
    sums = batch_sums(table, *common, parts, False)
    table, _ = lax.optimization_barrier((table, sums[0]))
    far_sums = batch_sums(table, *common, far_parts, True)
    terms = [sums[0], sums[1]] + [swap(sums[k], k) for k in range(2, near)]
    far_sums, terms = lax.optimization_barrier((far_sums, terms))
    far_terms = []
    for b in range(nb):
        chunk = [far_sums[b]] + [swap(far_sums[nb * k + b], k) for k in range(1, near)]
        merged = merge(sets, chunk, cols)
        far_sums, merged, terms[1] = lax.optimization_barrier((far_sums, merged, terms[1]))
        far_terms.append(swap(merged, near))
    terms[1] = swap(terms[1], 1)
    keep, give = finish(sets, core, terms, far_terms)
    got = across(give)
    pair = jnp.where(r == 0, jnp.stack([keep, got], axis=1), jnp.stack([got, keep], axis=1))
    return pair.reshape(nb * FB, cols // cores)


def solution(mesh):
    in_specs = (
        P(("groups", "dom"), None),
        P("groups"),
        P(("groups", "dom"), None),
        P(("groups", "dom", "rows"), None),
        P(("groups", "dom", "rows")),
        P(("groups", "dom", "rows"), None, None),
        P(("groups", "dom", "rows"), None, None),
        P(("groups", "dom", "rows"), None),
        P(None, "groups"),
        P("groups"),
    )
    out_specs = P(("groups", "dom"), "rows")

    def run(*args):
        n, cores = mesh.shape["dom"], mesh.shape["rows"]
        rows_here = args[0].shape[0] // (mesh.shape["groups"] * n)
        split = rows_here % FB == 0 and cores == 2 and n >= 4 and n & (n - 1) == 0
        body = per_device if split else per_device_any
        return jax.shard_map(body, mesh=mesh, in_specs=in_specs, out_specs=out_specs, check_vma=False)(*args)

    return run
```

```python
import functools
import math

import jax
import jax.numpy as jnp
from jax import lax
from jax.experimental import pallas as pl
from jax.experimental.pallas import tpu as pltpu
from jax.sharding import PartitionSpec as P

FB = 128
TMAX = 4
UMAX = 8
GROUP = 6
MIB = 1024 * 1024


def coulomb(centre_x, centre_y, centre_z, spread, point_x, point_y, point_z):
    dist = (centre_x - point_x) ** 2 + (centre_y - point_y) ** 2 + (centre_z - point_z) ** 2
    return 1.0 / jnp.sqrt(dist + spread * spread)


def lookup_owner(owner, block_ids):
    match = block_ids[:, None] == jnp.arange(owner.shape[0], dtype=jnp.int32)[None, :]
    return jnp.sum(jnp.where(match, owner[None, :], 0), axis=1)


def answer_for(density, column_sets):
    rows_here = density.shape[0]
    sources, wanted = column_sets.shape
    blocked = density.reshape(rows_here, density.shape[1] // FB, FB)
    picked = jnp.take(blocked, column_sets.reshape(-1), axis=1)
    return picked.reshape(rows_here, sources, wanted * FB).transpose(1, 0, 2)


def spread_rows(terms, stored, block_count, sources):
    columns = terms.shape[1]
    expanded = jnp.zeros((block_count, FB, columns), jnp.float32)
    expanded = expanded.at[stored].set(terms.reshape(UMAX, FB, columns))
    return expanded.reshape(sources, block_count * FB // sources, columns)


def collect(returned, column_sets, block_count):
    sources, rows_here, columns = returned.shape
    wanted = column_sets.shape[1]
    pieces = returned.reshape(sources, rows_here, wanted, FB).transpose(1, 0, 2, 3)
    pieces = pieces.reshape(rows_here, sources * wanted, FB)
    total = jnp.zeros((rows_here, block_count, FB), jnp.float32)
    total = total.at[:, column_sets.reshape(-1)].add(pieces)
    return total.reshape(rows_here, block_count * FB)


def per_device_any(density, owner, touched, blocks, counts, basis, points, weights, centers, widths):
    rows_count = lax.axis_size("rows")
    rows_index = lax.axis_index("rows")
    batches = blocks.shape[0]
    block_count = owner.shape[0]
    width = TMAX * FB
    share = UMAX // rows_count
    own_set = touched[0]
    all_sets = lax.all_gather(touched, "dom", axis=0, tiled=True)
    sources = all_sets.shape[0]
    half_sets = lax.dynamic_slice_in_dim(all_sets, rows_index * share, share, 1)
    got = lax.all_to_all(
        answer_for(density, all_sets), "dom", split_axis=0, concat_axis=0, tiled=True
    )
    panel = got.reshape(block_count * FB, UMAX * FB)
    stored = lookup_owner(owner, own_set)
    tile = jnp.take(panel.reshape(block_count, FB, UMAX * FB), stored, axis=0).reshape(
        UMAX, FB, UMAX, FB
    )
    centre_blocks = centers.reshape(3, block_count, FB)
    spread_blocks = widths.reshape(block_count, FB)
    slot_ids = jnp.arange(TMAX, dtype=jnp.int32)
    group = math.gcd(batches, 8)
    turns = batches // group

    def work(total, item):
        slots, count, values, coords, quad = item
        gid = jnp.take(own_set, slots.reshape(-1), axis=0)
        active = (slot_ids[None, :] < count[:, None]).astype(jnp.float32)
        rowmask = jnp.repeat(active, FB, axis=1)[:, :, None]
        xmask = jnp.where(rowmask > 0, values, jnp.zeros_like(values))
        xweighted = (xmask.astype(jnp.float32) * quad[:, None, :]).astype(jnp.bfloat16)
        dloc = tile[slots[:, :, None], :, slots[:, None, :], :]
        dloc = dloc.transpose(0, 1, 3, 2, 4).reshape(group, width, width)
        centre = jnp.take(centre_blocks, gid, axis=1).reshape(3, group, width)
        spread = jnp.take(spread_blocks, gid, axis=0).reshape(group, width)
        vfac = coulomb(
            centre[0][:, :, None],
            centre[1][:, :, None],
            centre[2][:, :, None],
            spread[:, :, None],
            coords[:, 0][:, None, :],
            coords[:, 1][:, None, :],
            coords[:, 2][:, None, :],
        )
        gval = jnp.einsum("brc,bcg->brg", dloc, xmask, preferred_element_type=jnp.float32)
        fval = (gval * vfac * rowmask).astype(jnp.bfloat16)
        parts = jnp.einsum("brg,bcg->brc", fval, xweighted, preferred_element_type=jnp.float32)
        pieces = parts.reshape(group, TMAX, FB, TMAX, FB).transpose(0, 1, 3, 2, 4)
        total = total.at[slots[:, :, None], :, slots[:, None, :], :].add(pieces)
        return (total, None)

    items = (
        blocks.reshape(turns, group, TMAX),
        counts.reshape(turns, group),
        basis.reshape(turns, group, width, basis.shape[2]),
        points.reshape(turns, group, 3, points.shape[2]),
        weights.reshape(turns, group, weights.shape[1]),
    )
    start = jnp.zeros((UMAX, FB, UMAX, FB), jnp.float32)
    local_sum, _ = lax.scan(work, start, items)
    local_flat = local_sum.reshape(UMAX * FB, UMAX * FB)
    halved = lax.psum_scatter(local_flat, "rows", scatter_dimension=1, tiled=True)
    returned = lax.all_to_all(
        spread_rows(halved, stored, block_count, sources),
        "dom",
        split_axis=0,
        concat_axis=0,
        tiled=True,
    )
    gathered_terms = collect(returned, half_sets, block_count)
    summed = lax.psum_scatter(gathered_terms, "rows", scatter_dimension=1, tiled=True)
    return summed.astype(jnp.bfloat16)


def call(kernel, scalars, arrays, in_specs, out_shapes, out_specs, scratch, grid=(1,), cost=None, vmem=44):
    return pl.pallas_call(
        kernel,
        grid_spec=pltpu.PrefetchScalarGridSpec(
            num_scalar_prefetch=len(scalars),
            grid=grid,
            in_specs=in_specs,
            out_specs=out_specs,
            scratch_shapes=scratch,
        ),
        out_shape=out_shapes,
        cost_estimate=pl.CostEstimate(flops=cost[0], bytes_accessed=cost[1], transcendentals=0),
        compiler_params=pltpu.CompilerParams(vmem_limit_bytes=vmem * MIB),
    )(*scalars, *arrays)


def whole(shape):
    return pl.BlockSpec(shape, lambda *_: (0,) * len(shape))


def pick_kernel(peers, *refs):
    sets, full, outs = refs[:peers], refs[peers], refs[peers + 1 :]
    for k in range(peers):
        for q in range(UMAX):
            cols = pl.ds(pl.multiple_of(sets[k][0, q] * FB, FB), FB)
            outs[k][:, :, q * FB : (q + 1) * FB] = full[:, :, cols]


def pick(sets, full):
    nb, sub, cols = full.shape
    shape = (nb, sub, UMAX * FB)
    peers = len(sets)
    return call(
        functools.partial(pick_kernel, peers),
        sets,
        [full],
        [whole(full.shape)],
        [jax.ShapeDtypeStruct(shape, full.dtype)] * peers,
        [whole(shape)] * peers,
        [],
        cost=(0, 2 * nb * sub * (cols + peers * UMAX * FB)),
    )


def centre_kernel(own_set, core, centers, widths, out, turned):
    sub = out.shape[2]
    for p in range(UMAX):
        cols = pl.ds(pl.multiple_of(own_set[0, p] * FB, FB), FB)
        width = widths[:, cols]
        rows = jnp.concatenate([centers[:, cols], width * width, jnp.zeros((4, FB), jnp.float32)], axis=0)
        turned[...] = rows.T
        start = pl.multiple_of(core[0] * sub, sub)
        for c in range(4):
            out[c, p] = jnp.broadcast_to(turned[pl.ds(start, sub), c : c + 1], (sub, FB))


def centre_rows(own_set, core, centers, widths, sub):
    shape = (4, UMAX, sub, FB)
    return call(
        centre_kernel,
        [own_set, core],
        [centers, widths],
        [whole(centers.shape), whole(widths.shape)],
        jax.ShapeDtypeStruct(shape, jnp.float32),
        whole(shape),
        [pltpu.VMEM((FB, 8), jnp.float32)],
        cost=(0, 2 * 4 * UMAX * sub * FB * 4),
    )


def table_places(batches, group):
    lives = batches
    rows = lives + batches // group
    slots = batches * TMAX
    return lives, rows, rows + slots, rows + 2 * slots, rows + 3 * slots, rows + 4 * slots


def table_kernel(nb, near, group, me, owner, own_set, blocks, packed, counts, out, kbs, fill, bundle, sem):
    copy = pltpu.make_async_copy(packed.at[TMAX], bundle, sem)
    copy.start()
    half = counts.shape[0]
    at_lives, at_near, at_far, at_pos, at_col, _ = table_places(2 * half, group)
    spare = nb * near
    for p in range(UMAX):
        stored = owner[own_set[0, p]]
        kbs[p] = (lax.div(stored, nb) ^ me[0]) * nb + lax.rem(stored, nb)
    for c in range(TMAX + 1):
        fill[c] = 0
    copy.wait()

    def count_of(side, b):
        return bundle[b, TMAX].astype(jnp.int32) if side else counts[b]

    for side in (0, 1):

        @pl.loop(0, half)
        def _(b):
            count = count_of(side, b)
            fill[count] = fill[count] + 1

    place = 0
    for c in range(TMAX, -1, -1):
        many = fill[c]
        fill[c] = place
        place = place + many

    for side in (0, 1):

        @pl.loop(0, half)
        def _(b):
            count = count_of(side, b)
            j = fill[count]
            fill[count] = j + 1
            out[j] = side * half + b

            @pl.when(lax.rem(j, group) == 0)
            def _():
                out[at_lives + lax.div(j, group)] = count

            for s in range(TMAX):
                pos = bundle[b, s].astype(jnp.int32) if side else blocks[s, b]
                on = s < count
                at = j * TMAX + s
                out[at_pos + at] = pos
                out[at_col + at] = jnp.where(on, pos, UMAX)
                kb = kbs[pos]
                out[at_near + at] = jnp.where(on & (kb < spare), kb, spare)
                out[at_far + at] = jnp.where(on & (kb >= spare), kb - spare, spare)


def batch_tables(me, owner, own_set, blocks, packed, counts, nb, near):
    batches = 2 * counts.shape[0]
    group = math.gcd(batches, GROUP)
    size = table_places(batches, group)[-1]
    return call(
        functools.partial(table_kernel, nb, near, group),
        [me, owner, own_set, blocks],
        [packed, counts],
        [pl.BlockSpec(memory_space=pl.ANY), pl.BlockSpec(memory_space=pltpu.SMEM)],
        jax.ShapeDtypeStruct((size,), jnp.int32),
        pl.BlockSpec(memory_space=pltpu.SMEM),
        [
            pltpu.SMEM((UMAX,), jnp.int32),
            pltpu.SMEM((TMAX + 1,), jnp.int32),
            pltpu.SMEM(packed.shape[1:], packed.dtype),
            pltpu.SemaphoreType.DMA,
        ],
        cost=(0, 8 * batches * TMAX),
    )


def pack_kernel(points, weights, blocks, counts, out):
    batches, pts = weights.shape
    out[0:3] = points[...]
    out[3] = weights[...]
    lane = lax.broadcasted_iota(jnp.int32, (1, pts), 1)

    @pl.loop(0, batches)
    def _(b):
        row = jnp.where(lane == TMAX, counts[b], 0)
        for s in range(TMAX):
            row = jnp.where(lane == s, blocks[s, b], row)
        out[4, pl.ds(b, 1), :] = row.astype(jnp.float32)


def pack(points, weights, blocks, counts):
    shape = (5, *weights.shape)
    return call(
        pack_kernel,
        [],
        [points, weights, blocks, counts],
        [whole(points.shape), whole(weights.shape)] + [pl.BlockSpec(memory_space=pltpu.SMEM)] * 2,
        jax.ShapeDtypeStruct(shape, jnp.float32),
        whole(shape),
        [],
        cost=(0, 10 * 4 * weights.size),
    )


def add_up(sets, terms, total):
    total[...] = jnp.zeros(total.shape, total.dtype)
    for k, term in enumerate(terms):
        for q in range(UMAX):
            cols = pl.ds(pl.multiple_of(sets[k][0, q] * FB, FB), FB)
            total[:, :, cols] += term[:, :, q * FB : (q + 1) * FB].astype(jnp.float32)


def merge_kernel(peers, *refs):
    sets, terms, out, total = refs[:peers], refs[peers : 2 * peers], refs[-2], refs[-1]
    add_up(sets, terms, total)
    out[...] = total[...].astype(out.dtype)


def merge(sets, terms, cols, dtype=jnp.bfloat16):
    nb, sub, wide = terms[0].shape
    shape = (nb, sub, cols)
    return call(
        functools.partial(merge_kernel, len(terms)),
        sets,
        terms,
        [whole(t.shape) for t in terms],
        jax.ShapeDtypeStruct(shape, dtype),
        whole(shape),
        [pltpu.VMEM(shape, jnp.float32)],
        cost=(0, 2 * nb * sub * (cols + 5 * wide)),
    )


def finish_kernel(core, near, *refs):
    fars, (out, give, keep, sem) = refs[:-4], refs[-4:]
    half = give.shape[2]
    for part, side in ((keep, core[0]), (give, 1 - core[0])):
        cols = pl.ds(pl.multiple_of(side * half, FB), half)
        for b, far in enumerate(fars):
            part[b] = (near[b, :, cols] + far[0, :, cols].astype(jnp.float32)).astype(part.dtype)
        if part is keep:
            copy = pltpu.make_async_copy(keep, out.at[:, side], sem)
            copy.start()
    copy.wait()


def finish(core, near, fars):
    nb, sub, cols = near.shape
    shape = (nb, sub, cols // 2)
    return call(
        finish_kernel,
        [core],
        [near, *fars],
        [whole(t.shape) for t in (near, *fars)],
        [jax.ShapeDtypeStruct((nb, 2, *shape[1:]), jnp.bfloat16), jax.ShapeDtypeStruct(shape, jnp.bfloat16)],
        [pl.BlockSpec(memory_space=pl.ANY), whole(shape)],
        [pltpu.VMEM(shape, jnp.bfloat16), pltpu.SemaphoreType.DMA],
        cost=(0, 2 * nb * sub * 4 * cols),
    )


def place_kernel(core, got, _, out, sem):
    copy = pltpu.make_async_copy(got, out.at[:, 1 - core[0]], sem)
    copy.start()
    copy.wait()


def place(core, got, out):
    return pl.pallas_call(
        place_kernel,
        grid_spec=pltpu.PrefetchScalarGridSpec(
            num_scalar_prefetch=1,
            grid=(1,),
            in_specs=[pl.BlockSpec(memory_space=pl.ANY)] * 2,
            out_specs=pl.BlockSpec(memory_space=pl.ANY),
            scratch_shapes=[pltpu.SemaphoreType.DMA],
        ),
        out_shape=jax.ShapeDtypeStruct(out.shape, out.dtype),
        input_output_aliases={2: 0},
        compiler_params=pltpu.CompilerParams(vmem_limit_bytes=36 * MIB),
    )(core, got, out)


def batch_kernel(group, pieces, split, table, *refs):
    xs, quads, centre_in = refs[0:2], refs[2:4], refs[4]
    parts = refs[5 : 5 + pieces]
    outs = refs[5 + pieces : -7]
    dense, acc, xbuf, qbuf, centre, sems, xsems = refs[-7:]
    nb, sub, wide = parts[0].shape
    spare = nb * pieces
    batches, _, pts = xbuf.shape
    half = batches // 2
    at_lives, at_near, at_far, at_pos, at_col, _ = table_places(batches, group)
    at_row = at_far if split else at_near

    def fetch(j, sem):
        b = table[j]
        for side in (0, 1):

            @pl.when((b >= half) if side else (b < half))
            def _():
                pltpu.make_async_copy(xs[side].at[b - half * side], xbuf.at[j], sem).start()

    copies = [
        pltpu.make_async_copy(part, dense.at[pl.ds(nb * k, nb), :, pl.ds(0, wide)], sems.at[k])
        for k, part in enumerate(parts)
    ]
    copies.append(pltpu.make_async_copy(centre_in, centre, sems.at[pieces]))
    for side in (0, 1):
        quad = qbuf.at[:, pl.ds(half * side, half)]
        copies.append(pltpu.make_async_copy(quads[side].at[pl.ds(0, 4)], quad, sems.at[pieces + 1 + side]))
    for copy in copies:
        copy.start()

    @pl.loop(0, batches // group)
    def _(h):
        for u in range(group):
            fetch(h * group + u, xsems.at[h])

    acc[...] = jnp.zeros(acc.shape, acc.dtype)
    dense[:, :, wide:] = jnp.zeros((spare + 1, sub, FB), dense.dtype)
    dense[spare, :, :wide] = jnp.zeros((sub, wide), dense.dtype)
    for copy in copies:
        copy.wait()

    def lanes(col):
        return jnp.concatenate([col] * (pts // FB), axis=1)

    def one(j, live):
        b = table[j]
        row = [table[at_row + j * TMAX + s] for s in range(live)]
        pos = [table[at_pos + j * TMAX + s] for s in range(live)]
        col = [pl.ds(pl.multiple_of(table[at_col + j * TMAX + s] * FB, FB), FB) for s in range(live)]
        x = xbuf[j, : live * FB, :]
        d = jnp.concatenate(
            [jnp.concatenate([dense[r, :, c] for c in col], axis=1) for r in row], axis=0
        )
        gval = jnp.dot(d, x, preferred_element_type=jnp.float32)
        fval = []
        for s in range(live):
            dist = None
            for axis in range(3):
                diff = lanes(centre[axis, pos[s]]) - qbuf[axis, pl.ds(b, 1), :]
                dist = diff * diff if dist is None else dist + diff * diff
            dist = dist + lanes(centre[3, pos[s]])
            fval.append((gval[s * sub : (s + 1) * sub] * lax.rsqrt(dist)).astype(jnp.bfloat16))
        fval = jnp.concatenate(fval, axis=0)
        xw = (x.astype(jnp.float32) * qbuf[3, pl.ds(b, 1), :]).astype(jnp.bfloat16)
        part = lax.dot_general(
            fval, xw, (((1,), (1,)), ((), ())), preferred_element_type=jnp.float32
        )
        return row, col, part

    @pl.loop(0, batches // group)
    def _(h):
        arrived = xbuf.at[pl.ds(h * group, group)]
        pltpu.make_async_copy(arrived, arrived, xsems.at[h]).wait()
        for live in range(2, TMAX + 1):

            @pl.when(table[at_lives + h] == live)
            def _():
                for row, col, part in [one(h * group + u, live) for u in range(group)]:
                    for s in range(live):
                        for t in range(live):
                            acc[row[s], :, col[t]] += part[s * sub : (s + 1) * sub, t * FB : (t + 1) * FB]

    start = 0
    for out in outs:
        rows = out.shape[0]
        out[...] = acc[start : start + rows, :, :wide].astype(out.dtype)
        start += rows


def batch_sums(table, xs, quads, centre, parts, split):
    _, width, pts = xs[0].shape
    batches = 2 * xs[0].shape[0]
    group = math.gcd(batches, GROUP)
    nb, sub, wide = parts[0].shape
    pieces = len(parts)
    size = 1 if split else nb
    out_shapes = [
        jax.ShapeDtypeStruct((size, sub, wide), jnp.bfloat16 if k else jnp.float32)
        for k in range(pieces)
        for _ in range(nb // size)
    ]
    flops = 2 * batches * 2 * width * (width // 2) * pts
    return call(
        functools.partial(batch_kernel, group, pieces, split),
        [table],
        [*xs, *quads, centre, *parts],
        [pl.BlockSpec(memory_space=pl.ANY)] * (5 + pieces),
        out_shapes,
        [whole(out.shape) for out in out_shapes],
        [
            pltpu.VMEM((nb * pieces + 1, sub, wide + FB), jnp.bfloat16),
            pltpu.VMEM((nb * pieces + 1, sub, wide + FB), jnp.float32),
            pltpu.VMEM((batches, width, pts), jnp.bfloat16),
            pltpu.VMEM((4, batches, pts), jnp.float32),
            pltpu.VMEM(centre.shape, jnp.float32),
            pltpu.SemaphoreType.DMA((pieces + 3,)),
            pltpu.SemaphoreType.DMA((batches // group,)),
        ],
        cost=(flops, 2 * batches * width * pts),
    )


def per_device(density, owner, touched, blocks, counts, basis, points, weights, centers, widths):
    n = lax.axis_size("dom")
    cores = lax.axis_size("rows")
    i = lax.axis_index("dom")
    r = lax.axis_index("rows")
    nb = density.shape[0] // FB
    sub = FB // cores
    cols = density.shape[1]
    near = n // 2
    core = r.reshape(1)

    def swap(x, k):
        return lax.ppermute(x, "dom", [(a, a ^ k) for a in range(n)])

    def across(x):
        return lax.ppermute(x, "rows", [(a, cores - 1 - a) for a in range(cores)])

    def stay(x):
        return pltpu.with_memory_space_constraint(x, pltpu.HBM)

    own = lax.dynamic_index_in_dim(density.reshape(nb, cores, sub, cols), r, 1, keepdims=False)
    sets = [touched] + [swap(touched, k) for k in range(1, near)]
    packed = pack(stay(points.transpose(1, 0, 2)), stay(weights), stay(blocks.T), stay(counts))
    packed_b = across(packed)
    own, sets, basis = lax.optimization_barrier((own, sets, basis))
    far = swap(own, near)
    sets[0] = stay(touched)
    picked = pick(sets, own)
    parts = [picked[0]] + [swap(picked[k], k) for k in range(1, near)]
    xs = (stay(basis), across(basis))
    quads = (packed, packed_b)
    table = batch_tables(i.reshape(1), stay(owner), sets[0], stay(blocks.T), packed_b, stay(counts), nb, near)
    centre = centre_rows(sets[0], core, stay(centers), stay(widths.reshape(1, -1)), sub)

    far, table, centre = lax.optimization_barrier((far, table, centre))
    picked = pick(sets, far)
    far_parts = [picked[0]] + [swap(picked[k], k) for k in range(1, near)]
    table, _ = lax.optimization_barrier((table, picked[0]))

    common = (xs, quads, centre)
    sums = batch_sums(table, *common, parts, False)
    table, _ = lax.optimization_barrier((table, sums[0]))
    far_sums = batch_sums(table, *common, far_parts, True)
    terms = [sums[0], sums[1]] + [swap(sums[k], k) for k in range(2, near)]
    far_sums, terms = lax.optimization_barrier((far_sums, terms))
    terms[1] = swap(terms[1], 1)
    near_sum = merge(sets, terms, cols, jnp.float32)
    far_terms = []
    for b in range(nb):
        chunk = [far_sums[b]] + [swap(far_sums[nb * k + b], k) for k in range(1, near)]
        if b == nb - 1:
            chunk, near_sum = lax.optimization_barrier((chunk, near_sum))
        merged = merge(sets, chunk, cols)
        far_sums, merged = lax.optimization_barrier((far_sums, merged))
        far_terms.append(swap(merged, near))
    out, give = finish(core, near_sum, far_terms)
    return place(core, across(give), out).reshape(nb * FB, cols // cores)


def solution(mesh):
    in_specs = (
        P(("groups", "dom"), None),
        P("groups"),
        P(("groups", "dom"), None),
        P(("groups", "dom", "rows"), None),
        P(("groups", "dom", "rows")),
        P(("groups", "dom", "rows"), None, None),
        P(("groups", "dom", "rows"), None, None),
        P(("groups", "dom", "rows"), None),
        P(None, "groups"),
        P("groups"),
    )
    out_specs = P(("groups", "dom"), "rows")

    def run(*args):
        n, cores = mesh.shape["dom"], mesh.shape["rows"]
        rows_here = args[0].shape[0] // (mesh.shape["groups"] * n)
        split = rows_here % FB == 0 and cores == 2 and n >= 4 and n & (n - 1) == 0
        body = per_device if split else per_device_any
        return jax.shard_map(body, mesh=mesh, in_specs=in_specs, out_specs=out_specs, check_vma=False)(*args)

    return run
```
